128 devices in a mesh: row: 16 (over y_lo, z, core), col: 8 (over y_hi, x).
Axes of the slice: x: 4, y: 4 (y_hi: 2, y_lo: 2; y = y_hi * 2 + y_lo), z: 4, core: 2. Of those that a mesh axis runs over, the one named last changes fastest.
Arguments:
- inputs: bfloat16 [2048, 12288], P('row', 'col'), may hold values from -7 to 7
- w_qkv: bfloat16 [12288, 48, 384], P('col', 'row'), may hold values from -1 to 1
- w_out: bfloat16 [48, 128, 12288], P('row', None, 'col'), may hold values from -0.078125 to 0.078125
- grad_block: bfloat16 [2048, 12288], P('row', 'col'), may hold values from -3 to 3
Outputs:
- block_out: bfloat16 [2048, 12288], P('row', 'col')
- grad_qkv: float32 [12288, 48, 384], P('col', 'row')
- grad_out: float32 [48, 128, 12288], P('row', None, 'col')
The draws below stay inside these ranges and needn't reach their ends.
All inputs are finite; a program needn't handle non-finite values.
Results may differ from the reference program's by a relative error of at most 0.04.
Values may be sent and summed in bfloat16 or wider, within the bound.
A program may use at most 128 MiB of HBM per device.

```python
import jax
import jax.numpy as jnp
from jax import lax

D = 12288
HEADS = 48
HD = 128
LEN = 2048
N_ROW = 16
N_COL = 8


def draw_inputs(key, part):
    key = jax.random.fold_in(key, 11)
    values = jnp.clip(jax.random.normal(key, (LEN, D), jnp.float32), -4.0, 4.0)
    return values.astype(jnp.bfloat16)


def draw_w_qkv(key, part):
    key = jax.random.fold_in(key, 23)
    scale_factor = D ** (-0.5)
    whole = jnp.clip(jax.random.normal(key, (D, HEADS, 3, HD), jnp.float32), -5.0, 5.0)
    return (whole * scale_factor).reshape(D, HEADS, 3 * HD).astype(jnp.bfloat16)


def block_levels(key, dims, shards, least, top_value):
    def one(axis_at, parts):
        steps = jax.random.uniform(jax.random.fold_in(jax.random.fold_in(key, 6), axis_at), (parts,), jnp.float32, least / len(shards), top_value / len(shards))
        return jnp.repeat(jnp.exp(steps), dims[axis_at] // parts).reshape((-1,) + (1,) * (len(dims) - axis_at - 1))

    factor_of = one(*shards[0])
    for cut in shards[1:]:
        factor_of = factor_of * one(*cut)
    return factor_of


def bell_draw(own_key, shape, deviation, limit, cuts=(), kind=jnp.bfloat16):
    level = block_levels(own_key, shape, cuts, -0.22, 0.18) if cuts else 1.0
    drawn = jax.random.normal(own_key, shape, jnp.float32) * deviation * level
    return jnp.minimum(jnp.maximum(drawn, -limit), limit).astype(kind)


def setup_inputs(seed: int = 0) -> dict:
    splits = jax.random.split(jax.random.key(seed), 5)
    inputs = draw_inputs(jax.random.fold_in(splits[4], 71), 0)
    w_qkv = draw_w_qkv(jax.random.fold_in(splits[4], 71), 0)
    w_out = bell_draw(splits[2], (HEADS, HD, D), (HEADS * HD) ** -0.5, 0.078125, ((0, 16), (2, 8)))
    grad_block = bell_draw(splits[3], (LEN, D), 0.5, 3.0, ((0, 16), (1, 8)))
    return {"inputs": inputs, "w_qkv": w_qkv, "w_out": w_out, "grad_block": grad_block}


masked_fill = -1.0e30


def rounded(values):
    return lax.optimization_barrier(values.astype(jnp.bfloat16)).astype(jnp.float32)


def reference(inputs, w_qkv, w_out, grad_block):
    seq_len = LEN
    feat_cols = D // N_COL
    group_width = (HEADS // N_ROW) * HD
    scale_factor = HD ** -0.5
    qkv_flat = w_qkv.reshape(D, HEADS * 3 * HD)
    qkv_sum = jnp.zeros((seq_len, HEADS * 3 * HD), jnp.float32)
    for col_index in range(N_COL):
        low_col = col_index * feat_cols
        qkv_sum = qkv_sum + rounded(jnp.dot(inputs[:, low_col:low_col + feat_cols], qkv_flat[low_col:low_col + feat_cols], preferred_element_type=jnp.float32))
    qkv = qkv_sum.astype(jnp.bfloat16).reshape(seq_len, HEADS, 3 * HD)
    queries = jnp.transpose(qkv[:, :, :HD], (1, 0, 2))
    key_rows = jnp.transpose(qkv[:, :, HD:2 * HD], (1, 0, 2))
    value_rows = jnp.transpose(qkv[:, :, 2 * HD:], (1, 0, 2))
    positions = jnp.arange(seq_len)
    causal = positions[None, :] <= positions[:, None]

    def head_probability(query_head, key_head):
        scores = jnp.dot(query_head, key_head.T, preferred_element_type=jnp.float32) * scale_factor
        scores = jnp.where(causal, scores, masked_fill)
        row_max = jnp.max(scores, axis=1, keepdims=True)
        exponent = jnp.exp(scores - row_max)
        return exponent / jnp.sum(exponent, axis=1, keepdims=True)

    def forward_head(operands):
        query_head, key_head, value_head = operands
        weights = head_probability(query_head, key_head).astype(jnp.bfloat16)
        return jnp.dot(weights, value_head, preferred_element_type=jnp.float32).astype(jnp.bfloat16)

    attended = lax.map(forward_head, (queries, key_rows, value_rows))
    attended_flat = jnp.transpose(attended, (1, 0, 2)).reshape(seq_len, HEADS * HD)
    out_flat = w_out.reshape(HEADS * HD, D)
    block_sum = jnp.zeros((seq_len, D), jnp.float32)
    for row_index in range(N_ROW):
        low_head = row_index * group_width
        block_sum = block_sum + rounded(jnp.dot(attended_flat[:, low_head:low_head + group_width], out_flat[low_head:low_head + group_width], preferred_element_type=jnp.float32))
    block_out = block_sum.astype(jnp.bfloat16)
    grad_out = jnp.dot(attended_flat.T, grad_block, preferred_element_type=jnp.float32).reshape(HEADS, HD, D)
    grad_sum = jnp.zeros((seq_len, HEADS * HD), jnp.float32)
    for col_index in range(N_COL):
        low_col = col_index * feat_cols
        grad_sum = grad_sum + rounded(jnp.dot(grad_block[:, low_col:low_col + feat_cols], out_flat[:, low_col:low_col + feat_cols].T, preferred_element_type=jnp.float32))
    grad_attended = jnp.transpose(grad_sum.astype(jnp.bfloat16).reshape(seq_len, HEADS, HD), (1, 0, 2))
    query_block = seq_len // N_COL

    def backward_head(operands):
        query_head, key_head, value_head, grad_head = operands
        probability = head_probability(query_head, key_head)
        weights = probability.astype(jnp.bfloat16)
        grad_prob = jnp.dot(grad_head, value_head.T, preferred_element_type=jnp.float32)
        grad_scores = (probability * (grad_prob - jnp.sum(probability * grad_prob, axis=1, keepdims=True)) * scale_factor).astype(jnp.bfloat16)
        grad_query = jnp.dot(grad_scores, key_head, preferred_element_type=jnp.float32).astype(jnp.bfloat16)
        score_blocks = grad_scores.astype(jnp.float32).reshape(N_COL, query_block, seq_len)
        weight_blocks = weights.astype(jnp.float32).reshape(N_COL, query_block, seq_len)
        query_blocks = query_head.astype(jnp.float32).reshape(N_COL, query_block, HD)
        grad_blocks = grad_head.astype(jnp.float32).reshape(N_COL, query_block, HD)
        key_parts = jnp.einsum("cqk,cqd->ckd", score_blocks, query_blocks)
        value_parts = jnp.einsum("cqk,cqd->ckd", weight_blocks, grad_blocks)
        grad_key = jnp.sum(rounded(key_parts), axis=0).astype(jnp.bfloat16)
        grad_value = jnp.sum(rounded(value_parts), axis=0).astype(jnp.bfloat16)
        return grad_query, grad_key, grad_value

    grad_query, grad_key, grad_value = lax.map(backward_head, (queries, key_rows, value_rows, grad_attended))
    grad_rows = jnp.concatenate([grad_query, grad_key, grad_value], axis=2)
    grad_rows = jnp.transpose(grad_rows, (1, 0, 2)).reshape(seq_len, HEADS * 3 * HD)
    grad_qkv = jnp.dot(inputs.T, grad_rows, preferred_element_type=jnp.float32).reshape(D, HEADS, 3 * HD)
    return block_out, grad_qkv, grad_out
```

```python
import jax
import jax.numpy as jnp
from jax import lax
from jax.experimental import pallas as pl
from jax.experimental.pallas import tpu as pltpu
from jax.sharding import PartitionSpec as P

MESH = pl.DeviceIdType.MESH
BF16 = jnp.bfloat16
F32 = jnp.float32


class Place:
    def __init__(self):
        r = lax.axis_index("row")
        c = lax.axis_index("col")
        self.ylo, self.z, self.core = r // 8, (r // 2) % 4, r % 2
        self.yhi, self.x = c // 4, c % 4

    def at(self, ylo=0, z=0, core=0, yhi=0, x=0):
        return (
            lax.rem(self.ylo + ylo, 2) * 8 + lax.rem(self.z + z + 4, 4) * 2 + lax.rem(self.core + core, 2),
            lax.rem(self.yhi + yhi, 2) * 4 + lax.rem(self.x + x + 4, 4),
        )

    def slot(self, ylo=0, z=0, core=0):
        return self.at(ylo=ylo, z=z, core=core)[0]

    def col_x(self, x):
        return lax.rem(self.x + x + 4, 4)


def meet(partners):
    barrier = pltpu.get_barrier_semaphore()
    for partner in partners:
        pl.semaphore_signal(barrier, inc=1, device_id=partner, device_id_type=MESH)
    pl.semaphore_wait(barrier, len(partners))


def remote(src, dst, send, recv, device):
    return pltpu.make_async_remote_copy(
        src_ref=src, dst_ref=dst, send_sem=send, recv_sem=recv, device_id=device, device_id_type=MESH
    )


def project_kernel(
    x_ref, g_ref, w_hbm, wo_ref,
    all_out, sum_out,
    held, part, relay, near, far, mine, total, w_ref,
    ag_send, ag_recv, s1_send, s1_recv, s2_send, s2_recv, s3_send, s3_recv, s4_send, s4_recv,
    out_sem, w_sem, own_sem,
):
    me = Place()
    up, down = dict(z=1), dict(z=-1)
    own_rows = (x_ref, g_ref)
    right, left, across, twin = me.at(x=1), me.at(x=-1), me.at(yhi=1), me.at(core=1)
    is_home = me.core == me.yhi
    w_copy = pltpu.make_async_copy(w_hbm, w_ref, w_sem)
    w_copy.start()
    own_copy = []
    for a in (0, 1):
        copy = pltpu.make_async_copy(own_rows[a], held.at[a, me.slot()], own_sem.at[a])
        copy.start()
        own_copy.append(copy)
    meet([me.at(ylo=1), me.at(**up), me.at(**down), twin, right, left, across])

    def gather(a, k):
        whole = pl.ds(0, 128)
        first, second = pl.ds(0, 64), pl.ds(64, 64)
        slot, rows, device = {
            0: (me.slot(), whole, me.at(ylo=1)),
            1: (me.slot(), whole, me.at(**up)),
            2: (me.slot(), whole, me.at(**down)),
            3: (me.slot(ylo=1), whole, me.at(**up)),
            4: (me.slot(ylo=1), whole, me.at(**down)),
            5: (me.slot(z=-1), first, me.at(**up)),
            6: (me.slot(z=1), second, me.at(**down)),
            7: (me.slot(ylo=1, z=-1), first, me.at(**up)),
            8: (me.slot(ylo=1, z=1), second, me.at(**down)),
            9: (me.slot(), whole, twin),
            10: (me.slot(ylo=1), whole, twin),
            11: (me.slot(z=-1), whole, twin),
            12: (me.slot(z=1), whole, twin),
            13: (me.slot(ylo=1, z=-1), whole, twin),
            14: (me.slot(ylo=1, z=1), whole, twin),
            15: (me.slot(z=2), whole, twin),
            16: (me.slot(ylo=1, z=2), whole, twin),
        }[k]
        ref = held.at[a, slot, rows]
        src = own_rows[a] if k in (0, 1, 2, 9) else ref
        return remote(src, ref, ag_send.at[a, k], ag_recv.at[a, k], device)

    def go(a, *kinds):
        for k in kinds:
            gather(a, k).start()

    def landed(a, *kinds):
        for k in kinds:
            gather(a, k).wait_recv()

    def block_of(s):
        ylo = jnp.where((s == 1) | (s == 4) | (s == 5) | (s == 7), 1, 0)
        z = jnp.where((s == 2) | (s == 4), 3, jnp.where((s == 3) | (s == 5), 1, jnp.where(s >= 6, 2, 0)))
        return lax.rem(me.ylo + ylo, 2) * 4 + lax.rem(me.z + z, 4)

    def unit(a):
        return pl.ds(0, 3) if a == 0 else pl.ds(3, 1)

    def keep(a, s):
        pair = pl.ds(block_of(s) * 2, 2)
        return pltpu.make_async_copy(held.at[a, pair], all_out.at[a, pair], out_sem.at[a, s])

    def rs1(a, s):
        start = me.col_x(2) * 64
        return [
            remote(part.at[s, unit(a), pl.ds(pl.multiple_of(start + 32 * d, 32), 32)], relay.at[s, d, unit(a)],
                   s1_send.at[a, s, d], s1_recv.at[a, s, d], (right, left)[d])
            for d in (0, 1)
        ]

    def rs2(a, s):
        return [
            remote(part.at[s, unit(a), pl.ds(pl.multiple_of(me.col_x((1, -1)[d]) * 64, 64), 64)], near.at[s, d, unit(a)],
                   s2_send.at[a, s, d], s2_recv.at[a, s, d], (right, left)[d])
            for d in (0, 1)
        ]

    def rs3(a, s):
        return remote(mine.at[s, unit(a)], far.at[s, unit(a)], s3_send.at[a, s], s3_recv.at[a, s], across)

    def rs4(a, s):
        rows = total.at[block_of(s), unit(a)]
        return remote(rows, rows, s4_send.at[a, s], s4_recv.at[a, s], twin)

    def multiply(a, s):
        rows = held.at[a, pl.ds(block_of(s) * 2, 2)]
        keep(a, s).start()
        if a == 0:
            @pl.loop(0, 3)
            def _(h):
                part[s, h] = jnp.dot(
                    rows[...].reshape(256, 1536), w_ref[h], preferred_element_type=F32
                ).astype(BF16)
        else:
            part[s, 3] = lax.dot_general(
                rows[...].reshape(256, 1536), wo_ref[...].reshape(384, 1536),
                (((1,), (1,)), ((), ())), preferred_element_type=F32,
            ).astype(BF16)
        for copy in rs1(a, s):
            copy.start()

    def each(steps, body):
        lo, hi = steps
        if hi - lo == 1:
            body(lo)
        else:
            pl.loop(lo, hi)(body)

    def work(a, *steps):
        def body(s):
            gather_twin(a, s)
            multiply(a, s)
        each(steps, body)

    def gather_twin(a, s):
        remote(held.at[a, 0], held.at[a, 0], ag_send.at[a, 9 + s], ag_recv.at[a, 9 + s], twin).wait_recv()

    def add_relay(a, *steps):
        def body(s):
            sends = rs2(a, s)
            for d in (0, 1):
                rs1(a, s)[d].wait_recv()
                rows = pl.ds(pl.multiple_of(me.col_x((1, -1)[d]) * 64 + 32 * d, 32), 32)
                part[s, unit(a), rows] = (
                    part[s, unit(a), rows].astype(F32) + relay[s, d, unit(a)].astype(F32)
                ).astype(BF16)
                sends[d].start()
        each(steps, body)

    def add_near(a, *steps):
        def body(s):
            for d in (0, 1):
                rs2(a, s)[d].wait_recv()
            rows = pl.ds(pl.multiple_of(me.x * 64, 64), 64)
            mine[s, unit(a)] = (
                part[s, unit(a), rows].astype(F32)
                + near[s, 0, unit(a)].astype(F32)
                + near[s, 1, unit(a)].astype(F32)
            ).astype(BF16)

            @pl.when(jnp.logical_not(is_home))
            def _():
                rs3(a, s).start()
        each(steps, body)

    def add_far(a, *steps):
        @pl.when(is_home)
        def _():
            def body(s):
                rs3(a, s).wait_recv()
                total[block_of(s), unit(a)] = (
                    mine[s, unit(a)].astype(F32) + far[s, unit(a)].astype(F32)
                ).astype(BF16)
                rs4(a, s).start()
            each(steps, body)

    go(0, 9, 0, 1, 2)
    go(1, 9)
    w_copy.wait()
    for copy in own_copy:
        copy.wait()
    work(0, 0, 1)
    work(1, 0, 1)
    landed(0, 0)
    go(0, 3, 4, 10)
    go(1, 0)
    landed(0, 1)
    go(0, 5, 11)
    landed(0, 2)
    go(0, 6, 12)
    work(0, 1, 4)
    add_relay(0, 0, 1)
    add_relay(1, 0, 1)
    add_relay(0, 1, 2)
    landed(0, 3)
    go(0, 7, 13)
    landed(0, 4)
    go(0, 8, 14)
    go(1, 1, 2)
    work(0, 4, 6)
    add_near(0, 0, 1)
    add_near(1, 0, 1)
    add_relay(0, 2, 4)
    landed(0, 5, 6)
    go(0, 15)
    landed(1, 0)
    go(1, 3, 4, 10)
    landed(0, 7, 8)
    go(0, 16)
    work(0, 6, 8)
    work(1, 1, 2)
    add_near(0, 1, 4)
    add_relay(0, 4, 6)
    landed(1, 1)
    go(1, 5, 11)
    landed(1, 2)
    go(1, 6, 12)
    work(1, 2, 4)
    add_far(0, 0, 4)
    add_relay(0, 6, 8)
    add_near(0, 4, 6)
    landed(1, 3)
    go(1, 7, 13)
    landed(1, 4)
    go(1, 8, 14)
    work(1, 4, 6)
    add_relay(1, 1, 4)
    add_near(0, 6, 8)
    landed(1, 5, 6)
    go(1, 15)
    landed(1, 7, 8)
    go(1, 16)
    work(1, 6, 8)
    add_far(0, 4, 8)
    add_relay(1, 4, 6)
    add_near(1, 1, 4)
    add_relay(1, 6, 8)
    add_near(1, 4, 8)
    add_far(1, 0, 8)

    for a in (0, 1):
        @pl.when(jnp.logical_not(is_home))
        def _():
            @pl.loop(0, 8)
            def _(s):
                rs3(a, s).wait_send()
                rs4(a, s).wait_recv()

        @pl.when(is_home)
        def _():
            @pl.loop(0, 8)
            def _(s):
                rs4(a, s).wait_send()
    result = pltpu.make_async_copy(total, sum_out, w_sem)
    result.start()
    for a in (0, 1):
        for k in range(17):
            gather(a, k).wait_send()

        @pl.loop(0, 8)
        def _(s):
            keep(a, s).wait()
            for d in (0, 1):
                rs1(a, s)[d].wait_send()
                rs2(a, s)[d].wait_send()
    result.wait()


def project(inputs, grad_block, w_qkv, w_out):
    dma = pltpu.SemaphoreType.DMA
    anywhere = pl.BlockSpec(memory_space=pl.ANY)
    vmem = pl.BlockSpec(memory_space=pltpu.VMEM)
    return pl.pallas_call(
        project_kernel,
        name="project",
        out_shape=(
            jax.ShapeDtypeStruct((2, 16, 128, 1536), BF16),
            jax.ShapeDtypeStruct((8, 4, 64, 384), BF16),
        ),
        in_specs=[vmem, vmem, anywhere, vmem],
        out_specs=(anywhere, anywhere),
        scratch_shapes=[
            pltpu.VMEM((2, 16, 128, 1536), BF16),
            pltpu.VMEM((8, 4, 256, 384), BF16),
            pltpu.VMEM((8, 2, 4, 32, 384), BF16),
            pltpu.VMEM((8, 2, 4, 64, 384), BF16),
            pltpu.VMEM((8, 4, 64, 384), BF16),
            pltpu.VMEM((8, 4, 64, 384), BF16),
            pltpu.VMEM((8, 4, 64, 384), BF16),
            pltpu.VMEM((3, 1536, 384), BF16),
            dma((2, 17)), dma((2, 17)),
            dma((2, 8, 2)), dma((2, 8, 2)),
            dma((2, 8, 2)), dma((2, 8, 2)),
            dma((2, 8)), dma((2, 8)),
            dma((2, 8)), dma((2, 8)),
            dma((2, 8)), dma(()), dma((2,)),
        ],
        compiler_params=pltpu.CompilerParams(
            collective_id=1, has_side_effects=True, vmem_limit_bytes=60 << 20
        ),
    )(inputs, grad_block, jnp.transpose(w_qkv, (1, 0, 2)), w_out)


def attend_kernel(
    rows_ref, out,
    kv, scores, slopes, part, twin_part, relay, near, result,
    ag_send, ag_recv, tw_send, tw_recv, s1_send, s1_recv, s2_send, s2_recv, up_send, up_recv, out_sem,
):
    me = Place()
    right, left, twin = me.at(x=1), me.at(x=-1), me.at(core=1)
    is_home = me.core == me.yhi
    scale = 128 ** (-0.5)
    fill = -1e30

    def own(x=0):
        return pl.ds(pl.multiple_of(me.col_x(x) * 64, 64), 64)

    my_rows = pl.ds(pl.multiple_of(me.core * 32, 32), 32)
    low, high = pl.ds(0, 4), pl.ds(4, 4)
    every = pl.ds(0, 8)
    for h in range(3):
        for j in (0, 1):
            kv[j, h, :, own()] = rows_ref[:, h, :, 128 + 128 * j:256 + 128 * j]
    meet([twin, right, left])

    def gather(h, k):
        x, blocks, device = {
            0: (0, every, right),
            1: (0, every, left),
            2: (-1, low, right),
            3: (1, high, left),
            4: (-1, every, twin),
            5: (1, every, twin),
            6: (2, every, twin),
        }[k]
        ref = kv.at[me.core, h, blocks, own(x)]
        return remote(ref, ref, ag_send.at[h, k], ag_recv.at[h, k], device)

    def pass_on(h):
        for d in (0, 1):
            gather(h, d).wait_recv()
            gather(h, 2 + d).start()
            gather(h, 4 + d).start()

    def complete(h):
        gather(h, 2).wait_recv()
        gather(h, 3).wait_recv()
        gather(h, 6).start()
        for k in (4, 5, 6):
            gather(h, k).wait_recv()

    def attend(h):
        query = rows_ref[:, h, my_rows, 0:128].reshape(256, 128)
        cotangent = rows_ref[:, 3, my_rows, h * 128:(h + 1) * 128].reshape(256, 128)
        transposed = (((1,), (1,)), ((), ()))
        first = (((0,), (0,)), ((), ()))

        def masked(b, lanes):
            width = 256 - lanes
            s = lax.dot_general(kv[0, h, b], query[lanes:], transposed, preferred_element_type=F32) * scale
            key_at = b * 256 + lax.broadcasted_iota(jnp.int32, (256, width), 0)
            column = lanes + lax.broadcasted_iota(jnp.int32, (1, width), 1)
            query_at = (column // 32) * 256 + me.x * 64 + me.core * 32 + column % 32
            return jnp.where(key_at <= query_at, s, fill)

        def top(lanes):
            def body(b, m):
                s = masked(b, lanes)
                scores[b, :, lanes:] = s
                return jnp.maximum(m, jnp.max(s, axis=0, keepdims=True))
            return body

        m = lax.fori_loop(0, 4, top(0), jnp.full((1, 256), fill, F32))
        m_high = lax.fori_loop(4, 8, top(128), m[:, 128:])
        m = jnp.concatenate([m[:, :128], m_high], axis=1)

        def sums(lanes, m):
            def body(b, carry):
                total, slope = carry
                e = jnp.exp(scores[b, :, lanes:] - m)
                scores[b, :, lanes:] = e
                dp = lax.dot_general(kv[1, h, b], cotangent[lanes:], transposed, preferred_element_type=F32)
                slopes[b, :, lanes:] = dp
                return (total + jnp.sum(e, axis=0, keepdims=True), slope + jnp.sum(e * dp, axis=0, keepdims=True))
            return body

        zero = jnp.zeros((1, 256), F32)
        total, slope = lax.fori_loop(0, 4, sums(0, m), (zero, zero))
        total_high, slope_high = lax.fori_loop(4, 8, sums(128, m_high), (total[:, 128:], slope[:, 128:]))
        total = jnp.concatenate([total[:, :128], total_high], axis=1)
        slope = jnp.concatenate([slope[:, :128], slope_high], axis=1)
        inverse = 1.0 / total
        slope = slope * inverse

        def grads(lanes):
            def body(b, carry):
                att, dq = carry
                p = scores[b, :, lanes:] * inverse[:, lanes:]
                w = p.astype(BF16)
                ds = (p * (slopes[b, :, lanes:] - slope[:, lanes:]) * scale).astype(BF16)
                part[h, 0, b] = jnp.dot(ds, query[lanes:], preferred_element_type=F32).astype(BF16)
                part[h, 1, b] = jnp.dot(w, cotangent[lanes:], preferred_element_type=F32).astype(BF16)
                att = att + lax.dot_general(kv[1, h, b], w, first, preferred_element_type=F32)
                dq = dq + lax.dot_general(kv[0, h, b], ds, first, preferred_element_type=F32)
                return att, dq
            return body

        square = jnp.zeros((128, 256), F32)
        att, dq = lax.fori_loop(0, 4, grads(0), (square, square))
        att_high, dq_high = lax.fori_loop(4, 8, grads(128), (att[:, 128:], dq[:, 128:]))
        for t, lo, hi in ((0, att, att_high), (1, dq, dq_high)):
            rows = jnp.concatenate([lo[:, :128], hi], axis=1).T.astype(BF16)
            result[t, h, :, my_rows] = rows.reshape(8, 32, 128)

    def to_twin(h):
        return remote(part.at[h, 1 - me.core], twin_part.at[h], tw_send.at[h], tw_recv.at[h], twin)

    def lift(h, t):
        if t < 2:
            ref = result.at[t, h, every, my_rows]
        else:
            ref = result.at[2 + me.core, h]
        return remote(ref, ref, up_send.at[h, t], up_recv.at[h, t], twin)

    def after(h):
        to_twin(h).start()

        @pl.when(jnp.logical_not(is_home))
        def _():
            lift(h, 0).start()
            lift(h, 1).start()

    def rs1(h, d):
        return remote(part.at[h, me.core, (low, high)[d], own(2)], relay.at[h, d],
                      s1_send.at[h, d], s1_recv.at[h, d], (right, left)[d])

    def rs2(h, d):
        return remote(part.at[h, me.core, every, own((1, -1)[d])], near.at[h, d],
                      s2_send.at[h, d], s2_recv.at[h, d], (right, left)[d])

    def add_twin(h):
        to_twin(h).wait_recv()

        @pl.loop(0, 8)
        def _(b):
            part[h, me.core, b] = (part[h, me.core, b].astype(F32) + twin_part[h, b].astype(F32)).astype(BF16)

        for d in (0, 1):
            rs1(h, d).start()

    def add_relay(h):
        for d in (0, 1):
            rs1(h, d).wait_recv()
            here = part.at[h, me.core, (low, high)[d], own((1, -1)[d])]
            here[...] = (here[...].astype(F32) + relay[h, d].astype(F32)).astype(BF16)
            rs2(h, d).start()

    def add_near(h):
        for d in (0, 1):
            rs2(h, d).wait_recv()
        result[2 + me.core, h] = (
            part[h, me.core, :, own()].astype(F32) + near[h, 0].astype(F32) + near[h, 1].astype(F32)
        ).astype(BF16)

        @pl.when(jnp.logical_not(is_home))
        def _():
            lift(h, 2).start()

    for h in range(3):
        gather(h, 0).start()
        gather(h, 1).start()
    pass_on(0)
    pass_on(1)
    complete(0)
    attend(0)
    after(0)
    pass_on(2)
    complete(1)
    add_twin(0)
    attend(1)
    after(1)
    add_relay(0)
    complete(2)
    add_twin(1)
    attend(2)
    after(2)
    add_relay(1)
    add_near(0)
    add_twin(2)
    add_near(1)
    add_relay(2)
    add_near(2)

    @pl.when(jnp.logical_not(is_home))
    def _():
        for h in range(3):
            for t in range(3):
                lift(h, t).wait_send()

    @pl.when(is_home)
    def _():
        their_rows = pl.ds(pl.multiple_of(32 - me.core * 32, 32), 32)
        for h in range(3):
            for t in range(3):
                ref = result.at[t, h, every, their_rows] if t < 2 else result.at[3 - me.core, h]
                remote(ref, ref, up_send.at[h, t], up_recv.at[h, t], twin).wait_recv()

    copy = pltpu.make_async_copy(result, out, out_sem)
    copy.start()
    for h in range(3):
        for k in range(7):
            gather(h, k).wait_send()
        to_twin(h).wait_send()
        for d in (0, 1):
            rs1(h, d).wait_send()
            rs2(h, d).wait_send()
    copy.wait()


def attend_heads(rows):
    dma = pltpu.SemaphoreType.DMA
    return pl.pallas_call(
        attend_kernel,
        name="attend",
        out_shape=jax.ShapeDtypeStruct((4, 3, 8, 64, 128), BF16),
        in_specs=[pl.BlockSpec(memory_space=pltpu.VMEM)],
        out_specs=pl.BlockSpec(memory_space=pl.ANY),
        scratch_shapes=[
            pltpu.VMEM((2, 3, 8, 256, 128), BF16),
            pltpu.VMEM((8, 256, 256), F32),
            pltpu.VMEM((8, 256, 256), F32),
            pltpu.VMEM((3, 2, 8, 256, 128), BF16),
            pltpu.VMEM((3, 8, 256, 128), BF16),
            pltpu.VMEM((3, 2, 4, 64, 128), BF16),
            pltpu.VMEM((3, 2, 8, 64, 128), BF16),
            pltpu.VMEM((4, 3, 8, 64, 128), BF16),
            dma((3, 7)), dma((3, 7)),
            dma((3,)), dma((3,)),
            dma((3, 2)), dma((3, 2)),
            dma((3, 2)), dma((3, 2)),
            dma((3, 3)), dma((3, 3)),
            dma(()),
        ],
        compiler_params=pltpu.CompilerParams(
            collective_id=2, has_side_effects=True, vmem_limit_bytes=60 << 20
        ),
    )(rows)

slice_at = (0, -1, 1, 2)


def combine_kernel(
    all_hbm, rows_hbm, wo_ref,
    block_out, grad_qkv, grad_out,
    held, stage, turned, tokens_g, turned_a, part, twin_part, relay, near, far, final, ours, theirs,
    own_sem, x_sem, g_sem, ag_send, ag_recv, tw_send, tw_recv, s1_send, s1_recv, s2_send, s2_recv, s3_send, s3_recv, end_send, end_recv,
):
    me = Place()
    right, left, across, twin = me.at(x=1), me.at(x=-1), me.at(yhi=1), me.at(core=1)
    up, down, beside = me.at(z=1), me.at(z=-1), me.at(ylo=1)
    is_home = me.core == me.yhi
    low, high, every = pl.ds(0, 4), pl.ds(4, 4), pl.ds(0, 8)

    def rows(i):
        return pl.ds(pl.multiple_of(me.col_x(slice_at[i]) * 64, 64), 64)

    def load_x(i):
        return pltpu.make_async_copy(all_hbm.at[0, every, rows(i)], stage.at[i % 2], x_sem.at[i])

    def load_g(i):
        return pltpu.make_async_copy(all_hbm.at[1, every, rows(i)], tokens_g.at[i], g_sem.at[i])

    def load_own(t):
        return pltpu.make_async_copy(rows_hbm.at[t], held.at[t, :, every, rows(0)], own_sem.at[t])

    @pl.when(is_home)
    def _():
        for t in range(4):
            load_own(t).start()

    for i in range(4):
        load_g(i).start()
    load_x(0).start()
    load_x(1).start()
    meet([right, left, across, twin, up, down, beside])

    def gather(t, k):
        i, blocks, device = {
            0: (0, every, across),
            1: (0, every, right),
            2: (0, every, left),
            3: (1, low, right),
            4: (2, high, left),
        }[k]
        ref = held.at[t, :, blocks, rows(i)]
        return remote(ref, ref, ag_send.at[t, k], ag_recv.at[t, k], device)

    def ready(t):
        @pl.when(is_home)
        def _():
            load_own(t).wait()
            gather(t, 0).start()

        @pl.when(jnp.logical_not(is_home))
        def _():
            gather(t, 0).wait_recv()

        gather(t, 1).start()
        gather(t, 2).start()

    def pass_on(t):
        for d in (0, 1):
            gather(t, 1 + d).wait_recv()
            gather(t, 3 + d).start()

    def complete(t):
        gather(t, 3).wait_recv()
        gather(t, 4).wait_recv()

    def turn(i):
        load_x(i).wait()

        @pl.loop(0, 12)
        def _(n):
            lanes = pl.ds(pl.multiple_of(n * 128, 128), 128)
            turned[i, lanes] = stage[i % 2, :, :, lanes].reshape(512, 128).T

        if i < 2:
            load_x(i + 2).start()

    def to_twin(i):
        return remote(part.at[i, 1 - me.core], twin_part.at[i], tw_send.at[i], tw_recv.at[i], twin)

    def multiply_out(i):
        mine = jnp.concatenate([held[0, h, :, rows(i)].reshape(512, 128) for h in range(3)], axis=1)
        turned_a[...] = mine.T
        load_g(i).wait()

        @pl.loop(0, 2)
        def _(j):
            @pl.loop(0, 2)
            def _(n):
                lanes = pl.ds(pl.multiple_of(j * 768 + n * 384, 384), 384)
                inner = pl.ds(pl.multiple_of(n * 384, 384), 384)
                part[i, j, :, :, :, inner] = jnp.dot(
                    mine, wo_ref[:, :, lanes].reshape(384, 384), preferred_element_type=F32
                ).astype(BF16).reshape(2, 4, 64, 384)

        to_twin(i).start()

        @pl.loop(0, 4)
        def _(n):
            lanes = pl.ds(pl.multiple_of(n * 384, 384), 384)
            term = jnp.dot(
                turned_a[...], tokens_g[i, :, :, lanes].reshape(512, 384), preferred_element_type=F32
            ).reshape(3, 128, 384)
            if i == 0:
                grad_out[:, :, lanes] = term
            else:
                grad_out[:, :, lanes] += term

    def multiply_grads(i):
        @pl.loop(0, 3)
        def _(h):
            grads = jnp.concatenate([held[t, h, :, rows(i)].reshape(512, 128) for t in (1, 2, 3)], axis=1)

            @pl.loop(0, 3)
            def _(m):
                features = pl.ds(pl.multiple_of(m * 512, 512), 512)
                term = jnp.dot(turned[i, features], grads, preferred_element_type=F32)
                if i == 0:
                    grad_qkv[h, features] = term
                else:
                    grad_qkv[h, features] += term

    def z_at(z):
        return lax.rem(me.z + z + 4, 4)

    def rs1(i, d):
        return remote(part.at[i, me.core, d, z_at(2)], relay.at[i, d], s1_send.at[i, d], s1_recv.at[i, d], (up, down)[d])

    def rs2(i, d):
        return remote(part.at[i, me.core, :, z_at((1, -1)[d])], near.at[i, d], s2_send.at[i, d], s2_recv.at[i, d], (up, down)[d])

    def rs3(i):
        return remote(part.at[i, me.core, 1 - me.ylo, me.z], far.at[i], s3_send.at[i], s3_recv.at[i], beside)

    def add(ref, *terms):
        value = ref[...].astype(F32)
        for term in terms:
            value = value + term.astype(F32)
        ref[...] = value.astype(BF16)

    def add_twin(i):
        to_twin(i).wait_recv()

        @pl.loop(0, 4)
        def _(z):
            for y in (0, 1):
                add(part.at[i, me.core, y, z], twin_part[i, y, z])

        for d in (0, 1):
            rs1(i, d).start()

    def add_relay(i):
        for d in (0, 1):
            rs1(i, d).wait_recv()
            add(part.at[i, me.core, d, z_at((1, -1)[d])], relay[i, d])
            rs2(i, d).start()

    def add_near(i):
        for d in (0, 1):
            rs2(i, d).wait_recv()
        for y in (0, 1):
            add(part.at[i, me.core, y, me.z], near[i, 0, y], near[i, 1, y])
        rs3(i).start()

    def add_far(i):
        rs3(i).wait_recv()
        final[rows(i)] = (part[i, me.core, me.ylo, me.z].astype(F32) + far[i].astype(F32)).astype(BF16)

    ready(0)
    ready(1)
    multiply_out(0)
    turn(0)
    add_twin(0)
    turn(1)
    pass_on(0)
    ready(2)
    multiply_out(1)
    multiply_out(2)
    add_relay(0)
    add_twin(1)
    add_twin(2)
    turn(2)
    pass_on(1)
    ready(3)
    complete(0)
    multiply_out(3)
    add_near(0)
    add_relay(1)
    add_relay(2)
    add_twin(3)
    multiply_grads(0)
    turn(3)
    pass_on(2)
    add_near(1)
    add_near(2)
    add_relay(3)
    add_near(3)
    pass_on(3)
    multiply_grads(1)
    multiply_grads(2)
    for i in range(4):
        add_far(i)
    their_rows = pl.ds(pl.multiple_of(128 - me.core * 128, 128), 128)
    end = remote(final.at[their_rows], theirs, end_send, end_recv, twin)
    end.start()
    complete(1)
    complete(2)
    complete(3)
    multiply_grads(3)
    end.wait_recv()
    ours[...] = final[pl.ds(pl.multiple_of(me.core * 128, 128), 128)]

    @pl.when(me.core == 0)
    def _():
        block_out[:, :768] = ours[...]
        block_out[:, 768:] = theirs[...]

    @pl.when(me.core == 1)
    def _():
        block_out[:, :768] = theirs[...]
        block_out[:, 768:] = ours[...]

    @pl.when(is_home)
    def _():
        for t in range(4):
            gather(t, 0).wait_send()

    for t in range(4):
        for k in range(1, 5):
            gather(t, k).wait_send()
    for i in range(4):
        to_twin(i).wait_send()
        for d in (0, 1):
            rs1(i, d).wait_send()
            rs2(i, d).wait_send()
        rs3(i).wait_send()
    end.wait_send()


def combine(tokens, rows, w_out):
    dma = pltpu.SemaphoreType.DMA
    anywhere = pl.BlockSpec(memory_space=pl.ANY)
    vmem = pl.BlockSpec(memory_space=pltpu.VMEM)
    return pl.pallas_call(
        combine_kernel,
        name="combine",
        out_shape=(
            jax.ShapeDtypeStruct((128, 1536), BF16),
            jax.ShapeDtypeStruct((3, 1536, 384), F32),
            jax.ShapeDtypeStruct((3, 128, 1536), F32),
        ),
        in_specs=[anywhere, anywhere, vmem],
        out_specs=(vmem, vmem, vmem),
        scratch_shapes=[
            pltpu.VMEM((4, 3, 8, 256, 128), BF16),
            pltpu.VMEM((2, 8, 64, 1536), BF16),
            pltpu.VMEM((4, 1536, 512), BF16),
            pltpu.VMEM((4, 8, 64, 1536), BF16),
            pltpu.VMEM((384, 512), BF16),
            pltpu.VMEM((4, 2, 2, 4, 64, 768), BF16),
            pltpu.VMEM((4, 2, 4, 64, 768), BF16),
            pltpu.VMEM((4, 2, 64, 768), BF16),
            pltpu.VMEM((4, 2, 2, 64, 768), BF16),
            pltpu.VMEM((4, 64, 768), BF16),
            pltpu.VMEM((256, 768), BF16),
            pltpu.VMEM((128, 768), BF16),
            pltpu.VMEM((128, 768), BF16),
            dma((4,)), dma((4,)), dma((4,)),
            dma((4, 5)), dma((4, 5)),
            dma((4,)), dma((4,)),
            dma((4, 2)), dma((4, 2)),
            dma((4, 2)), dma((4, 2)),
            dma((4,)), dma((4,)),
            dma(()), dma(()),
        ],
        compiler_params=pltpu.CompilerParams(
            collective_id=3, has_side_effects=True, vmem_limit_bytes=62 << 20
        ),
    )(tokens.reshape(2, 8, 256, 1536), rows, w_out)


def local(inputs, w_qkv, w_out, grad_block):
    tokens, sums = project(inputs, grad_block, w_qkv, w_out)
    rows = attend_heads(sums)
    block_out, grad_qkv, grad_out = combine(tokens, rows, w_out)
    return block_out, jnp.transpose(grad_qkv, (1, 0, 2)), grad_out


def solution(mesh):
    placed = (P("row", "col"), P("col", "row", None), P("row", None, "col"), P("row", "col"))
    return jax.shard_map(
        local,
        mesh=mesh,
        in_specs=placed,
        out_specs=(P("row", "col"), P("col", "row", None), P("row", None, "col")),
        check_vma=False,
    )
```

```python
import jax
import jax.numpy as jnp
from jax import lax
from jax.experimental import pallas as pl
from jax.experimental.pallas import tpu as pltpu
from jax.sharding import PartitionSpec as P

MESH = pl.DeviceIdType.MESH
BF16 = jnp.bfloat16
F32 = jnp.float32


class Place:
    def __init__(self):
        r = lax.axis_index("row")
        c = lax.axis_index("col")
        self.ylo, self.z, self.core = r // 8, (r // 2) % 4, r % 2
        self.yhi, self.x = c // 4, c % 4

    def at(self, ylo=0, z=0, core=0, yhi=0, x=0):
        return (
            lax.rem(self.ylo + ylo, 2) * 8 + lax.rem(self.z + z + 4, 4) * 2 + lax.rem(self.core + core, 2),
            lax.rem(self.yhi + yhi, 2) * 4 + lax.rem(self.x + x + 4, 4),
        )

    def slot(self, ylo=0, z=0, core=0):
        return self.at(ylo=ylo, z=z, core=core)[0]

    def col_x(self, x):
        return lax.rem(self.x + x + 4, 4)


def meet(partners):
    barrier = pltpu.get_barrier_semaphore()
    for partner in partners:
        pl.semaphore_signal(barrier, inc=1, device_id=partner, device_id_type=MESH)
    pl.semaphore_wait(barrier, len(partners))


def remote(src, dst, send, recv, device):
    return pltpu.make_async_remote_copy(
        src_ref=src, dst_ref=dst, send_sem=send, recv_sem=recv, device_id=device, device_id_type=MESH
    )


slice_at = (0, -1, 1, 2)


def block_kernel(
    x_ref, g_ref, w_hbm, wo_ref,
    x_out, grads_out, block_out, grad_out,
    held, part, relay, near, far, total, w_ref,
    kv, scores, slopes, grads, twin_grads, grads_relay, grads_near, result,
    wide, turned, block_relay, block_near, block_far, final, theirs,
    ag_send, ag_recv, s1_send, s1_recv, s2_send, s2_recv, s3_send, s3_recv, s4_send, s4_recv, x_sem, w_sem, own_sem,
    kv_send, kv_recv, tw_send, tw_recv, g1_send, g1_recv, g2_send, g2_recv, up_send, up_recv,
    wide_send, wide_recv, here_sem, out_sem, b0_send, b0_recv, b1_send, b1_recv, b2_send, b2_recv, b3_send, b3_recv,
    end_send, end_recv,
):
    me = Place()
    up, down, beside = me.at(z=1), me.at(z=-1), me.at(ylo=1)
    right, left, across, twin = me.at(x=1), me.at(x=-1), me.at(yhi=1), me.at(core=1)
    is_home = me.core == me.yhi
    is_away = jnp.logical_not(is_home)
    scale = 128 ** (-0.5)
    fill = -1e30
    own_rows = (x_ref, g_ref)
    low, high, every = pl.ds(0, 4), pl.ds(4, 4), pl.ds(0, 8)
    my_rows = pl.ds(pl.multiple_of(me.core * 32, 32), 32)
    their_rows = pl.ds(pl.multiple_of(32 - me.core * 32, 32), 32)

    def own(x=0):
        return pl.ds(pl.multiple_of(me.col_x(x) * 64, 64), 64)

    w_copy = pltpu.make_async_copy(w_hbm, w_ref, w_sem)
    w_copy.start()
    own_copy = []
    for a in (0, 1):
        copy = pltpu.make_async_copy(own_rows[a], held.at[a, pl.ds(me.slot() * 2, 2)], own_sem.at[a])
        copy.start()
        own_copy.append(copy)
    meet([beside, up, down, twin, right, left, across])

    def gather(a, k):
        slot, device = {
            0: (me.slot(), beside),
            1: (me.slot(), up),
            2: (me.slot(), down),
            3: (me.slot(ylo=1), up),
            4: (me.slot(ylo=1), down),
            5: (me.slot(z=-1), up),
            6: (me.slot(z=1), down),
            7: (me.slot(ylo=1, z=-1), up),
            8: (me.slot(ylo=1, z=1), down),
            9: (me.slot(), twin),
            10: (me.slot(ylo=1), twin),
            11: (me.slot(z=-1), twin),
            12: (me.slot(z=1), twin),
            13: (me.slot(ylo=1, z=-1), twin),
            14: (me.slot(ylo=1, z=1), twin),
            15: (me.slot(z=2), twin),
            16: (me.slot(ylo=1, z=2), twin),
        }[k]
        if k in (5, 7):
            rows = pl.ds(slot * 2, 1)
        elif k in (6, 8):
            rows = pl.ds(slot * 2 + 1, 1)
        else:
            rows = pl.ds(slot * 2, 2)
        ref = held.at[a, rows]
        src = own_rows[a] if k in (0, 1, 2, 9) else ref
        return remote(src, ref, ag_send.at[a, k], ag_recv.at[a, k], device)

    def go(a, *kinds):
        for k in kinds:
            gather(a, k).start()

    def landed(a, *kinds):
        for k in kinds:
            gather(a, k).wait_recv()

    def block_of(s):
        ylo = jnp.where((s == 1) | (s == 4) | (s == 5) | (s == 7), 1, 0)
        z = jnp.where((s == 2) | (s == 4), 3, jnp.where((s == 3) | (s == 5), 1, jnp.where(s >= 6, 2, 0)))
        return lax.rem(me.ylo + ylo, 2) * 4 + lax.rem(me.z + z, 4)

    def unit(a):
        return pl.ds(0, 3) if a == 0 else pl.ds(3, 1)

    def keep(s):
        block = pl.ds(block_of(s) * 4, 4)
        return pltpu.make_async_copy(held.at[0, block], x_out.at[block], x_sem.at[s])

    def rs1(a, s, d):
        rows = pl.ds(pl.multiple_of(me.col_x(2) * 64 + 32 * d, 32), 32)
        return remote(part.at[s, unit(a), rows], relay.at[s, d, unit(a)], s1_send.at[a, s, d], s1_recv.at[a, s, d], (right, left)[d])

    def rs2(a, s, d):
        return remote(part.at[s, unit(a), own((1, -1)[d])], near.at[s, d, unit(a)],
                      s2_send.at[a, s, d], s2_recv.at[a, s, d], (right, left)[d])

    def rs3(a, s):
        return remote(part.at[s, unit(a), own()], far.at[s, unit(a)], s3_send.at[a, s], s3_recv.at[a, s], across)

    def rs4(a, s):
        ref = total.at[block_of(s), unit(a)]
        return remote(ref, ref, s4_send.at[a, s], s4_recv.at[a, s], twin)

    def each(steps, body):
        lo, hi = steps
        if hi - lo == 1:
            body(lo)
        else:
            pl.loop(lo, hi)(body)

    def work(a, *steps):
        def body(s):
            remote(held.at[a, pl.ds(0, 2)], held.at[a, pl.ds(0, 2)], ag_send.at[a, 9 + s], ag_recv.at[a, 9 + s], twin).wait_recv()
            rows = held.at[a, pl.ds(block_of(s) * 4, 4)]
            if a == 0:
                keep(s).start()

                @pl.loop(0, 3)
                def _(h):
                    part[s, h] = jnp.dot(
                        rows[...].reshape(256, 1536), w_ref[h], preferred_element_type=F32
                    ).astype(BF16)
            else:
                part[s, 3] = lax.dot_general(
                    rows[...].reshape(256, 1536), wo_ref[...].reshape(384, 1536),
                    (((1,), (1,)), ((), ())), preferred_element_type=F32,
                ).astype(BF16)
            for d in (0, 1):
                rs1(a, s, d).start()
        each(steps, body)

    def add(ref, *terms):
        value = ref[...].astype(F32)
        for term in terms:
            value = value + term.astype(F32)
        ref[...] = value.astype(BF16)

    def add_relay(a, *steps):
        def body(s):
            for d in (0, 1):
                rs1(a, s, d).wait_recv()
                rows = pl.ds(pl.multiple_of(me.col_x((1, -1)[d]) * 64 + 32 * d, 32), 32)
                add(part.at[s, unit(a), rows], relay[s, d, unit(a)])
                rs2(a, s, d).start()
        each(steps, body)

    def add_near(a, *steps):
        def body(s):
            for d in (0, 1):
                rs2(a, s, d).wait_recv()
            add(part.at[s, unit(a), own()], near[s, 0, unit(a)], near[s, 1, unit(a)])

            @pl.when(is_away)
            def _():
                rs3(a, s).start()
        each(steps, body)

    def kv_gather(s, k):
        x, rows, device = {
            0: (0, 0, right),
            1: (0, 0, left),
            2: (-1, 1, right),
            3: (1, 2, left),
            4: (-1, 0, twin),
            5: (1, 0, twin),
            6: (2, 0, twin),
        }[k]
        start = me.col_x(x) * 64
        if rows == 0:
            span = pl.ds(pl.multiple_of(start, 64), 64)
        else:
            span = pl.ds(pl.multiple_of(start + 32 * (rows - 1), 32), 32)
        ref = kv.at[me.core, block_of(s), span]
        return remote(ref, ref, kv_send.at[s, k], kv_recv.at[s, k], device)

    def add_far(a, *steps):
        def body(s):
            block = block_of(s)

            @pl.when(is_home)
            def _():
                rs3(a, s).wait_recv()
                total[block, unit(a)] = (
                    part[s, unit(a), own()].astype(F32) + far[s, unit(a)].astype(F32)
                ).astype(BF16)
                rs4(a, s).start()

            @pl.when(is_away)
            def _():
                rs4(a, s).wait_recv()

            if a == 0:
                for j in (0, 1):
                    for h in range(3):
                        kv[j, block, own(), h * 128:(h + 1) * 128] = total[block, h, :, 128 + 128 * j:256 + 128 * j]
                kv_gather(s, 0).start()
                kv_gather(s, 1).start()
        each(steps, body)

    def kv_relay(*steps):
        def body(s):
            for d in (0, 1):
                kv_gather(s, d).wait_recv()
                kv_gather(s, 2 + d).start()
                kv_gather(s, 4 + d).start()
        each(steps, body)

    def kv_done(*steps):
        def body(s):
            kv_gather(s, 2).wait_recv()
            kv_gather(s, 3).wait_recv()
            kv_gather(s, 6).start()
        each(steps, body)

    def kv_whole(*steps):
        def body(s):
            for k in (4, 5, 6):
                kv_gather(s, k).wait_recv()
        each(steps, body)

    def attend(h):
        query = total[:, h, my_rows, 0:128].reshape(256, 128)
        cotangent = total[:, 3, my_rows, h * 128:(h + 1) * 128].reshape(256, 128)
        transposed = (((1,), (1,)), ((), ()))
        first = (((0,), (0,)), ((), ()))

        def masked(b, lanes):
            width = 256 - lanes
            s = lax.dot_general(kv[0, b, :, h * 128:(h + 1) * 128], query[lanes:], transposed, preferred_element_type=F32) * scale
            key_at = b * 256 + lax.broadcasted_iota(jnp.int32, (256, width), 0)
            column = lanes + lax.broadcasted_iota(jnp.int32, (1, width), 1)
            query_at = (column // 32) * 256 + me.x * 64 + me.core * 32 + column % 32
            return jnp.where(key_at <= query_at, s, fill)

        def top(lanes):
            def body(b, m):
                s = masked(b, lanes)
                scores[b, :, lanes:] = s
                return jnp.maximum(m, jnp.max(s, axis=0, keepdims=True))
            return body

        m = lax.fori_loop(0, 4, top(0), jnp.full((1, 256), fill, F32))
        m_high = lax.fori_loop(4, 8, top(128), m[:, 128:])
        m = jnp.concatenate([m[:, :128], m_high], axis=1)

        def sums(lanes, m):
            def body(b, carry):
                norm, slope = carry
                e = jnp.exp(scores[b, :, lanes:] - m)
                scores[b, :, lanes:] = e
                dp = lax.dot_general(kv[1, b, :, h * 128:(h + 1) * 128], cotangent[lanes:], transposed, preferred_element_type=F32)
                slopes[b, :, lanes:] = dp
                return (norm + jnp.sum(e, axis=0, keepdims=True), slope + jnp.sum(e * dp, axis=0, keepdims=True))
            return body

        zero = jnp.zeros((1, 256), F32)
        norm, slope = lax.fori_loop(0, 4, sums(0, m), (zero, zero))
        norm_high, slope_high = lax.fori_loop(4, 8, sums(128, m_high), (norm[:, 128:], slope[:, 128:]))
        norm = jnp.concatenate([norm[:, :128], norm_high], axis=1)
        slope = jnp.concatenate([slope[:, :128], slope_high], axis=1)
        inverse = 1.0 / norm
        slope = slope * inverse

        def backward(lanes):
            def body(b, carry):
                att, dq = carry
                p = scores[b, :, lanes:] * inverse[:, lanes:]
                w = p.astype(BF16)
                ds = (p * (slopes[b, :, lanes:] - slope[:, lanes:]) * scale).astype(BF16)
                grads[h, 0, b] = jnp.dot(ds, query[lanes:], preferred_element_type=F32).astype(BF16)
                grads[h, 1, b] = jnp.dot(w, cotangent[lanes:], preferred_element_type=F32).astype(BF16)
                att = att + lax.dot_general(kv[1, b, :, h * 128:(h + 1) * 128], w, first, preferred_element_type=F32)
                dq = dq + lax.dot_general(kv[0, b, :, h * 128:(h + 1) * 128], ds, first, preferred_element_type=F32)
                return att, dq
            return body

        square = jnp.zeros((128, 256), F32)
        att, dq = lax.fori_loop(0, 4, backward(0), (square, square))
        att_high, dq_high = lax.fori_loop(4, 8, backward(128), (att[:, 128:], dq[:, 128:]))
        for t, lo, hi in ((0, att, att_high), (1, dq, dq_high)):
            rows = jnp.concatenate([lo[:, :128], hi], axis=1).T.astype(BF16)
            result[t, h, :, my_rows] = rows.reshape(8, 32, 128)

    def to_twin(h):
        return remote(grads.at[h, 1 - me.core], twin_grads.at[h], tw_send.at[h], tw_recv.at[h], twin)

    def gs1(h, d):
        return remote(grads.at[h, me.core, (low, high)[d], own(2)], grads_relay.at[h, d],
                      g1_send.at[h, d], g1_recv.at[h, d], (right, left)[d])

    def gs2(h, d):
        return remote(grads.at[h, me.core, every, own((1, -1)[d])], grads_near.at[h, d],
                      g2_send.at[h, d], g2_recv.at[h, d], (right, left)[d])

    def add_twin(h):
        to_twin(h).wait_recv()

        @pl.loop(0, 8)
        def _(b):
            add(grads.at[h, me.core, b], twin_grads[h, b])

        for d in (0, 1):
            gs1(h, d).start()

    def add_grads_relay(h):
        for d in (0, 1):
            gs1(h, d).wait_recv()
            add(grads.at[h, me.core, (low, high)[d], own((1, -1)[d])], grads_relay[h, d])
            gs2(h, d).start()

    def add_grads_near(h):
        for d in (0, 1):
            gs2(h, d).wait_recv()
        result[2 + me.core, h] = (
            grads[h, me.core, :, own()].astype(F32) + grads_near[h, 0].astype(F32) + grads_near[h, 1].astype(F32)
        ).astype(BF16)

        @pl.when(is_away)
        def _():
            lift(h, 2).start()

    def lift(h, t):
        if t < 2:
            ref = result.at[t, h, every, my_rows]
        else:
            ref = result.at[2 + me.core, h]
        return remote(ref, ref, up_send.at[h, t], up_recv.at[h, t], twin)

    def lifted(h, t):
        ref = result.at[t, h, every, their_rows] if t < 2 else result.at[3 - me.core, h]
        remote(ref, ref, up_send.at[h, t], up_recv.at[h, t], twin).wait_recv()

    def after(h):
        to_twin(h).start()

        @pl.when(is_away)
        def _():
            lift(h, 0).start()
            lift(h, 1).start()

    def spread(h, t, k):
        x, blocks, device = {
            0: (0, every, across),
            1: (0, every, right),
            2: (0, every, left),
            3: (-1, low, right),
            4: (1, high, left),
        }[k]
        ref = wide.at[t, h, blocks, own(x)]
        src = result.at[t, h] if k == 0 else ref
        return remote(src, ref, wide_send.at[h, t, k], wide_recv.at[h, t, k], device)

    def here(h, t):
        return pltpu.make_async_copy(result.at[t, h], wide.at[t, h, every, own()], here_sem.at[h, t])

    def spread_home(h, types):
        @pl.when(is_home)
        def _():
            if types[0] < 2:
                lifted(h, 0)
                lifted(h, 1)
            else:
                lifted(h, 2)
            for t in types:
                spread(h, t, 0).start()
                here(h, t).start()
            for t in types:
                here(h, t).wait()
                spread(h, t, 1).start()
                spread(h, t, 2).start()

    def spread_away(h, types):
        @pl.when(is_away)
        def _():
            for t in types:
                spread(h, t, 0).wait_recv()
                spread(h, t, 1).start()
                spread(h, t, 2).start()

    def spread_relay(h, types):
        for t in types:
            for d in (0, 1):
                spread(h, t, 1 + d).wait_recv()
                spread(h, t, 3 + d).start()

    def keep_grads(h, t):
        return pltpu.make_async_copy(wide.at[t, h], grads_out.at[t - 1, h], out_sem.at[h, t - 1])

    def spread_done(h, types):
        for t in types:
            spread(h, t, 3).wait_recv()
            spread(h, t, 4).wait_recv()
            if t > 0:
                keep_grads(h, t).start()

    def block_lanes(core, n=None):
        if n is None:
            return pl.ds(pl.multiple_of(core * 768, 768), 768)
        return pl.ds(pl.multiple_of(core * 768 + n * 384, 384), 384)

    def b0(i, n):
        return remote(held.at[0, pl.ds(i * 8, 8), :, block_lanes(1 - me.core, n)], near.at[:, n, i],
                      b0_send.at[i, n], b0_recv.at[i, n], twin)

    def z_at(z):
        return lax.rem(me.z + z + 4, 4)

    def term_at(i, y, z):
        return held.at[0, i * 8 + y * 4 + z, :, block_lanes(me.core)]

    def b1(i, d):
        return remote(term_at(i, d, z_at(2)), block_relay.at[i, d], b1_send.at[i, d], b1_recv.at[i, d], (up, down)[d])

    def b2(i, d, y):
        return remote(term_at(i, y, z_at((1, -1)[d])), block_near.at[i, d, y], b2_send.at[i, d, y], b2_recv.at[i, d, y], (up, down)[d])

    def b3(i):
        return remote(term_at(i, 1 - me.ylo, me.z), block_far.at[i], b3_send.at[i], b3_recv.at[i], beside)

    def multiply_out(i):
        mine = jnp.concatenate([wide[0, h, :, own(slice_at[i])].reshape(512, 128) for h in range(3)], axis=1)
        turned[...] = mine.T

        @pl.loop(0, 4)
        def _(n):
            lanes = pl.ds(pl.multiple_of(n * 384, 384), 384)
            held[0, pl.ds(i * 8, 8), :, lanes] = jnp.dot(
                mine, wo_ref[:, :, lanes].reshape(384, 384), preferred_element_type=F32
            ).astype(BF16).reshape(8, 64, 384)

        b0(i, 0).start()
        b0(i, 1).start()

        @pl.loop(0, 4)
        def _(n):
            lanes = pl.ds(pl.multiple_of(n * 384, 384), 384)
            tokens = [held[1, b * 4 + me.col_x(slice_at[i]), :, lanes] for b in range(8)]
            term = jnp.dot(
                turned[...], jnp.concatenate(tokens, axis=0), preferred_element_type=F32
            ).reshape(3, 128, 384)
            if i == 0:
                grad_out[:, :, lanes] = term
            else:
                grad_out[:, :, lanes] += term

    def add_block_twin(i):
        for n in (0, 1):
            b0(i, n).wait_recv()

            @pl.loop(0, 8)
            def _(b):
                add(held.at[0, i * 8 + b, :, block_lanes(me.core, n)], near[b, n, i])

        for d in (0, 1):
            b1(i, d).start()

    def add_block_relay(i):
        for d in (0, 1):
            b2(i, d, 1 - d).start()
        for d in (0, 1):
            b1(i, d).wait_recv()
            add(term_at(i, d, z_at((1, -1)[d])), block_relay[i, d])
            b2(i, d, d).start()

    def add_block_near(i):
        for d in (0, 1):
            for y in (0, 1):
                b2(i, d, y).wait_recv()
        for y in (0, 1):
            add(term_at(i, y, me.z), block_near[i, 0, y], block_near[i, 1, y])
        b3(i).start()

    def add_block_far(i):
        b3(i).wait_recv()
        final[own(slice_at[i])] = (term_at(i, me.ylo, me.z)[...].astype(F32) + block_far[i].astype(F32)).astype(BF16)

    go(0, 9, 0, 1, 2)
    go(1, 9)
    w_copy.wait()
    for copy in own_copy:
        copy.wait()
    work(0, 0, 1)
    work(1, 0, 1)
    landed(0, 0)
    go(0, 3, 4, 10)
    go(1, 0)
    landed(0, 1)
    go(0, 5, 11)
    landed(0, 2)
    go(0, 6, 12)
    work(0, 1, 4)
    add_relay(0, 0, 1)
    add_relay(1, 0, 1)
    add_relay(0, 1, 3)
    landed(0, 3)
    go(0, 7, 13)
    landed(0, 4)
    go(0, 8, 14)
    go(1, 1, 2)
    work(0, 4, 6)
    add_relay(0, 3, 4)
    add_near(0, 0, 1)
    add_near(1, 0, 1)
    landed(0, 5, 6)
    go(0, 15)
    landed(1, 0)
    go(1, 3, 4, 10)
    landed(0, 7, 8)
    go(0, 16)
    work(0, 6, 8)
    work(1, 1, 2)
    add_near(0, 1, 4)
    add_relay(0, 4, 6)
    add_far(0, 0, 1)
    landed(1, 1)
    go(1, 5, 11)
    landed(1, 2)
    go(1, 6, 12)
    work(1, 2, 4)
    add_far(0, 1, 4)
    add_relay(0, 6, 8)
    add_near(0, 4, 6)
    kv_relay(0, 1)
    landed(1, 3)
    go(1, 7, 13)
    landed(1, 4)
    go(1, 8, 14)
    work(1, 4, 6)
    add_far(0, 4, 6)
    kv_relay(1, 4)
    add_near(0, 6, 8)
    add_relay(1, 1, 4)
    kv_done(0, 1)
    landed(1, 5, 6)
    go(1, 15)
    landed(1, 7, 8)
    go(1, 16)
    work(1, 6, 8)
    add_far(0, 6, 8)
    kv_relay(4, 6)
    kv_done(1, 4)
    add_relay(1, 4, 6)
    add_near(1, 1, 4)
    kv_relay(6, 8)
    kv_done(4, 6)
    add_relay(1, 6, 8)
    add_near(1, 4, 6)
    add_far(1, 0, 4)
    add_near(1, 6, 8)
    kv_done(6, 8)
    add_far(1, 4, 8)
    kv_whole(0, 8)

    first, second = (0, 1), (2, 3)
    attend(0)
    after(0)
    spread_home(0, first)
    add_twin(0)
    attend(1)
    after(1)
    spread_home(1, first)
    spread_away(0, first)
    add_twin(1)
    add_grads_relay(0)
    spread_relay(0, first)
    attend(2)
    after(2)
    spread_home(2, first)
    spread_away(1, first)
    add_twin(2)
    add_grads_relay(1)
    add_grads_near(0)
    spread_relay(1, first)
    spread_away(2, first)
    spread_home(0, second)
    for k in range(17):
        gather(0, k).wait_send()
    pl.loop(0, 8)(lambda s: keep(s).wait())
    multiply_out(0)
    spread_done(0, first)
    add_grads_relay(2)
    spread_relay(2, first)
    add_grads_near(1)
    spread_away(0, second)
    spread_home(1, second)
    add_block_twin(0)
    multiply_out(1)
    multiply_out(2)
    add_grads_near(2)
    spread_away(1, second)
    spread_home(2, second)
    spread_relay(0, second)
    add_block_twin(1)
    add_block_twin(2)
    add_block_relay(0)
    spread_away(2, second)
    spread_done(1, first)
    spread_done(2, first)
    multiply_out(3)
    spread_relay(1, second)
    add_block_near(0)
    add_block_relay(1)
    add_block_relay(2)
    add_block_twin(3)
    spread_relay(2, second)
    add_block_near(1)
    add_block_near(2)
    add_block_relay(3)
    for i in range(3):
        add_block_far(i)
    spread_done(0, second)
    spread_done(1, second)
    add_block_near(3)
    add_block_far(3)
    their_half = pl.ds(pl.multiple_of(128 - me.core * 128, 128), 128)
    end = remote(final.at[their_half], theirs, end_send, end_recv, twin)
    end.start()
    end.wait_recv()
    mine = final[pl.ds(pl.multiple_of(me.core * 128, 128), 128)]

    @pl.when(me.core == 0)
    def _():
        block_out[:, :768] = mine
        block_out[:, 768:] = theirs[...]

    @pl.when(me.core == 1)
    def _():
        block_out[:, :768] = theirs[...]
        block_out[:, 768:] = mine

    spread_done(2, second)

    @pl.when(is_away)
    def _():
        for a in (0, 1):
            pl.loop(0, 8)(lambda s: rs3(a, s).wait_send())
        for h in range(3):
            for t in range(3):
                lift(h, t).wait_send()

    @pl.when(is_home)
    def _():
        for a in (0, 1):
            pl.loop(0, 8)(lambda s: rs4(a, s).wait_send())
        for h in range(3):
            for t in range(4):
                spread(h, t, 0).wait_send()

    for k in range(17):
        gather(1, k).wait_send()

    @pl.loop(0, 8)
    def _(s):
        for a in (0, 1):
            for d in (0, 1):
                rs1(a, s, d).wait_send()
                rs2(a, s, d).wait_send()
        for k in range(7):
            kv_gather(s, k).wait_send()

    for h in range(3):
        to_twin(h).wait_send()
        for d in (0, 1):
            gs1(h, d).wait_send()
            gs2(h, d).wait_send()
        for t in range(4):
            for k in range(1, 5):
                spread(h, t, k).wait_send()
            if t > 0:
                keep_grads(h, t).wait()
    for i in range(4):
        for d in (0, 1):
            b0(i, d).wait_send()
            b1(i, d).wait_send()
            for y in (0, 1):
                b2(i, d, y).wait_send()
        b3(i).wait_send()
    end.wait_send()


def block(inputs, grad_block, w_qkv, w_out):
    dma = pltpu.SemaphoreType.DMA
    anywhere = pl.BlockSpec(memory_space=pl.ANY)
    vmem = pl.BlockSpec(memory_space=pltpu.VMEM)
    return pl.pallas_call(
        block_kernel,
        name="block",
        out_shape=(
            jax.ShapeDtypeStruct((32, 64, 1536), BF16),
            jax.ShapeDtypeStruct((3, 3, 8, 256, 128), BF16),
            jax.ShapeDtypeStruct((128, 1536), BF16),
            jax.ShapeDtypeStruct((3, 128, 1536), F32),
        ),
        in_specs=[vmem, vmem, anywhere, vmem],
        out_specs=(anywhere, anywhere, vmem, vmem),
        scratch_shapes=[
            pltpu.VMEM((2, 32, 64, 1536), BF16),
            pltpu.VMEM((8, 4, 256, 384), BF16),
            pltpu.VMEM((8, 2, 4, 32, 384), BF16),
            pltpu.VMEM((8, 2, 4, 64, 384), BF16),
            pltpu.VMEM((8, 4, 64, 384), BF16),
            pltpu.VMEM((8, 4, 64, 384), BF16),
            pltpu.VMEM((3, 1536, 384), BF16),
            pltpu.VMEM((2, 8, 256, 384), BF16),
            pltpu.VMEM((8, 256, 256), F32),
            pltpu.VMEM((8, 256, 256), F32),
            pltpu.VMEM((3, 2, 8, 256, 128), BF16),
            pltpu.VMEM((3, 8, 256, 128), BF16),
            pltpu.VMEM((3, 2, 4, 64, 128), BF16),
            pltpu.VMEM((3, 2, 8, 64, 128), BF16),
            pltpu.VMEM((4, 3, 8, 64, 128), BF16),
            pltpu.VMEM((4, 3, 8, 256, 128), BF16),
            pltpu.VMEM((384, 512), BF16),
            pltpu.VMEM((4, 2, 64, 768), BF16),
            pltpu.VMEM((4, 2, 2, 64, 768), BF16),
            pltpu.VMEM((4, 64, 768), BF16),
            pltpu.VMEM((256, 768), BF16),
            pltpu.VMEM((128, 768), BF16),
            dma((2, 17)), dma((2, 17)),
            dma((2, 8, 2)), dma((2, 8, 2)),
            dma((2, 8, 2)), dma((2, 8, 2)),
            dma((2, 8)), dma((2, 8)),
            dma((2, 8)), dma((2, 8)),
            dma((8,)), dma(()), dma((2,)),
            dma((8, 7)), dma((8, 7)),
            dma((3,)), dma((3,)),
            dma((3, 2)), dma((3, 2)),
            dma((3, 2)), dma((3, 2)),
            dma((3, 3)), dma((3, 3)),
            dma((3, 4, 5)), dma((3, 4, 5)),
            dma((3, 4)), dma((3, 3)),
            dma((4, 2)), dma((4, 2)),
            dma((4, 2)), dma((4, 2)),
            dma((4, 2, 2)), dma((4, 2, 2)),
            dma((4,)), dma((4,)),
            dma(()), dma(()),
        ],
        compiler_params=pltpu.CompilerParams(
            collective_id=1, has_side_effects=True, vmem_limit_bytes=63 << 20
        ),
    )(inputs.reshape(2, 64, 1536), grad_block.reshape(2, 64, 1536), jnp.transpose(w_qkv, (1, 0, 2)), w_out)


def weight_kernel(x_ref, rows_hbm, block_hbm, grad_out_hbm, out_ref, block_copy, grad_out_copy, rows, sem):
    step = pl.program_id(0)
    copies = [
        pltpu.make_async_copy(block_hbm, block_copy, sem.at[3]),
        pltpu.make_async_copy(grad_out_hbm, grad_out_copy, sem.at[4]),
    ]

    @pl.when(step == 0)
    def _():
        loads = [pltpu.make_async_copy(rows_hbm.at[:, h], rows.at[h], sem.at[h]) for h in range(3)]
        for load in loads:
            load.start()
        for copy in copies:
            copy.start()
        for load in loads:
            load.wait()

    turned = x_ref[...].reshape(2048, 256).T
    for h in range(3):
        factor = jnp.concatenate([rows[h, t].reshape(2048, 128) for t in range(3)], axis=1)
        out_ref[h] = jnp.dot(turned, factor, preferred_element_type=F32)

    @pl.when(step == pl.num_programs(0) - 1)
    def _():
        for copy in copies:
            copy.wait()


def weight_grad(tokens, rows, block_rows, grad_out):
    anywhere = pl.BlockSpec(memory_space=pl.ANY)
    return pl.pallas_call(
        weight_kernel,
        name="weight_grad",
        grid=(6,),
        out_shape=(
            jax.ShapeDtypeStruct((3, 1536, 384), F32),
            jax.ShapeDtypeStruct((128, 1536), BF16),
            jax.ShapeDtypeStruct((3, 128, 1536), F32),
        ),
        in_specs=[pl.BlockSpec((32, 64, 256), lambda m: (0, 0, m)), anywhere, anywhere, anywhere],
        out_specs=(pl.BlockSpec((3, 256, 384), lambda m: (0, m, 0)), anywhere, anywhere),
        scratch_shapes=[pltpu.VMEM((3, 3, 8, 256, 128), BF16), pltpu.SemaphoreType.DMA((5,))],
        compiler_params=pltpu.CompilerParams(vmem_limit_bytes=48 << 20),
    )(tokens, rows, block_rows, grad_out)


def local(inputs, w_qkv, w_out, grad_block):
    tokens, rows, block_rows, grad_out = block(inputs, grad_block, w_qkv, w_out)
    grad_qkv, block_out, grad_out = weight_grad(tokens, rows, block_rows, grad_out)
    return block_out, jnp.transpose(grad_qkv, (1, 0, 2)), grad_out


def solution(mesh):
    placed = (P("row", "col"), P("col", "row", None), P("row", None, "col"), P("row", "col"))
    return jax.shard_map(
        local,
        mesh=mesh,
        in_specs=placed,
        out_specs=(P("row", "col"), P("col", "row", None), P("row", None, "col")),
        check_vma=False,
    )
```

```python
import jax
import jax.numpy as jnp
from jax import lax
from jax.experimental import pallas as pl
from jax.experimental.pallas import tpu as pltpu
from jax.sharding import PartitionSpec as P

MESH = pl.DeviceIdType.MESH
BF16 = jnp.bfloat16
F32 = jnp.float32


class Place:
    def __init__(self):
        r = lax.axis_index("row")
        c = lax.axis_index("col")
        self.ylo, self.z, self.core = r // 8, (r // 2) % 4, r % 2
        self.yhi, self.x = c // 4, c % 4

    def at(self, ylo=0, z=0, core=0, yhi=0, x=0):
        return (
            lax.rem(self.ylo + ylo, 2) * 8 + lax.rem(self.z + z + 4, 4) * 2 + lax.rem(self.core + core, 2),
            lax.rem(self.yhi + yhi, 2) * 4 + lax.rem(self.x + x + 4, 4),
        )

    def slot(self, ylo=0, z=0, core=0):
        return self.at(ylo=ylo, z=z, core=core)[0]

    def col_x(self, x):
        return lax.rem(self.x + x + 4, 4)


def meet(partners):
    barrier = pltpu.get_barrier_semaphore()
    for partner in partners:
        pl.semaphore_signal(barrier, inc=1, device_id=partner, device_id_type=MESH)
    pl.semaphore_wait(barrier, len(partners))


def remote(src, dst, send, recv, device):
    return pltpu.make_async_remote_copy(
        src_ref=src, dst_ref=dst, send_sem=send, recv_sem=recv, device_id=device, device_id_type=MESH
    )


slice_at = (0, -1, 1, 2)
along_x_first = (1,)
across_first = ()


def block_kernel(
    x_hbm, g_hbm, w_hbm, wo_hbm,
    turned_out, grads_out, block_hbm, grad_out_hbm,
    held, part, relay, near, far, crossed, total, w_ref, wo_ref, block_out, grad_out,
    kv, scores, slopes, grads, twin_grads, grads_relay, grads_near, result,
    wide, turned, block_relay, block_near, block_far, final, theirs,
    ag_send, ag_recv, s1_send, s1_recv, s2_send, s2_recv, s3_send, s3_recv, s4_send, s4_recv, x_sem, w_sem, own_sem, cross_send, cross_recv, last_sem,
    kv_send, kv_recv, tw_send, tw_recv, g1_send, g1_recv, g2_send, g2_recv, up_send, up_recv,
    wide_send, wide_recv, here_sem, out_sem, b0_send, b0_recv, b1_send, b1_recv, b2_send, b2_recv, b3_send, b3_recv,
    end_send, end_recv,
):
    me = Place()
    up, down, beside = me.at(z=1), me.at(z=-1), me.at(ylo=1)
    right, left, across, twin = me.at(x=1), me.at(x=-1), me.at(yhi=1), me.at(core=1)
    is_home = me.core == me.yhi
    is_away = jnp.logical_not(is_home)
    scale = 128 ** (-0.5)
    fill = -1e30
    low, high, every = pl.ds(0, 4), pl.ds(4, 4), pl.ds(0, 8)
    my_rows = pl.ds(pl.multiple_of(me.core * 32, 32), 32)
    their_rows = pl.ds(pl.multiple_of(32 - me.core * 32, 32), 32)

    def own(x=0):
        return pl.ds(pl.multiple_of(me.col_x(x) * 64, 64), 64)

    own_copy = [
        pltpu.make_async_copy(ref, held.at[a, pl.ds(me.slot() * 2, 2)], own_sem.at[a])
        for a, ref in enumerate((x_hbm, g_hbm))
    ]
    w_copy = pltpu.make_async_copy(w_hbm, w_ref, w_sem.at[0])
    wo_copy = pltpu.make_async_copy(wo_hbm, wo_ref, w_sem.at[1])
    own_copy[0].start()
    w_copy.start()
    own_copy[1].start()
    wo_copy.start()
    meet([beside, up, down, twin, right, left, across])

    def gather(a, k):
        slot, device = {
            0: (me.slot(), beside),
            1: (me.slot(), up),
            2: (me.slot(), down),
            3: (me.slot(ylo=1), up),
            4: (me.slot(ylo=1), down),
            5: (me.slot(z=-1), up),
            6: (me.slot(z=1), down),
            7: (me.slot(ylo=1, z=-1), up),
            8: (me.slot(ylo=1, z=1), down),
            9: (me.slot(), twin),
            10: (me.slot(ylo=1), twin),
            11: (me.slot(z=-1), twin),
            12: (me.slot(z=1), twin),
            13: (me.slot(ylo=1, z=-1), twin),
            14: (me.slot(ylo=1, z=1), twin),
            15: (me.slot(z=2), twin),
            16: (me.slot(ylo=1, z=2), twin),
        }[k]
        if k in (5, 7):
            rows = pl.ds(slot * 2, 1)
        elif k in (6, 8):
            rows = pl.ds(slot * 2 + 1, 1)
        else:
            rows = pl.ds(slot * 2, 2)
        ref = held.at[a, rows]
        return remote(ref, ref, ag_send.at[a, k], ag_recv.at[a, k], device)

    def go(a, *kinds):
        for k in kinds:
            gather(a, k).start()

    def landed(a, *kinds):
        for k in kinds:
            gather(a, k).wait_recv()

    def block_of(s):
        ylo = jnp.where((s == 1) | (s == 4) | (s == 5) | (s == 7), 1, 0)
        z = jnp.where((s == 2) | (s == 4), 3, jnp.where((s == 3) | (s == 5), 1, jnp.where(s >= 6, 2, 0)))
        return lax.rem(me.ylo + ylo, 2) * 4 + lax.rem(me.z + z, 4)

    def unit(a):
        return pl.ds(0, 3) if a == 0 else pl.ds(3, 1)

    def keep(s):
        columns = pl.ds(pl.multiple_of(block_of(s) * 256, 256), 256)
        return pltpu.make_async_copy(w_ref.at[s % 3, :, 0:256], turned_out.at[:, columns], x_sem.at[s])

    def turn(*steps):
        for s in range(*steps):
            if s >= 3:
                keep(s - 3).wait()

            @pl.loop(0, 12)
            def _(n):
                lanes = pl.ds(pl.multiple_of(n * 128, 128), 128)
                rows = held[0, pl.ds(block_of(s) * 4, 4), :, lanes].reshape(256, 128)
                w_ref[s % 3, lanes, 0:256] = rows.T

            keep(s).start()

    def rs1(a, s, d):
        rows = pl.ds(pl.multiple_of(me.col_x(2) * 64 + 32 * d, 32), 32)
        return remote(part.at[s, unit(a), rows], relay.at[s, d, unit(a)], s1_send.at[a, s, d], s1_recv.at[a, s, d], (right, left)[d])

    def rs2(a, s, d):
        return remote(part.at[s, unit(a), own((1, -1)[d])], near.at[s, d, unit(a)],
                      s2_send.at[a, s, d], s2_recv.at[a, s, d], (right, left)[d])

    def rs3(a, s):
        return remote(part.at[s, unit(a), own()], far.at[s, unit(a)], s3_send.at[a, s], s3_recv.at[a, s], across)

    def rs4(a, s):
        ref = total.at[block_of(s), unit(a)]
        return remote(ref, ref, s4_send.at[a, s], s4_recv.at[a, s], twin)

    def is_crossed(a, steps):
        return a == 0 and steps[0] in across_first

    def cross(s):
        return remote(part.at[s, unit(0)], crossed.at[s - min(across_first)],
                      cross_send.at[s - min(across_first)], cross_recv.at[s - min(across_first)], across)

    def each(steps, body):
        lo, hi = steps
        if hi - lo == 1:
            body(lo)
        else:
            pl.loop(lo, hi)(body)

    def work(a, *steps):
        def body(s):
            remote(held.at[a, pl.ds(0, 2)], held.at[a, pl.ds(0, 2)], ag_send.at[a, 9 + s], ag_recv.at[a, 9 + s], twin).wait_recv()
            rows = held.at[a, pl.ds(block_of(s) * 4, 4)]
            if a == 0:
                @pl.loop(0, 3)
                def _(h):
                    part[s, h] = jnp.dot(
                        rows[...].reshape(256, 1536), w_ref[h], preferred_element_type=F32
                    ).astype(BF16)
            else:
                part[s, 3] = lax.dot_general(
                    rows[...].reshape(256, 1536), wo_ref[...].reshape(384, 1536),
                    (((1,), (1,)), ((), ())), preferred_element_type=F32,
                ).astype(BF16)
            if is_crossed(a, steps):
                pl.when(is_away)(lambda: cross(s).start())
            else:
                for d in (0, 1):
                    rs1(a, s, d).start()
        each(steps, body)

    def add_crossed(*steps):
        @pl.when(is_home)
        def _():
            def body(s):
                cross(s).wait_recv()
                for h in range(3):
                    add(part.at[s, h], crossed[s - min(across_first), h])
                for d in (0, 1):
                    rs1(0, s, d).start()
            each(steps, body)

    def add(ref, *terms):
        value = ref[...].astype(F32)
        for term in terms:
            value = value + term.astype(F32)
        ref[...] = value.astype(BF16)

    def add_relay(a, *steps):
        def body(s):
            for d in (0, 1):
                rs1(a, s, d).wait_recv()
                rows = pl.ds(pl.multiple_of(me.col_x((1, -1)[d]) * 64 + 32 * d, 32), 32)
                add(part.at[s, unit(a), rows], relay[s, d, unit(a)])
                rs2(a, s, d).start()
        if is_crossed(a, steps):
            pl.when(is_home)(lambda: each(steps, body))
        else:
            each(steps, body)

    def add_near(a, *steps):
        def body(s):
            for d in (0, 1):
                rs2(a, s, d).wait_recv()
            add(part.at[s, unit(a), own()], near[s, 0, unit(a)], near[s, 1, unit(a)])
            if not is_crossed(a, steps):
                pl.when(is_away)(lambda: rs3(a, s).start())
        if is_crossed(a, steps):
            pl.when(is_home)(lambda: each(steps, body))
        else:
            each(steps, body)

    def kv_gather(s, k):
        x, rows, device = {
            0: (0, 0, right),
            1: (0, 0, left),
            2: (-1, 1, right),
            3: (1, 2, left),
            4: (-1, 0, twin),
            5: (1, 0, twin),
            6: (2, 0, twin),
        }[k]
        start = me.col_x(x) * 64
        if rows == 0:
            span = pl.ds(pl.multiple_of(start, 64), 64)
        else:
            span = pl.ds(pl.multiple_of(start + 32 * (rows - 1), 32), 32)
        ref = kv.at[me.core, block_of(s), span]
        return remote(ref, ref, kv_send.at[s, k], kv_recv.at[s, k], device)

    def add_far(a, *steps):
        def body(s):
            block = block_of(s)

            @pl.when(is_home)
            def _():
                if is_crossed(a, steps):
                    total[block, unit(a)] = part[s, unit(a), own()]
                else:
                    rs3(a, s).wait_recv()
                    total[block, unit(a)] = (
                        part[s, unit(a), own()].astype(F32) + far[s, unit(a)].astype(F32)
                    ).astype(BF16)
                rs4(a, s).start()

            @pl.when(is_away)
            def _():
                rs4(a, s).wait_recv()

            if a == 0:
                for j in (0, 1):
                    for h in range(3):
                        kv[j, block, own(), h * 128:(h + 1) * 128] = total[block, h, :, 128 + 128 * j:256 + 128 * j]
                kv_gather(s, 0).start()
                kv_gather(s, 1).start()
        each(steps, body)

    def kv_relay(*steps):
        def body(s):
            for d in (0, 1):
                kv_gather(s, d).wait_recv()
                kv_gather(s, 2 + d).start()
                kv_gather(s, 4 + d).start()
        each(steps, body)

    def kv_done(*steps):
        def body(s):
            kv_gather(s, 2).wait_recv()
            kv_gather(s, 3).wait_recv()
            kv_gather(s, 6).start()
        each(steps, body)

    def kv_whole(*steps):
        def body(s):
            for k in (4, 5, 6):
                kv_gather(s, k).wait_recv()
        each(steps, body)

    def attend(h):
        query = total[:, h, my_rows, 0:128].reshape(256, 128)
        cotangent = total[:, 3, my_rows, h * 128:(h + 1) * 128].reshape(256, 128)
        transposed = (((1,), (1,)), ((), ()))
        first = (((0,), (0,)), ((), ()))

        def masked(b, lanes):
            width = 256 - lanes
            s = lax.dot_general(kv[0, b, :, h * 128:(h + 1) * 128], query[lanes:], transposed, preferred_element_type=F32) * scale
            key_at = b * 256 + lax.broadcasted_iota(jnp.int32, (256, width), 0)
            column = lanes + lax.broadcasted_iota(jnp.int32, (1, width), 1)
            query_at = (column // 32) * 256 + me.x * 64 + me.core * 32 + column % 32
            return jnp.where(key_at <= query_at, s, fill)

        def top(lanes):
            def body(b, m):
                s = masked(b, lanes)
                scores[b, :, lanes:] = s
                return jnp.maximum(m, jnp.max(s, axis=0, keepdims=True))
            return body

        m = lax.fori_loop(0, 4, top(0), jnp.full((1, 256), fill, F32))
        m_high = lax.fori_loop(4, 8, top(128), m[:, 128:])
        m = jnp.concatenate([m[:, :128], m_high], axis=1)

        def sums(lanes, m):
            def body(b, carry):
                norm, slope = carry
                e = jnp.exp(scores[b, :, lanes:] - m)
                scores[b, :, lanes:] = e
                dp = lax.dot_general(kv[1, b, :, h * 128:(h + 1) * 128], cotangent[lanes:], transposed, preferred_element_type=F32)
                slopes[b, :, lanes:] = dp
                return (norm + jnp.sum(e, axis=0, keepdims=True), slope + jnp.sum(e * dp, axis=0, keepdims=True))
            return body

        zero = jnp.zeros((1, 256), F32)
        norm, slope = lax.fori_loop(0, 4, sums(0, m), (zero, zero))
        norm_high, slope_high = lax.fori_loop(4, 8, sums(128, m_high), (norm[:, 128:], slope[:, 128:]))
        norm = jnp.concatenate([norm[:, :128], norm_high], axis=1)
        slope = jnp.concatenate([slope[:, :128], slope_high], axis=1)
        inverse = 1.0 / norm
        slope = slope * inverse

        def backward(lanes):
            def body(b, carry):
                att, dq = carry
                p = scores[b, :, lanes:] * inverse[:, lanes:]
                w = p.astype(BF16)
                ds = (p * (slopes[b, :, lanes:] - slope[:, lanes:]) * scale).astype(BF16)
                grads[h, 0, b] = jnp.dot(ds, query[lanes:], preferred_element_type=F32).astype(BF16)
                grads[h, 1, b] = jnp.dot(w, cotangent[lanes:], preferred_element_type=F32).astype(BF16)
                att = att + lax.dot_general(kv[1, b, :, h * 128:(h + 1) * 128], w, first, preferred_element_type=F32)
                dq = dq + lax.dot_general(kv[0, b, :, h * 128:(h + 1) * 128], ds, first, preferred_element_type=F32)
                return att, dq
            return body

        square = jnp.zeros((128, 256), F32)
        att, dq = lax.fori_loop(0, 4, backward(0), (square, square))
        att_high, dq_high = lax.fori_loop(4, 8, backward(128), (att[:, 128:], dq[:, 128:]))
        for t, lo, hi in ((0, att, att_high), (1, dq, dq_high)):
            rows = jnp.concatenate([lo[:, :128], hi], axis=1).T.astype(BF16)
            result[t, h, :, my_rows] = rows.reshape(8, 32, 128)

    def to_twin(h):
        return remote(grads.at[h, 1 - me.core], twin_grads.at[h], tw_send.at[h], tw_recv.at[h], twin)

    def gs1(h, d):
        return remote(grads.at[h, me.core, (low, high)[d], own(2)], grads_relay.at[h, d],
                      g1_send.at[h, d], g1_recv.at[h, d], (right, left)[d])

    def gs2(h, d):
        return remote(grads.at[h, me.core, every, own((1, -1)[d])], grads_near.at[h, d],
                      g2_send.at[h, d], g2_recv.at[h, d], (right, left)[d])

    def add_twin(h):
        to_twin(h).wait_recv()

        @pl.loop(0, 8)
        def _(b):
            add(grads.at[h, me.core, b], twin_grads[h, b])

        for d in (0, 1):
            gs1(h, d).start()

    def add_grads_relay(h):
        for d in (0, 1):
            gs1(h, d).wait_recv()
            add(grads.at[h, me.core, (low, high)[d], own((1, -1)[d])], grads_relay[h, d])
            gs2(h, d).start()

    def add_grads_near(h):
        for d in (0, 1):
            gs2(h, d).wait_recv()
        result[2 + me.core, h] = (
            grads[h, me.core, :, own()].astype(F32) + grads_near[h, 0].astype(F32) + grads_near[h, 1].astype(F32)
        ).astype(BF16)

        @pl.when(is_away)
        def _():
            lift(h, 2).start()

    def lift(h, t):
        if t < 2:
            ref = result.at[t, h, every, my_rows]
        else:
            ref = result.at[2 + me.core, h]
        return remote(ref, ref, up_send.at[h, t], up_recv.at[h, t], twin)

    def lifted(h, t):
        ref = result.at[t, h, every, their_rows] if t < 2 else result.at[3 - me.core, h]
        remote(ref, ref, up_send.at[h, t], up_recv.at[h, t], twin).wait_recv()

    def after(h):
        to_twin(h).start()

        @pl.when(is_away)
        def _():
            lift(h, 0).start()
            lift(h, 1).start()

    def spread(h, t, k):
        x, blocks, device = {
            0: (0, every, across),
            1: (0, every, right),
            2: (0, every, left),
            3: (-1, low, right),
            4: (1, high, left),
            5: (-1, every, across),
            6: (1, every, across),
            7: (2, every, across),
        }[k]
        ref = wide.at[t, h, blocks, own(x)]
        src = result.at[t, h] if k == 0 else ref
        return remote(src, ref, wide_send.at[h, t, k], wide_recv.at[h, t, k], device)

    def here(h, t):
        return pltpu.make_async_copy(result.at[t, h], wide.at[t, h, every, own()], here_sem.at[h, t])

    def spread_home(h, types):
        @pl.when(is_home)
        def _():
            for t in types:
                if t < 3:
                    lifted(h, t)
                spread(h, t, 0).start()
                here(h, t).start()
            for t in types:
                here(h, t).wait()
                spread(h, t, 1).start()
                spread(h, t, 2).start()

    def spread_away(h, types):
        @pl.when(is_away)
        def _():
            for t in types:
                spread(h, t, 0).wait_recv()
                if t not in along_x_first:
                    spread(h, t, 1).start()
                    spread(h, t, 2).start()

    def spread_relay(h, types):
        def around(t):
            for d in (0, 1):
                spread(h, t, 1 + d).wait_recv()
                spread(h, t, 3 + d).start()
                if t in along_x_first:
                    spread(h, t, 5 + d).start()

        for t in types:
            if t not in along_x_first:
                around(t)

        def home_rows():
            for t in types:
                if t in along_x_first:
                    around(t)

        def away_rows():
            for t in types:
                if t in along_x_first:
                    spread(h, t, 5).wait_recv()
                    spread(h, t, 6).wait_recv()

        pl.when(is_home)(home_rows)
        pl.when(is_away)(away_rows)

    def keep_grads(h, t):
        lanes = pl.ds(h * 384 + (t - 1) * 128, 128)
        return pltpu.make_async_copy(wide.at[t, h], grads_out.at[:, :, lanes], out_sem.at[h, t - 1])

    def spread_done(h, types):
        def arrived(t):
            spread(h, t, 3).wait_recv()
            spread(h, t, 4).wait_recv()

        def home_rows():
            for t in types:
                if t in along_x_first:
                    arrived(t)
                    spread(h, t, 7).start()

        def away_rows():
            for t in types:
                if t in along_x_first:
                    spread(h, t, 7).wait_recv()

        for t in types:
            if t not in along_x_first:
                arrived(t)
        pl.when(is_home)(home_rows)
        pl.when(is_away)(away_rows)
        for t in types:
            if t > 0:
                keep_grads(h, t).start()

    def block_lanes(core, n=None):
        if n is None:
            return pl.ds(pl.multiple_of(core * 768, 768), 768)
        return pl.ds(pl.multiple_of(core * 768 + n * 384, 384), 384)

    def b0(i, n):
        return remote(held.at[0, pl.ds(i * 8, 8), :, block_lanes(1 - me.core, n)], near.at[:, n, i],
                      b0_send.at[i, n], b0_recv.at[i, n], twin)

    def z_at(z):
        return lax.rem(me.z + z + 4, 4)

    def term_at(i, y, z):
        return held.at[0, i * 8 + y * 4 + z, :, block_lanes(me.core)]

    def b1(i, d):
        return remote(term_at(i, d, z_at(2)), block_relay.at[i, d], b1_send.at[i, d], b1_recv.at[i, d], (up, down)[d])

    def b2(i, d, y):
        return remote(term_at(i, y, z_at((1, -1)[d])), block_near.at[i, d, y], b2_send.at[i, d, y], b2_recv.at[i, d, y], (up, down)[d])

    def b3(i):
        return remote(term_at(i, 1 - me.ylo, me.z), block_far.at[i], b3_send.at[i], b3_recv.at[i], beside)

    def multiply_out(i):
        mine = jnp.concatenate([wide[0, h, :, own(slice_at[i])].reshape(512, 128) for h in range(3)], axis=1)
        turned[...] = mine.T

        @pl.loop(0, 4)
        def _(n):
            lanes = pl.ds(pl.multiple_of(n * 384, 384), 384)
            held[0, pl.ds(i * 8, 8), :, lanes] = jnp.dot(
                mine, wo_ref[:, :, lanes].reshape(384, 384), preferred_element_type=F32
            ).astype(BF16).reshape(8, 64, 384)

        b0(i, 0).start()
        b0(i, 1).start()

        @pl.loop(0, 4)
        def _(n):
            lanes = pl.ds(pl.multiple_of(n * 384, 384), 384)
            tokens = [held[1, b * 4 + me.col_x(slice_at[i]), :, lanes] for b in range(8)]
            term = jnp.dot(
                turned[...], jnp.concatenate(tokens, axis=0), preferred_element_type=F32
            ).reshape(3, 128, 384)
            if i == 0:
                grad_out[:, :, lanes] = term
            else:
                grad_out[:, :, lanes] += term

    def add_block_twin(i):
        for n in (0, 1):
            b0(i, n).wait_recv()

            @pl.loop(0, 8)
            def _(b):
                add(held.at[0, i * 8 + b, :, block_lanes(me.core, n)], near[b, n, i])

        for d in (0, 1):
            b1(i, d).start()

    def add_block_relay(i):
        for d in (0, 1):
            b2(i, d, 1 - d).start()
        for d in (0, 1):
            b1(i, d).wait_recv()
            add(term_at(i, d, z_at((1, -1)[d])), block_relay[i, d])
            b2(i, d, d).start()

    def add_block_near(i):
        for d in (0, 1):
            for y in (0, 1):
                b2(i, d, y).wait_recv()
        for y in (0, 1):
            add(term_at(i, y, me.z), block_near[i, 0, y], block_near[i, 1, y])
        b3(i).start()

    def add_block_far(i):
        b3(i).wait_recv()
        final[own(slice_at[i])] = (term_at(i, me.ylo, me.z)[...].astype(F32) + block_far[i].astype(F32)).astype(BF16)

    own_copy[0].wait()
    go(0, 9, 0, 1, 2)
    w_copy.wait()
    work(0, 0, 1)
    own_copy[1].wait()
    go(1, 9)
    wo_copy.wait()
    work(1, 0, 1)
    add_relay(0, 0, 1)
    landed(0, 0)
    go(0, 3, 4, 10)
    add_relay(1, 0, 1)
    landed(0, 2)
    go(0, 6, 12)
    work(0, 1, 2)
    landed(0, 1)
    go(0, 5, 11)
    add_near(0, 0, 1)
    work(0, 2, 4)
    add_relay(0, 1, 2)
    add_relay(0, 3, 4)
    go(1, 1, 2)
    landed(0, 3)
    go(0, 7, 13)
    add_relay(0, 2, 3)
    landed(0, 5, 6)
    go(0, 15)
    landed(0, 4)
    go(0, 8, 14)
    go(1, 0)
    work(0, 4, 6)
    add_near(0, 3, 4)
    add_far(0, 0, 1)
    work(0, 6, 7)
    add_near(0, 1, 2)
    add_relay(0, 4, 5)
    kv_relay(0, 1)
    landed(0, 7, 8)
    go(0, 16)
    add_near(0, 2, 3)
    landed(1, 0)
    go(1, 3, 4, 10)
    landed(1, 2)
    go(1, 6, 12)
    landed(1, 1)
    go(1, 5, 11)
    add_far(0, 3, 4)
    add_far(0, 1, 2)
    add_near(1, 0, 1)
    add_relay(0, 5, 6)
    add_near(0, 4, 5)
    work(1, 1, 2)
    work(0, 7, 8)
    add_relay(0, 6, 7)
    work(1, 3, 4)
    landed(1, 4)
    go(1, 8, 14)
    landed(1, 3)
    go(1, 7, 13)
    add_relay(0, 7, 8)
    add_far(0, 2, 3)
    add_far(0, 4, 5)
    add_near(0, 5, 6)
    kv_relay(2, 3)
    landed(1, 5, 6)
    go(1, 15)
    add_relay(1, 1, 2)
    kv_relay(3, 4)
    kv_relay(1, 2)
    work(1, 2, 3)
    work(1, 5, 6)
    add_near(0, 7, 8)
    add_far(0, 5, 6)
    add_relay(1, 2, 3)
    kv_done(1, 2)
    add_near(0, 6, 7)
    work(1, 4, 5)
    kv_relay(4, 5)
    landed(1, 7, 8)
    go(1, 16)
    add_near(1, 1, 2)
    kv_relay(5, 6)
    kv_done(2, 3)
    add_relay(1, 3, 4)
    add_relay(1, 5, 6)
    kv_done(4, 5)
    kv_done(3, 4)
    work(1, 6, 7)
    kv_done(5, 6)
    add_far(0, 7, 8)
    add_far(1, 0, 1)
    kv_whole(4, 5)
    add_relay(1, 4, 5)
    add_near(1, 3, 4)
    work(1, 7, 8)
    kv_done(0, 1)
    add_near(1, 5, 6)
    add_relay(1, 6, 7)
    add_near(1, 2, 3)
    add_far(0, 6, 7)
    turn(0, 1)
    add_far(1, 1, 2)
    turn(1, 2)
    add_relay(1, 7, 8)
    kv_whole(0, 1)
    add_near(1, 4, 5)
    add_near(1, 6, 7)
    kv_relay(6, 8)
    kv_whole(2, 3)
    add_near(1, 7, 8)
    add_far(1, 3, 4)
    kv_done(6, 7)
    add_far(1, 2, 3)
    kv_whole(1, 2)
    add_far(1, 5, 6)
    kv_done(7, 8)
    add_far(1, 6, 7)
    add_far(1, 4, 5)
    add_far(1, 7, 8)
    kv_whole(3, 4)
    kv_whole(6, 8)
    kv_whole(5, 6)
    attend(0)
    after(0)
    spread_home(0, (0,))
    spread_home(0, (1,))
    add_twin(0)
    attend(1)
    add_grads_relay(0)
    after(1)
    spread_home(1, (0,))
    spread_home(1, (1,))
    spread_away(0, (1,))
    attend(2)
    after(2)
    spread_home(2, (0,))
    add_twin(1)
    spread_away(0, (0,))
    spread_away(1, (1,))
    spread_away(1, (0,))
    add_grads_near(0)
    spread_relay(1, (0,))
    turn(2, 3)
    spread_home(2, (1,))
    turn(3, 4)
    turn(4, 5)
    spread_away(2, (0,))
    spread_relay(0, (1,))
    turn(5, 6)
    turn(6, 7)
    turn(7, 8)
    add_twin(2)
    spread_relay(1, (1,))
    add_grads_relay(1)
    spread_away(2, (1,))
    for k in range(17):
        gather(0, k).wait_send()
    multiply_out(0)
    spread_relay(2, (1,))
    add_grads_near(1)
    spread_home(0, (2,))
    spread_relay(2, (0,))
    spread_relay(0, (0,))
    add_block_twin(0)
    add_grads_relay(2)
    multiply_out(1)
    add_block_relay(0)
    spread_home(1, (2,))
    spread_home(1, (3,))
    multiply_out(2)
    spread_done(1, (0,))
    spread_home(0, (3,))
    add_block_twin(1)
    add_grads_near(2)
    spread_home(2, (2,))
    spread_home(2, (3,))
    spread_done(0, (0,))
    spread_away(0, (2,))
    add_block_twin(2)
    spread_away(1, (2,))
    spread_done(2, (0,))
    spread_away(0, (3,))
    add_block_near(0)
    spread_away(1, (3,))
    spread_done(1, (1,))
    spread_away(2, (2,))
    add_block_relay(1)
    spread_away(2, (3,))
    add_block_relay(2)
    multiply_out(3)
    grad_out_copy = pltpu.make_async_copy(grad_out, grad_out_hbm, last_sem.at[0])
    grad_out_copy.start()
    spread_done(2, (1,))
    spread_relay(0, (3,))
    add_block_twin(3)
    add_block_near(1)
    spread_relay(2, (3,))
    spread_relay(1, (2,))
    add_block_near(2)
    spread_relay(0, (2,))
    add_block_relay(3)
    spread_done(0, (1,))
    spread_relay(1, (3,))
    add_block_near(3)
    spread_done(2, (3,))
    add_block_far(2)
    spread_relay(2, (2,))
    spread_done(1, (2,))
    add_block_far(0)
    spread_done(2, (2,))
    spread_done(0, (2,))
    add_block_far(1)
    add_block_far(3)
    their_half = pl.ds(pl.multiple_of(128 - me.core * 128, 128), 128)
    end = remote(final.at[their_half], theirs, end_send, end_recv, twin)
    end.start()
    end.wait_recv()
    mine = final[pl.ds(pl.multiple_of(me.core * 128, 128), 128)]

    @pl.when(me.core == 0)
    def _():
        block_out[:, :768] = mine
        block_out[:, 768:] = theirs[...]

    @pl.when(me.core == 1)
    def _():
        block_out[:, :768] = theirs[...]
        block_out[:, 768:] = mine

    block_copy = pltpu.make_async_copy(block_out, block_hbm, last_sem.at[1])
    block_copy.start()
    spread_done(0, (3,))
    spread_done(1, (3,))

    def sums_sent(a, s):
        for d in (0, 1):
            rs1(a, s, d).wait_send()
            rs2(a, s, d).wait_send()

    @pl.when(is_away)
    def _():
        for s in range(8):
            for a in (0, 1):
                if a == 0 and s in across_first:
                    cross(s).wait_send()
                else:
                    rs3(a, s).wait_send()
                    sums_sent(a, s)
        for h in range(3):
            for t in range(3):
                lift(h, t).wait_send()

    @pl.when(is_home)
    def _():
        for a in (0, 1):
            @pl.loop(0, 8)
            def _(s):
                rs4(a, s).wait_send()
                sums_sent(a, s)
        for h in range(3):
            for t in range(4):
                spread(h, t, 0).wait_send()
                if t in along_x_first:
                    for k in range(1, 8):
                        spread(h, t, k).wait_send()

    for k in range(17):
        gather(1, k).wait_send()

    @pl.loop(0, 8)
    def _(s):
        for k in range(7):
            kv_gather(s, k).wait_send()

    for h in range(3):
        to_twin(h).wait_send()
        for d in (0, 1):
            gs1(h, d).wait_send()
            gs2(h, d).wait_send()
        for t in range(4):
            if t not in along_x_first:
                for k in range(1, 5):
                    spread(h, t, k).wait_send()
            if t > 0:
                keep_grads(h, t).wait()
    for i in range(4):
        for d in (0, 1):
            b0(i, d).wait_send()
            b1(i, d).wait_send()
            for y in (0, 1):
                b2(i, d, y).wait_send()
        b3(i).wait_send()
    for s in (5, 6, 7):
        keep(s).wait()
    grad_out_copy.wait()
    block_copy.wait()
    end.wait_send()


def block(inputs, grad_block, w_qkv, w_out):
    dma = pltpu.SemaphoreType.DMA
    anywhere = pl.BlockSpec(memory_space=pl.ANY)
    return pl.pallas_call(
        block_kernel,
        name="block",
        out_shape=(
            jax.ShapeDtypeStruct((1536, 2048), BF16),
            jax.ShapeDtypeStruct((8, 256, 1152), BF16),
            jax.ShapeDtypeStruct((128, 1536), BF16),
            jax.ShapeDtypeStruct((3, 128, 1536), F32),
        ),
        in_specs=[anywhere] * 4,
        out_specs=(anywhere,) * 4,
        scratch_shapes=[
            pltpu.VMEM((2, 32, 64, 1536), BF16),
            pltpu.VMEM((8, 4, 256, 384), BF16),
            pltpu.VMEM((8, 2, 4, 32, 384), BF16),
            pltpu.VMEM((8, 2, 4, 64, 384), BF16),
            pltpu.VMEM((8, 4, 64, 384), BF16),
            pltpu.VMEM((max(len(across_first), 1), 3, 256, 384), BF16),
            pltpu.VMEM((8, 4, 64, 384), BF16),
            pltpu.VMEM((3, 1536, 384), BF16),
            pltpu.VMEM((3, 128, 1536), BF16),
            pltpu.VMEM((128, 1536), BF16),
            pltpu.VMEM((3, 128, 1536), F32),
            pltpu.VMEM((2, 8, 256, 384), BF16),
            pltpu.VMEM((8, 256, 256), F32),
            pltpu.VMEM((8, 256, 256), F32),
            pltpu.VMEM((3, 2, 8, 256, 128), BF16),
            pltpu.VMEM((3, 8, 256, 128), BF16),
            pltpu.VMEM((3, 2, 4, 64, 128), BF16),
            pltpu.VMEM((3, 2, 8, 64, 128), BF16),
            pltpu.VMEM((4, 3, 8, 64, 128), BF16),
            pltpu.VMEM((4, 3, 8, 256, 128), BF16),
            pltpu.VMEM((384, 512), BF16),
            pltpu.VMEM((4, 2, 64, 768), BF16),
            pltpu.VMEM((4, 2, 2, 64, 768), BF16),
            pltpu.VMEM((4, 64, 768), BF16),
            pltpu.VMEM((256, 768), BF16),
            pltpu.VMEM((128, 768), BF16),
            dma((2, 17)), dma((2, 17)),
            dma((2, 8, 2)), dma((2, 8, 2)),
            dma((2, 8, 2)), dma((2, 8, 2)),
            dma((2, 8)), dma((2, 8)),
            dma((2, 8)), dma((2, 8)),
            dma((8,)), dma((2,)), dma((2,)), dma((max(len(across_first), 1),)), dma((max(len(across_first), 1),)), dma((2,)),
            dma((8, 7)), dma((8, 7)),
            dma((3,)), dma((3,)),
            dma((3, 2)), dma((3, 2)),
            dma((3, 2)), dma((3, 2)),
            dma((3, 3)), dma((3, 3)),
            dma((3, 4, 8)), dma((3, 4, 8)),
            dma((3, 4)), dma((3, 3)),
            dma((4, 2)), dma((4, 2)),
            dma((4, 2)), dma((4, 2)),
            dma((4, 2, 2)), dma((4, 2, 2)),
            dma((4,)), dma((4,)),
            dma(()), dma(()),
        ],
        compiler_params=pltpu.CompilerParams(
            collective_id=1, has_side_effects=True, vmem_limit_bytes=63 << 20
        ),
    )(inputs.reshape(2, 64, 1536), grad_block.reshape(2, 64, 1536), jnp.transpose(w_qkv, (1, 0, 2)), w_out)


def weight_kernel(x_hbm, rows_hbm, block_hbm, grad_out_hbm, out_hbm, block_copy, grad_out_copy, x, rows, out, block_rows, grad_out, x_sem, sem, out_sem):
    def load(m):
        features = pl.ds(m * 256, 256)
        return pltpu.make_async_copy(x_hbm.at[features], x.at[features], x_sem.at[m])

    def store(m, h):
        return pltpu.make_async_copy(out.at[m % 2, :, h * 384:(h + 1) * 384], out_hbm.at[h, pl.ds(m * 256, 256)], out_sem.at[m, h])

    copies = [
        pltpu.make_async_copy(rows_hbm, rows, sem.at[0]),
        pltpu.make_async_copy(block_hbm, block_rows, sem.at[1]),
        pltpu.make_async_copy(grad_out_hbm, grad_out, sem.at[2]),
    ]
    passed_on = [
        pltpu.make_async_copy(block_rows, block_copy, sem.at[1]),
        pltpu.make_async_copy(grad_out, grad_out_copy, sem.at[2]),
    ]
    copies[0].start()
    for m in range(6):
        load(m).start()
    copies[1].start()
    copies[2].start()
    copies[0].wait()
    for m in range(6):
        load(m).wait()
        if m >= 2:
            for h in range(3):
                store(m - 2, h).wait()
        out[m % 2] = jnp.dot(x[m * 256:(m + 1) * 256], rows[...].reshape(2048, 1152), preferred_element_type=F32)
        for h in range(3):
            store(m, h).start()
        if m == 1:
            for k in (1, 2):
                copies[k].wait()
                passed_on[k - 1].start()
    for m in (4, 5):
        for h in range(3):
            store(m, h).wait()
    for copy in passed_on:
        copy.wait()


def weight_grad(turned, rows, block_rows, grad_out):
    dma = pltpu.SemaphoreType.DMA
    anywhere = pl.BlockSpec(memory_space=pl.ANY)
    return pl.pallas_call(
        weight_kernel,
        name="weight_grad",
        out_shape=(
            jax.ShapeDtypeStruct((3, 1536, 384), F32),
            jax.ShapeDtypeStruct((128, 1536), BF16),
            jax.ShapeDtypeStruct((3, 128, 1536), F32),
        ),
        in_specs=[anywhere] * 4,
        out_specs=(anywhere,) * 3,
        scratch_shapes=[
            pltpu.VMEM((1536, 2048), BF16),
            pltpu.VMEM((8, 256, 1152), BF16),
            pltpu.VMEM((2, 256, 1152), F32),
            pltpu.VMEM((128, 1536), BF16),
            pltpu.VMEM((3, 128, 1536), F32),
            dma((6,)), dma((3,)), dma((6, 3)),
        ],
        compiler_params=pltpu.CompilerParams(vmem_limit_bytes=63 << 20),
    )(turned, rows, block_rows, grad_out)


def local(inputs, w_qkv, w_out, grad_block):
    turned, rows, block_rows, grad_out = block(inputs, grad_block, w_qkv, w_out)
    grad_qkv, block_out, grad_out = weight_grad(turned, rows, block_rows, grad_out)
    return block_out, jnp.transpose(grad_qkv, (1, 0, 2)), grad_out


def solution(mesh):
    placed = (P("row", "col"), P("col", "row", None), P("row", None, "col"), P("row", "col"))
    return jax.shard_map(
        local,
        mesh=mesh,
        in_specs=placed,
        out_specs=(P("row", "col"), P("col", "row", None), P("row", None, "col")),
        check_vma=False,
    )
```

```python
import jax
import jax.numpy as jnp
from jax import lax
from jax.experimental import pallas as pl
from jax.experimental.pallas import tpu as pltpu
from jax.sharding import PartitionSpec as P

MESH = pl.DeviceIdType.MESH
BF16 = jnp.bfloat16
F32 = jnp.float32


class Place:
    def __init__(self):
        r = lax.axis_index("row")
        c = lax.axis_index("col")
        self.ylo, self.z, self.core = r // 8, (r // 2) % 4, r % 2
        self.yhi, self.x = c // 4, c % 4

    def at(self, ylo=0, z=0, core=0, yhi=0, x=0):
        return (
            lax.rem(self.ylo + ylo, 2) * 8 + lax.rem(self.z + z + 4, 4) * 2 + lax.rem(self.core + core, 2),
            lax.rem(self.yhi + yhi, 2) * 4 + lax.rem(self.x + x + 4, 4),
        )

    def slot(self, ylo=0, z=0, core=0):
        return self.at(ylo=ylo, z=z, core=core)[0]

    def col_x(self, x):
        return lax.rem(self.x + x + 4, 4)


def meet(partners):
    barrier = pltpu.get_barrier_semaphore()
    for partner in partners:
        pl.semaphore_signal(barrier, inc=1, device_id=partner, device_id_type=MESH)
    pl.semaphore_wait(barrier, len(partners))


def remote(src, dst, send, recv, device):
    return pltpu.make_async_remote_copy(
        src_ref=src, dst_ref=dst, send_sem=send, recv_sem=recv, device_id=device, device_id_type=MESH
    )


slice_at = (0, -1, 1, 2)
along_x_first = (1,)


def block_kernel(
    x_hbm, g_hbm, w_hbm, wo_hbm,
    turned_out, grads_out, block_hbm, grad_out_hbm,
    held, part, relay, near, far, total, w_ref, wo_ref, block_out, grad_out,
    kv, scores, slopes, grads, twin_grads, grads_relay, grads_near, result,
    wide, turned, block_relay, block_near, block_far, final, theirs,
    ag_send, ag_recv, s1_send, s1_recv, s2_send, s2_recv, s3_send, s3_recv, s4_send, s4_recv, x_sem, w_sem, own_sem, last_sem,
    kv_send, kv_recv, tw_send, tw_recv, g1_send, g1_recv, g2_send, g2_recv, up_send, up_recv,
    wide_send, wide_recv, here_sem, out_sem, b0_send, b0_recv, b1_send, b1_recv, b2_send, b2_recv, b3_send, b3_recv,
    end_send, end_recv,
):
    me = Place()
    up, down, beside = me.at(z=1), me.at(z=-1), me.at(ylo=1)
    right, left, across, twin = me.at(x=1), me.at(x=-1), me.at(yhi=1), me.at(core=1)
    is_home = me.core == me.yhi
    is_away = jnp.logical_not(is_home)
    scale = 128 ** (-0.5)
    fill = -1e30
    low, high, every = pl.ds(0, 4), pl.ds(4, 4), pl.ds(0, 8)
    my_rows = pl.ds(pl.multiple_of(me.core * 32, 32), 32)
    their_rows = pl.ds(pl.multiple_of(32 - me.core * 32, 32), 32)

    def own(x=0):
        return pl.ds(pl.multiple_of(me.col_x(x) * 64, 64), 64)

    own_copy = [
        pltpu.make_async_copy(ref, held.at[a, pl.ds(me.slot() * 2, 2)], own_sem.at[a])
        for a, ref in enumerate((x_hbm, g_hbm))
    ]
    w_copy = pltpu.make_async_copy(w_hbm, w_ref, w_sem.at[0])
    wo_copy = pltpu.make_async_copy(wo_hbm, wo_ref, w_sem.at[1])
    own_copy[0].start()
    w_copy.start()
    own_copy[1].start()
    wo_copy.start()
    meet([beside, up, down, twin, right, left, across])

    def gather(a, k):
        slot, device = {
            0: (me.slot(), beside),
            1: (me.slot(), up),
            2: (me.slot(), down),
            3: (me.slot(ylo=1), up),
            4: (me.slot(ylo=1), down),
            5: (me.slot(z=-1), up),
            6: (me.slot(z=1), down),
            7: (me.slot(ylo=1, z=-1), up),
            8: (me.slot(ylo=1, z=1), down),
            9: (me.slot(), twin),
            10: (me.slot(ylo=1), twin),
            11: (me.slot(z=-1), twin),
            12: (me.slot(z=1), twin),
            13: (me.slot(ylo=1, z=-1), twin),
            14: (me.slot(ylo=1, z=1), twin),
            15: (me.slot(z=2), twin),
            16: (me.slot(ylo=1, z=2), twin),
        }[k]
        if k in (5, 7):
            rows = pl.ds(slot * 2, 1)
        elif k in (6, 8):
            rows = pl.ds(slot * 2 + 1, 1)
        else:
            rows = pl.ds(slot * 2, 2)
        ref = held.at[a, rows]
        return remote(ref, ref, ag_send.at[a, k], ag_recv.at[a, k], device)

    def go(a, *kinds):
        for k in kinds:
            gather(a, k).start()

    def landed(a, *kinds):
        for k in kinds:
            gather(a, k).wait_recv()

    def block_of(s):
        ylo = jnp.where((s == 1) | (s == 4) | (s == 5) | (s == 7), 1, 0)
        z = jnp.where((s == 2) | (s == 4), 3, jnp.where((s == 3) | (s == 5), 1, jnp.where(s >= 6, 2, 0)))
        return lax.rem(me.ylo + ylo, 2) * 4 + lax.rem(me.z + z, 4)

    def unit(a):
        return pl.ds(0, 3) if a == 0 else pl.ds(3, 1)

    def keep(s):
        columns = pl.ds(pl.multiple_of(block_of(s) * 256, 256), 256)
        return pltpu.make_async_copy(w_ref.at[s % 3, :, 0:256], turned_out.at[:, columns], x_sem.at[s])

    def turn(*steps):
        for s in range(*steps):
            if s >= 3:
                keep(s - 3).wait()

            @pl.loop(0, 12)
            def _(n):
                lanes = pl.ds(pl.multiple_of(n * 128, 128), 128)
                rows = held[0, pl.ds(block_of(s) * 4, 4), :, lanes].reshape(256, 128)
                w_ref[s % 3, lanes, 0:256] = rows.T

            keep(s).start()

    def rs1(a, s, d):
        rows = pl.ds(pl.multiple_of(me.col_x(2) * 64 + 32 * d, 32), 32)
        return remote(part.at[s, unit(a), rows], relay.at[s, d, unit(a)], s1_send.at[a, s, d], s1_recv.at[a, s, d], (right, left)[d])

    def rs2(a, s, d):
        return remote(part.at[s, unit(a), own((1, -1)[d])], near.at[s, d, unit(a)],
                      s2_send.at[a, s, d], s2_recv.at[a, s, d], (right, left)[d])

    def rs3(a, s):
        return remote(part.at[s, unit(a), own()], far.at[s, unit(a)], s3_send.at[a, s], s3_recv.at[a, s], across)

    def rs4(a, s):
        ref = total.at[block_of(s), unit(a)]
        return remote(ref, ref, s4_send.at[a, s], s4_recv.at[a, s], twin)

    def each(steps, body):
        lo, hi = steps
        if hi - lo == 1:
            body(lo)
        else:
            pl.loop(lo, hi)(body)

    def work(a, *steps):
        def body(s):
            remote(held.at[a, pl.ds(0, 2)], held.at[a, pl.ds(0, 2)], ag_send.at[a, 9 + s], ag_recv.at[a, 9 + s], twin).wait_recv()
            rows = held.at[a, pl.ds(block_of(s) * 4, 4)]
            if a == 0:
                @pl.loop(0, 3)
                def _(h):
                    part[s, h] = jnp.dot(
                        rows[...].reshape(256, 1536), w_ref[h], preferred_element_type=F32
                    ).astype(BF16)
            else:
                part[s, 3] = lax.dot_general(
                    rows[...].reshape(256, 1536), wo_ref[...].reshape(384, 1536),
                    (((1,), (1,)), ((), ())), preferred_element_type=F32,
                ).astype(BF16)
            for d in (0, 1):
                rs1(a, s, d).start()
        each(steps, body)

    def add(ref, *terms):
        value = ref[...].astype(F32)
        for term in terms:
            value = value + term.astype(F32)
        ref[...] = value.astype(BF16)

    def add_relay(a, *steps):
        def body(s):
            for d in (0, 1):
                rs1(a, s, d).wait_recv()
                rows = pl.ds(pl.multiple_of(me.col_x((1, -1)[d]) * 64 + 32 * d, 32), 32)
                add(part.at[s, unit(a), rows], relay[s, d, unit(a)])
                rs2(a, s, d).start()
        each(steps, body)

    def add_near(a, *steps):
        def body(s):
            for d in (0, 1):
                rs2(a, s, d).wait_recv()
            add(part.at[s, unit(a), own()], near[s, 0, unit(a)], near[s, 1, unit(a)])
            pl.when(is_away)(lambda: rs3(a, s).start())
        each(steps, body)

    def kv_gather(s, k):
        x, rows, device = {
            0: (0, 0, right),
            1: (0, 0, left),
            2: (-1, 1, right),
            3: (1, 2, left),
            4: (-1, 0, twin),
            5: (1, 0, twin),
            6: (2, 0, twin),
        }[k]
        start = me.col_x(x) * 64
        if rows == 0:
            span = pl.ds(pl.multiple_of(start, 64), 64)
        else:
            span = pl.ds(pl.multiple_of(start + 32 * (rows - 1), 32), 32)
        ref = kv.at[me.core, block_of(s), span]
        return remote(ref, ref, kv_send.at[s, k], kv_recv.at[s, k], device)

    def add_far(a, *steps):
        def body(s):
            block = block_of(s)

            @pl.when(is_home)
            def _():
                rs3(a, s).wait_recv()
                total[block, unit(a)] = (
                    part[s, unit(a), own()].astype(F32) + far[s, unit(a)].astype(F32)
                ).astype(BF16)
                rs4(a, s).start()

            @pl.when(is_away)
            def _():
                rs4(a, s).wait_recv()

            if a == 0:
                for j in (0, 1):
                    for h in range(3):
                        kv[j, block, own(), h * 128:(h + 1) * 128] = total[block, h, :, 128 + 128 * j:256 + 128 * j]
                kv_gather(s, 0).start()
                kv_gather(s, 1).start()
        each(steps, body)

    def kv_relay(*steps):
        def body(s):
            for d in (0, 1):
                kv_gather(s, d).wait_recv()
                kv_gather(s, 2 + d).start()
                kv_gather(s, 4 + d).start()
        each(steps, body)

    def kv_done(*steps):
        def body(s):
            kv_gather(s, 2).wait_recv()
            kv_gather(s, 3).wait_recv()
            kv_gather(s, 6).start()
        each(steps, body)

    def kv_whole(*steps):
        def body(s):
            for k in (4, 5, 6):
                kv_gather(s, k).wait_recv()
        each(steps, body)

    def part_free():
        for s in range(8):
            for d in (0, 1):
                rs1(0, s, d).wait_send()
                rs2(0, s, d).wait_send()

            @pl.when(is_away)
            def _():
                rs3(0, s).wait_send()

    transposed = (((1,), (1,)), ((), ()))
    by_rows = (((0,), (0,)), ((), ()))

    def query_of(h):
        return total[:, h, my_rows, 0:128].reshape(256, 128)

    def write_rows(t, h, low_half, high_half):
        rows = jnp.concatenate([low_half[:, :128], high_half], axis=1).T.astype(BF16)
        result[t, h, :, my_rows] = rows.reshape(8, 32, 128)

    def attend_forward(h):
        query = query_of(h)
        head = slice(h * 128, (h + 1) * 128)

        def masked(b, lanes):
            width = 256 - lanes
            s = lax.dot_general(kv[0, b, :, head], query[lanes:], transposed, preferred_element_type=F32) * scale
            key_at = b * 256 + lax.broadcasted_iota(jnp.int32, (256, width), 0)
            column = lanes + lax.broadcasted_iota(jnp.int32, (1, width), 1)
            query_at = (column // 32) * 256 + me.x * 64 + me.core * 32 + column % 32
            return jnp.where(key_at <= query_at, s, fill)

        def top(lanes):
            def body(b, m):
                s = masked(b, lanes)
                scores[b, :, lanes:] = s
                return jnp.maximum(m, jnp.max(s, axis=0, keepdims=True))
            return body

        m = lax.fori_loop(0, 4, top(0), jnp.full((1, 256), fill, F32), unroll=True)
        m_high = lax.fori_loop(4, 8, top(128), m[:, 128:], unroll=True)
        m = jnp.concatenate([m[:, :128], m_high], axis=1)

        def sums(lanes, m):
            def body(b, norm):
                e = jnp.exp(scores[b, :, lanes:] - m)
                scores[b, :, lanes:] = e
                return norm + jnp.sum(e, axis=0, keepdims=True)
            return body

        norm = lax.fori_loop(0, 4, sums(0, m), jnp.zeros((1, 256), F32), unroll=True)
        norm_high = lax.fori_loop(4, 8, sums(128, m_high), norm[:, 128:], unroll=True)
        inverse = 1.0 / jnp.concatenate([norm[:, :128], norm_high], axis=1)

        def rows(lanes):
            def body(b, att):
                w = (scores[b, :, lanes:] * inverse[:, lanes:]).astype(BF16)
                part[b, h, :, lanes:256] = w
                return att + lax.dot_general(kv[1, b, :, head], w, by_rows, preferred_element_type=F32)
            return body

        att = lax.fori_loop(0, 4, rows(0), jnp.zeros((128, 256), F32), unroll=True)
        att_high = lax.fori_loop(4, 8, rows(128), att[:, 128:], unroll=True)
        write_rows(0, h, att, att_high)
        pl.when(is_away)(lambda: lift(h, 0).start())

    def attend_backward(h):
        query = query_of(h)
        head = slice(h * 128, (h + 1) * 128)
        cotangent = total[:, 3, my_rows, head].reshape(256, 128)

        def sums(lanes):
            def body(b, slope):
                dp = lax.dot_general(kv[1, b, :, head], cotangent[lanes:], transposed, preferred_element_type=F32)
                slopes[b, :, lanes:] = dp
                return slope + jnp.sum(part[b, h, :, lanes:256].astype(F32) * dp, axis=0, keepdims=True)
            return body

        slope = lax.fori_loop(0, 4, sums(0), jnp.zeros((1, 256), F32), unroll=True)
        slope_high = lax.fori_loop(4, 8, sums(128), slope[:, 128:], unroll=True)
        slope = jnp.concatenate([slope[:, :128], slope_high], axis=1)

        def terms(lanes):
            def body(b, dq):
                w = part[b, h, :, lanes:256]
                ds = (w.astype(F32) * (slopes[b, :, lanes:] - slope[:, lanes:]) * scale).astype(BF16)
                grads[h, 0, b] = jnp.dot(ds, query[lanes:], preferred_element_type=F32).astype(BF16)
                grads[h, 1, b] = jnp.dot(w, cotangent[lanes:], preferred_element_type=F32).astype(BF16)
                return dq + lax.dot_general(kv[0, b, :, head], ds, by_rows, preferred_element_type=F32)
            return body

        dq = lax.fori_loop(0, 4, terms(0), jnp.zeros((128, 256), F32), unroll=True)
        dq_high = lax.fori_loop(4, 8, terms(128), dq[:, 128:], unroll=True)
        write_rows(1, h, dq, dq_high)
        to_twin(h).start()
        pl.when(is_away)(lambda: lift(h, 1).start())

    def to_twin(h):
        return remote(grads.at[h, 1 - me.core], twin_grads.at[h], tw_send.at[h], tw_recv.at[h], twin)

    def gs1(h, d):
        return remote(grads.at[h, me.core, (low, high)[d], own(2)], grads_relay.at[h, d],
                      g1_send.at[h, d], g1_recv.at[h, d], (right, left)[d])

    def gs2(h, d):
        return remote(grads.at[h, me.core, every, own((1, -1)[d])], grads_near.at[h, d],
                      g2_send.at[h, d], g2_recv.at[h, d], (right, left)[d])

    def add_twin(h):
        to_twin(h).wait_recv()

        @pl.loop(0, 8)
        def _(b):
            add(grads.at[h, me.core, b], twin_grads[h, b])

        for d in (0, 1):
            gs1(h, d).start()

    def add_grads_relay(h):
        for d in (0, 1):
            gs1(h, d).wait_recv()
            add(grads.at[h, me.core, (low, high)[d], own((1, -1)[d])], grads_relay[h, d])
            gs2(h, d).start()

    def add_grads_near(h):
        for d in (0, 1):
            gs2(h, d).wait_recv()
        result[2 + me.core, h] = (
            grads[h, me.core, :, own()].astype(F32) + grads_near[h, 0].astype(F32) + grads_near[h, 1].astype(F32)
        ).astype(BF16)

        @pl.when(is_away)
        def _():
            lift(h, 2).start()

    def lift(h, t):
        if t < 2:
            ref = result.at[t, h, every, my_rows]
        else:
            ref = result.at[2 + me.core, h]
        return remote(ref, ref, up_send.at[h, t], up_recv.at[h, t], twin)

    def lifted(h, t):
        ref = result.at[t, h, every, their_rows] if t < 2 else result.at[3 - me.core, h]
        remote(ref, ref, up_send.at[h, t], up_recv.at[h, t], twin).wait_recv()

    def spread(h, t, k):
        x, blocks, device = {
            0: (0, every, across),
            1: (0, every, right),
            2: (0, every, left),
            3: (-1, low, right),
            4: (1, high, left),
            5: (-1, every, across),
            6: (1, every, across),
            7: (2, every, across),
        }[k]
        ref = wide.at[t, h, blocks, own(x)]
        src = result.at[t, h] if k == 0 else ref
        return remote(src, ref, wide_send.at[h, t, k], wide_recv.at[h, t, k], device)

    def here(h, t):
        return pltpu.make_async_copy(result.at[t, h], wide.at[t, h, every, own()], here_sem.at[h, t])

    def spread_home(h, types):
        @pl.when(is_home)
        def _():
            for t in types:
                if t < 3:
                    lifted(h, t)
                spread(h, t, 0).start()
                here(h, t).start()
            for t in types:
                here(h, t).wait()
                spread(h, t, 1).start()
                spread(h, t, 2).start()

    def spread_away(h, types):
        @pl.when(is_away)
        def _():
            for t in types:
                spread(h, t, 0).wait_recv()
                if t not in along_x_first:
                    spread(h, t, 1).start()
                    spread(h, t, 2).start()

    def spread_relay(h, types):
        def around(t):
            for d in (0, 1):
                spread(h, t, 1 + d).wait_recv()
                spread(h, t, 3 + d).start()
                if t in along_x_first:
                    spread(h, t, 5 + d).start()

        for t in types:
            if t not in along_x_first:
                around(t)

        def home_rows():
            for t in types:
                if t in along_x_first:
                    around(t)

        def away_rows():
            for t in types:
                if t in along_x_first:
                    spread(h, t, 5).wait_recv()
                    spread(h, t, 6).wait_recv()

        pl.when(is_home)(home_rows)
        pl.when(is_away)(away_rows)

    def keep_grads(h, t):
        lanes = pl.ds(h * 384 + (t - 1) * 128, 128)
        return pltpu.make_async_copy(wide.at[t, h], grads_out.at[:, :, lanes], out_sem.at[h, t - 1])

    def spread_done(h, types):
        def arrived(t):
            spread(h, t, 3).wait_recv()
            spread(h, t, 4).wait_recv()

        def home_rows():
            for t in types:
                if t in along_x_first:
                    arrived(t)
                    spread(h, t, 7).start()

        def away_rows():
            for t in types:
                if t in along_x_first:
                    spread(h, t, 7).wait_recv()

        for t in types:
            if t not in along_x_first:
                arrived(t)
        pl.when(is_home)(home_rows)
        pl.when(is_away)(away_rows)
        for t in types:
            if t > 0:
                keep_grads(h, t).start()

    def block_lanes(core, n=None):
        if n is None:
            return pl.ds(pl.multiple_of(core * 768, 768), 768)
        return pl.ds(pl.multiple_of(core * 768 + n * 384, 384), 384)

    def b0(i, n):
        return remote(held.at[0, pl.ds(i * 8, 8), :, block_lanes(1 - me.core, n)], near.at[:, n, i],
                      b0_send.at[i, n], b0_recv.at[i, n], twin)

    def z_at(z):
        return lax.rem(me.z + z + 4, 4)

    def term_at(i, y, z):
        return held.at[0, i * 8 + y * 4 + z, :, block_lanes(me.core)]

    def b1(i, d):
        return remote(term_at(i, d, z_at(2)), block_relay.at[i, d], b1_send.at[i, d], b1_recv.at[i, d], (up, down)[d])

    def b2(i, d, y):
        return remote(term_at(i, y, z_at((1, -1)[d])), block_near.at[i, d, y], b2_send.at[i, d, y], b2_recv.at[i, d, y], (up, down)[d])

    def b3(i):
        return remote(term_at(i, 1 - me.ylo, me.z), block_far.at[i], b3_send.at[i], b3_recv.at[i], beside)

    def multiply_out(i):
        mine = jnp.concatenate([wide[0, h, :, own(slice_at[i])].reshape(512, 128) for h in range(3)], axis=1)
        turned[...] = mine.T

        @pl.loop(0, 4)
        def _(n):
            lanes = pl.ds(pl.multiple_of(n * 384, 384), 384)
            held[0, pl.ds(i * 8, 8), :, lanes] = jnp.dot(
                mine, wo_ref[:, :, lanes].reshape(384, 384), preferred_element_type=F32
            ).astype(BF16).reshape(8, 64, 384)

        b0(i, 0).start()
        b0(i, 1).start()

        @pl.loop(0, 4)
        def _(n):
            lanes = pl.ds(pl.multiple_of(n * 384, 384), 384)
            tokens = [held[1, b * 4 + me.col_x(slice_at[i]), :, lanes] for b in range(8)]
            term = jnp.dot(
                turned[...], jnp.concatenate(tokens, axis=0), preferred_element_type=F32
            ).reshape(3, 128, 384)
            if i == 0:
                grad_out[:, :, lanes] = term
            else:
                grad_out[:, :, lanes] += term

    def add_block_twin(i):
        for n in (0, 1):
            b0(i, n).wait_recv()

            @pl.loop(0, 8)
            def _(b):
                add(held.at[0, i * 8 + b, :, block_lanes(me.core, n)], near[b, n, i])

        for d in (0, 1):
            b1(i, d).start()

    def add_block_relay(i):
        for d in (0, 1):
            b2(i, d, 1 - d).start()
        for d in (0, 1):
            b1(i, d).wait_recv()
            add(term_at(i, d, z_at((1, -1)[d])), block_relay[i, d])
            b2(i, d, d).start()

    def add_block_near(i):
        for d in (0, 1):
            for y in (0, 1):
                b2(i, d, y).wait_recv()
        for y in (0, 1):
            add(term_at(i, y, me.z), block_near[i, 0, y], block_near[i, 1, y])
        b3(i).start()

    def add_block_far(i):
        b3(i).wait_recv()
        final[own(slice_at[i])] = (term_at(i, me.ylo, me.z)[...].astype(F32) + block_far[i].astype(F32)).astype(BF16)

    own_copy[0].wait()
    go(0, 9, 0, 1, 2)
    own_copy[1].wait()
    go(1, 9)
    wo_copy.wait()
    work(1, 0, 1)
    w_copy.wait()
    work(0, 0, 1)
    add_relay(0, 0, 1)
    landed(0, 0)
    go(0, 3, 4, 10)
    landed(0, 2)
    go(0, 6, 12)
    landed(0, 1)
    go(0, 5, 11)
    add_relay(1, 0, 1)
    work(0, 1, 4)
    add_relay(0, 2, 3)
    add_near(0, 0, 1)
    landed(0, 4)
    go(0, 8, 14)
    add_relay(0, 1, 2)
    go(1, 0)
    add_relay(0, 3, 4)
    landed(0, 3)
    go(0, 7, 13)
    work(0, 4, 5)
    go(1, 1, 2)
    add_near(1, 0, 1)
    work(0, 5, 6)
    add_far(0, 0, 1)
    landed(0, 5, 6)
    go(0, 15)
    landed(0, 7, 8)
    go(0, 16)
    work(0, 6, 7)
    add_near(0, 3, 4)
    landed(1, 0)
    go(1, 3, 4, 10)
    work(0, 7, 8)
    add_relay(0, 4, 5)
    work(1, 1, 2)
    add_far(0, 3, 4)
    add_near(0, 1, 2)
    add_relay(0, 5, 6)
    add_near(0, 4, 5)
    add_relay(0, 6, 7)
    kv_relay(3, 4)
    add_far(1, 0, 1)
    kv_relay(0, 1)
    turn(0, 1)
    landed(1, 1)
    go(1, 5, 11)
    add_far(0, 1, 2)
    landed(1, 2)
    go(1, 6, 12)
    add_near(0, 5, 6)
    add_near(0, 2, 3)
    landed(1, 3)
    go(1, 7, 13)
    add_far(0, 4, 5)
    work(1, 2, 3)
    landed(1, 4)
    go(1, 8, 14)
    add_relay(0, 7, 8)
    work(1, 3, 4)
    work(1, 5, 6)
    landed(1, 5, 6)
    go(1, 15)
    add_far(0, 5, 6)
    add_near(0, 6, 8)
    add_far(0, 2, 3)
    kv_relay(1, 2)
    kv_relay(4, 5)
    landed(1, 7, 8)
    go(1, 16)
    add_relay(1, 1, 3)
    work(1, 6, 7)
    work(1, 4, 5)
    kv_done(3, 4)
    add_near(1, 1, 2)
    kv_done(1, 2)
    kv_done(4, 5)
    add_relay(1, 5, 6)
    work(1, 7, 8)
    kv_done(0, 1)
    kv_relay(2, 3)
    add_relay(1, 6, 7)
    add_relay(1, 3, 4)
    add_near(1, 2, 3)
    add_relay(1, 4, 5)
    add_near(1, 5, 6)
    turn(1, 2)
    add_far(0, 7, 8)
    kv_whole(0, 1)
    add_relay(1, 7, 8)
    add_near(1, 3, 4)
    add_far(1, 1, 2)
    kv_done(2, 3)
    add_far(0, 6, 7)
    add_far(1, 2, 3)
    add_near(1, 4, 5)
    add_near(1, 6, 7)
    kv_relay(7, 8)
    add_far(1, 5, 6)
    kv_relay(5, 6)
    kv_whole(1, 2)
    add_near(1, 7, 8)
    kv_whole(4, 5)
    kv_whole(3, 4)
    kv_relay(6, 7)
    kv_done(7, 8)
    turn(2, 3)
    kv_done(5, 6)
    add_far(1, 3, 4)
    kv_done(6, 7)
    kv_whole(2, 3)
    add_far(1, 6, 7)
    kv_whole(7, 8)
    add_far(1, 4, 5)
    add_far(1, 7, 8)
    kv_whole(5, 7)
    part_free()
    attend_forward(0)
    attend_backward(0)
    spread_home(0, (0,))
    attend_forward(1)
    spread_away(0, (0,))
    add_twin(0)
    attend_backward(1)
    spread_home(0, (1,))
    add_grads_relay(0)
    turn(3, 4)
    attend_forward(2)
    spread_away(0, (1,))
    spread_home(1, (1,))
    spread_home(1, (0,))
    attend_backward(2)
    spread_home(2, (0,))
    spread_away(1, (0,))
    spread_away(2, (0,))
    spread_away(1, (1,))
    add_twin(1)
    spread_relay(0, (1,))
    turn(4, 5)
    turn(5, 6)
    spread_home(2, (1,))
    spread_away(2, (1,))
    add_twin(2)
    add_grads_near(0)
    add_grads_relay(1)
    turn(6, 7)
    turn(7, 8)
    spread_relay(0, (0,))
    spread_relay(1, (1,))
    for k in range(17):
        gather(0, k).wait_send()
    multiply_out(0)
    spread_relay(2, (1,))
    add_grads_near(1)
    add_grads_relay(2)
    spread_relay(1, (0,))
    spread_home(0, (2,))
    spread_relay(2, (0,))
    spread_home(0, (3,))
    add_block_twin(0)
    spread_away(0, (2,))
    multiply_out(1)
    add_block_relay(0)
    multiply_out(2)
    add_block_twin(1)
    spread_home(1, (2,))
    spread_done(0, (0,))
    spread_done(1, (0,))
    spread_away(0, (3,))
    add_grads_near(2)
    add_block_twin(2)
    spread_away(1, (2,))
    spread_relay(0, (2,))
    add_block_near(0)
    add_block_relay(1)
    spread_done(1, (1,))
    spread_home(2, (2,))
    spread_relay(0, (3,))
    add_block_relay(2)
    spread_home(2, (3,))
    spread_done(2, (0,))
    multiply_out(3)
    grad_out_copy = pltpu.make_async_copy(grad_out, grad_out_hbm, last_sem.at[0])
    grad_out_copy.start()
    spread_home(1, (3,))
    add_block_far(0)
    add_block_near(1)
    spread_away(2, (2,))
    spread_away(2, (3,))
    spread_away(1, (3,))
    spread_relay(1, (2,))
    spread_done(0, (3,))
    spread_done(0, (2,))
    add_block_twin(3)
    spread_done(2, (1,))
    add_block_near(2)
    add_block_relay(3)
    spread_done(0, (1,))
    spread_relay(2, (2,))
    spread_relay(2, (3,))
    add_block_far(2)
    spread_relay(1, (3,))
    spread_done(1, (2,))
    add_block_near(3)
    spread_done(2, (3,))
    spread_done(2, (2,))
    add_block_far(1)
    spread_done(1, (3,))
    add_block_far(3)
    their_half = pl.ds(pl.multiple_of(128 - me.core * 128, 128), 128)
    end = remote(final.at[their_half], theirs, end_send, end_recv, twin)
    end.start()
    end.wait_recv()
    mine = final[pl.ds(pl.multiple_of(me.core * 128, 128), 128)]

    @pl.when(me.core == 0)
    def _():
        block_out[:, :768] = mine
        block_out[:, 768:] = theirs[...]

    @pl.when(me.core == 1)
    def _():
        block_out[:, :768] = theirs[...]
        block_out[:, 768:] = mine

    block_copy = pltpu.make_async_copy(block_out, block_hbm, last_sem.at[1])
    block_copy.start()

    @pl.when(is_away)
    def _():
        pl.loop(0, 8)(lambda s: rs3(1, s).wait_send())
        for h in range(3):
            for t in range(3):
                lift(h, t).wait_send()

    @pl.when(is_home)
    def _():
        for a in (0, 1):
            @pl.loop(0, 8)
            def _(s):
                rs4(a, s).wait_send()
        for h in range(3):
            for t in range(4):
                spread(h, t, 0).wait_send()
                if t in along_x_first:
                    for k in range(1, 8):
                        spread(h, t, k).wait_send()

    for k in range(17):
        gather(1, k).wait_send()

    @pl.loop(0, 8)
    def _(s):
        for d in (0, 1):
            rs1(1, s, d).wait_send()
            rs2(1, s, d).wait_send()
        for k in range(7):
            kv_gather(s, k).wait_send()

    for h in range(3):
        to_twin(h).wait_send()
        for d in (0, 1):
            gs1(h, d).wait_send()
            gs2(h, d).wait_send()
        for t in range(4):
            if t not in along_x_first:
                for k in range(1, 5):
                    spread(h, t, k).wait_send()
            if t > 0:
                keep_grads(h, t).wait()
    for i in range(4):
        for d in (0, 1):
            b0(i, d).wait_send()
            b1(i, d).wait_send()
            for y in (0, 1):
                b2(i, d, y).wait_send()
        b3(i).wait_send()
    for s in (5, 6, 7):
        keep(s).wait()
    grad_out_copy.wait()
    block_copy.wait()
    end.wait_send()


def block(inputs, grad_block, w_qkv, w_out):
    dma = pltpu.SemaphoreType.DMA
    anywhere = pl.BlockSpec(memory_space=pl.ANY)
    return pl.pallas_call(
        block_kernel,
        name="block",
        out_shape=(
            jax.ShapeDtypeStruct((1536, 2048), BF16),
            jax.ShapeDtypeStruct((8, 256, 1152), BF16),
            jax.ShapeDtypeStruct((128, 1536), BF16),
            jax.ShapeDtypeStruct((3, 128, 1536), F32),
        ),
        in_specs=[anywhere] * 4,
        out_specs=(anywhere,) * 4,
        scratch_shapes=[
            pltpu.VMEM((2, 32, 64, 1536), BF16),
            pltpu.VMEM((8, 4, 256, 384), BF16),
            pltpu.VMEM((8, 2, 4, 32, 384), BF16),
            pltpu.VMEM((8, 2, 4, 64, 384), BF16),
            pltpu.VMEM((8, 4, 64, 384), BF16),
            pltpu.VMEM((8, 4, 64, 384), BF16),
            pltpu.VMEM((3, 1536, 384), BF16),
            pltpu.VMEM((3, 128, 1536), BF16),
            pltpu.VMEM((128, 1536), BF16),
            pltpu.VMEM((3, 128, 1536), F32),
            pltpu.VMEM((2, 8, 256, 384), BF16),
            pltpu.VMEM((8, 256, 256), F32),
            pltpu.VMEM((8, 256, 256), F32),
            pltpu.VMEM((3, 2, 8, 256, 128), BF16),
            pltpu.VMEM((3, 8, 256, 128), BF16),
            pltpu.VMEM((3, 2, 4, 64, 128), BF16),
            pltpu.VMEM((3, 2, 8, 64, 128), BF16),
            pltpu.VMEM((4, 3, 8, 64, 128), BF16),
            pltpu.VMEM((4, 3, 8, 256, 128), BF16),
            pltpu.VMEM((384, 512), BF16),
            pltpu.VMEM((4, 2, 64, 768), BF16),
            pltpu.VMEM((4, 2, 2, 64, 768), BF16),
            pltpu.VMEM((4, 64, 768), BF16),
            pltpu.VMEM((256, 768), BF16),
            pltpu.VMEM((128, 768), BF16),
            dma((2, 17)), dma((2, 17)),
            dma((2, 8, 2)), dma((2, 8, 2)),
            dma((2, 8, 2)), dma((2, 8, 2)),
            dma((2, 8)), dma((2, 8)),
            dma((2, 8)), dma((2, 8)),
            dma((8,)), dma((2,)), dma((2,)), dma((2,)),
            dma((8, 7)), dma((8, 7)),
            dma((3,)), dma((3,)),
            dma((3, 2)), dma((3, 2)),
            dma((3, 2)), dma((3, 2)),
            dma((3, 3)), dma((3, 3)),
            dma((3, 4, 8)), dma((3, 4, 8)),
            dma((3, 4)), dma((3, 3)),
            dma((4, 2)), dma((4, 2)),
            dma((4, 2)), dma((4, 2)),
            dma((4, 2, 2)), dma((4, 2, 2)),
            dma((4,)), dma((4,)),
            dma(()), dma(()),
        ],
        compiler_params=pltpu.CompilerParams(
            collective_id=1, has_side_effects=True, vmem_limit_bytes=63 << 20
        ),
    )(inputs.reshape(2, 64, 1536), grad_block.reshape(2, 64, 1536), jnp.transpose(w_qkv, (1, 0, 2)), w_out)


def weight_kernel(x_hbm, rows_hbm, block_hbm, grad_out_hbm, out_hbm, block_copy, grad_out_copy, x, rows, out, block_rows, grad_out, x_sem, sem, out_sem):
    def load(m):
        features = pl.ds(m * 256, 256)
        return pltpu.make_async_copy(x_hbm.at[features], x.at[features], x_sem.at[m])

    def store(m, h):
        return pltpu.make_async_copy(out.at[m % 2, :, h * 384:(h + 1) * 384], out_hbm.at[h, pl.ds(m * 256, 256)], out_sem.at[m, h])

    copies = [
        pltpu.make_async_copy(rows_hbm, rows, sem.at[0]),
        pltpu.make_async_copy(block_hbm, block_rows, sem.at[1]),
        pltpu.make_async_copy(grad_out_hbm, grad_out, sem.at[2]),
    ]
    passed_on = [
        pltpu.make_async_copy(block_rows, block_copy, sem.at[1]),
        pltpu.make_async_copy(grad_out, grad_out_copy, sem.at[2]),
    ]
    copies[0].start()
    for m in range(6):
        load(m).start()
    copies[1].start()
    copies[2].start()
    copies[0].wait()
    for m in range(6):
        load(m).wait()
        if m >= 2:
            for h in range(3):
                store(m - 2, h).wait()
        out[m % 2] = jnp.dot(x[m * 256:(m + 1) * 256], rows[...].reshape(2048, 1152), preferred_element_type=F32)
        for h in range(3):
            store(m, h).start()
        if m == 1:
            for k in (1, 2):
                copies[k].wait()
                passed_on[k - 1].start()
    for m in (4, 5):
        for h in range(3):
            store(m, h).wait()
    for copy in passed_on:
        copy.wait()


def weight_grad(turned, rows, block_rows, grad_out):
    dma = pltpu.SemaphoreType.DMA
    anywhere = pl.BlockSpec(memory_space=pl.ANY)
    return pl.pallas_call(
        weight_kernel,
        name="weight_grad",
        out_shape=(
            jax.ShapeDtypeStruct((3, 1536, 384), F32),
            jax.ShapeDtypeStruct((128, 1536), BF16),
            jax.ShapeDtypeStruct((3, 128, 1536), F32),
        ),
        in_specs=[anywhere] * 4,
        out_specs=(anywhere,) * 3,
        scratch_shapes=[
            pltpu.VMEM((1536, 2048), BF16),
            pltpu.VMEM((8, 256, 1152), BF16),
            pltpu.VMEM((2, 256, 1152), F32),
            pltpu.VMEM((128, 1536), BF16),
            pltpu.VMEM((3, 128, 1536), F32),
            dma((6,)), dma((3,)), dma((6, 3)),
        ],
        compiler_params=pltpu.CompilerParams(vmem_limit_bytes=63 << 20),
    )(turned, rows, block_rows, grad_out)


def local(inputs, w_qkv, w_out, grad_block):
    turned, rows, block_rows, grad_out = block(inputs, grad_block, w_qkv, w_out)
    grad_qkv, block_out, grad_out = weight_grad(turned, rows, block_rows, grad_out)
    return block_out, jnp.transpose(grad_qkv, (1, 0, 2)), grad_out


def solution(mesh):
    placed = (P("row", "col"), P("col", "row", None), P("row", None, "col"), P("row", "col"))
    return jax.shard_map(
        local,
        mesh=mesh,
        in_specs=placed,
        out_specs=(P("row", "col"), P("col", "row", None), P("row", None, "col")),
        check_vma=False,
    )
```

```python
import jax
import jax.numpy as jnp
from jax import lax
from jax.experimental import pallas as pl
from jax.experimental.pallas import tpu as pltpu
from jax.sharding import PartitionSpec as P

MESH = pl.DeviceIdType.MESH
BF16 = jnp.bfloat16
F32 = jnp.float32


class Place:
    def __init__(self):
        r = lax.axis_index("row")
        c = lax.axis_index("col")
        self.ylo, self.z, self.core = r // 8, (r // 2) % 4, r % 2
        self.yhi, self.x = c // 4, c % 4

    def at(self, ylo=0, z=0, core=0, yhi=0, x=0):
        return (
            lax.rem(self.ylo + ylo, 2) * 8 + lax.rem(self.z + z + 4, 4) * 2 + lax.rem(self.core + core, 2),
            lax.rem(self.yhi + yhi, 2) * 4 + lax.rem(self.x + x + 4, 4),
        )

    def slot(self, ylo=0, z=0, core=0):
        return self.at(ylo=ylo, z=z, core=core)[0]

    def col_x(self, x):
        return lax.rem(self.x + x + 4, 4)


def meet(partners):
    barrier = pltpu.get_barrier_semaphore()
    for partner in partners:
        pl.semaphore_signal(barrier, inc=1, device_id=partner, device_id_type=MESH)
    pl.semaphore_wait(barrier, len(partners))


def remote(src, dst, send, recv, device):
    return pltpu.make_async_remote_copy(
        src_ref=src, dst_ref=dst, send_sem=send, recv_sem=recv, device_id=device, device_id_type=MESH
    )


slice_at = (0, -1, 1, 2)
along_x_first = (1,)


def block_kernel(
    x_hbm, g_hbm, w_hbm, wo_hbm,
    turned_out, grads_out, block_hbm, grad_out_hbm,
    held, part, relay, near, far, total, w_ref, wo_ref, block_out, grad_out,
    kv, scores, slopes, grads, twin_grads, grads_relay, grads_near, result,
    wide, turned, block_relay, block_near, block_far, final, theirs,
    ag_send, ag_recv, s1_send, s1_recv, s2_send, s2_recv, s3_send, s3_recv, s4_send, s4_recv, x_sem, w_sem, own_sem, last_sem,
    kv_send, kv_recv, tw_send, tw_recv, g1_send, g1_recv, g2_send, g2_recv, up_send, up_recv,
    wide_send, wide_recv, here_sem, out_sem, b0_send, b0_recv, b1_send, b1_recv, b2_send, b2_recv, b3_send, b3_recv,
    end_send, end_recv,
):
    me = Place()
    up, down, beside = me.at(z=1), me.at(z=-1), me.at(ylo=1)
    right, left, across, twin = me.at(x=1), me.at(x=-1), me.at(yhi=1), me.at(core=1)
    is_home = me.core == me.yhi
    is_away = jnp.logical_not(is_home)
    scale = 128 ** (-0.5)
    fill = -1e30
    low, high, every = pl.ds(0, 4), pl.ds(4, 4), pl.ds(0, 8)
    my_rows = pl.ds(pl.multiple_of(me.core * 32, 32), 32)
    their_rows = pl.ds(pl.multiple_of(32 - me.core * 32, 32), 32)

    def own(x=0):
        return pl.ds(pl.multiple_of(me.col_x(x) * 64, 64), 64)

    own_copy = [
        pltpu.make_async_copy(ref, held.at[a, pl.ds(me.slot() * 2, 2)], own_sem.at[a])
        for a, ref in enumerate((x_hbm, g_hbm))
    ]
    w_copy = [pltpu.make_async_copy(w_hbm.at[h], w_ref.at[:, h * 384:(h + 1) * 384], w_sem.at[h]) for h in range(3)]
    wo_copy = pltpu.make_async_copy(wo_hbm, wo_ref, w_sem.at[3])
    own_copy[0].start()
    for copy in w_copy:
        copy.start()
    own_copy[1].start()
    wo_copy.start()
    meet([beside, up, down, twin, right, left, across])

    def gather(a, k):
        slot, device = {
            0: (me.slot(), beside),
            1: (me.slot(), up),
            2: (me.slot(), down),
            3: (me.slot(ylo=1), up),
            4: (me.slot(ylo=1), down),
            5: (me.slot(z=-1), up),
            6: (me.slot(z=1), down),
            7: (me.slot(ylo=1, z=-1), up),
            8: (me.slot(ylo=1, z=1), down),
            9: (me.slot(), twin),
            10: (me.slot(ylo=1), twin),
            11: (me.slot(z=-1), twin),
            12: (me.slot(z=1), twin),
            13: (me.slot(ylo=1, z=-1), twin),
            14: (me.slot(ylo=1, z=1), twin),
            15: (me.slot(z=2), twin),
            16: (me.slot(ylo=1, z=2), twin),
        }[k]
        if k in (5, 7):
            rows = pl.ds(slot * 2, 1)
        elif k in (6, 8):
            rows = pl.ds(slot * 2 + 1, 1)
        else:
            rows = pl.ds(slot * 2, 2)
        ref = held.at[a, rows]
        return remote(ref, ref, ag_send.at[a, k], ag_recv.at[a, k], device)

    def go(a, *kinds):
        for k in kinds:
            gather(a, k).start()

    def landed(a, *kinds):
        for k in kinds:
            gather(a, k).wait_recv()

    def block_of(s):
        ylo = jnp.where((s == 1) | (s == 4) | (s == 5) | (s == 7), 1, 0)
        z = jnp.where((s == 2) | (s == 4), 3, jnp.where((s == 3) | (s == 5), 1, jnp.where(s >= 6, 2, 0)))
        return lax.rem(me.ylo + ylo, 2) * 4 + lax.rem(me.z + z, 4)

    def unit(a):
        return pl.ds(0, 3) if a == 0 else pl.ds(3, 1)

    def keep(s):
        columns = pl.ds(pl.multiple_of(block_of(s) * 256, 256), 256)
        return pltpu.make_async_copy(w_ref.at[:, s % 4 * 256:s % 4 * 256 + 256], turned_out.at[:, columns], x_sem.at[s])

    def turn(*steps):
        for s in range(*steps):
            if s >= 4:
                keep(s - 4).wait()
            for n in range(12):
                lanes = slice(n * 128, (n + 1) * 128)
                rows = held[0, pl.ds(block_of(s) * 4, 4), :, lanes].reshape(256, 128)
                w_ref[lanes, s % 4 * 256:s % 4 * 256 + 256] = rows.T

            keep(s).start()

    def rs1(a, s, d):
        rows = pl.ds(pl.multiple_of(me.col_x(2) * 64 + 32 * d, 32), 32)
        return remote(part.at[s, unit(a), rows], relay.at[s, d, unit(a)], s1_send.at[a, s, d], s1_recv.at[a, s, d], (right, left)[d])

    def rs2(a, s, d):
        return remote(part.at[s, unit(a), own((1, -1)[d])], near.at[s, d, unit(a)],
                      s2_send.at[a, s, d], s2_recv.at[a, s, d], (right, left)[d])

    def rs3(a, s):
        return remote(part.at[s, unit(a), own()], far.at[s, unit(a)], s3_send.at[a, s], s3_recv.at[a, s], across)

    def rs4(a, s):
        ref = total.at[block_of(s), unit(a)]
        return remote(ref, ref, s4_send.at[a, s], s4_recv.at[a, s], twin)

    def each(steps, body):
        lo, hi = steps
        if hi - lo == 1:
            body(lo)
        else:
            pl.loop(lo, hi)(body)

    def work(a, *steps):
        def body(s):
            remote(held.at[a, pl.ds(0, 2)], held.at[a, pl.ds(0, 2)], ag_send.at[a, 9 + s], ag_recv.at[a, 9 + s], twin).wait_recv()
            rows = held.at[a, pl.ds(block_of(s) * 4, 4)]
            if a == 0:
                product = jnp.dot(
                    rows[...].reshape(256, 1536), w_ref[...], preferred_element_type=F32
                ).astype(BF16)
                for h in range(3):
                    part[s, h] = product[:, h * 384:(h + 1) * 384]
            else:
                part[s, 3] = lax.dot_general(
                    rows[...].reshape(256, 1536), wo_ref[...].reshape(384, 1536),
                    (((1,), (1,)), ((), ())), preferred_element_type=F32,
                ).astype(BF16)
            for d in (0, 1):
                rs1(a, s, d).start()
        each(steps, body)

    def add(ref, *terms):
        value = ref[...].astype(F32)
        for term in terms:
            value = value + term.astype(F32)
        ref[...] = value.astype(BF16)

    def add_relay(a, *steps):
        def body(s):
            for d in (0, 1):
                rs1(a, s, d).wait_recv()
                rows = pl.ds(pl.multiple_of(me.col_x((1, -1)[d]) * 64 + 32 * d, 32), 32)
                add(part.at[s, unit(a), rows], relay[s, d, unit(a)])
                rs2(a, s, d).start()
        each(steps, body)

    def add_near(a, *steps):
        def body(s):
            for d in (0, 1):
                rs2(a, s, d).wait_recv()
            add(part.at[s, unit(a), own()], near[s, 0, unit(a)], near[s, 1, unit(a)])
            pl.when(is_away)(lambda: rs3(a, s).start())
        each(steps, body)

    def kv_gather(s, k):
        x, rows, device = {
            0: (0, 0, right),
            1: (0, 0, left),
            2: (-1, 1, right),
            3: (1, 2, left),
            4: (-1, 0, twin),
            5: (1, 0, twin),
            6: (2, 0, twin),
        }[k]
        start = me.col_x(x) * 64
        if rows == 0:
            span = pl.ds(pl.multiple_of(start, 64), 64)
        else:
            span = pl.ds(pl.multiple_of(start + 32 * (rows - 1), 32), 32)
        ref = kv.at[me.core, block_of(s), span]
        return remote(ref, ref, kv_send.at[s, k], kv_recv.at[s, k], device)

    def add_far(a, *steps):
        def body(s):
            block = block_of(s)

            @pl.when(is_home)
            def _():
                rs3(a, s).wait_recv()
                total[block, unit(a)] = (
                    part[s, unit(a), own()].astype(F32) + far[s, unit(a)].astype(F32)
                ).astype(BF16)
                rs4(a, s).start()

            @pl.when(is_away)
            def _():
                rs4(a, s).wait_recv()

            if a == 0:
                for j in (0, 1):
                    for h in range(3):
                        kv[j, block, own(), h * 128:(h + 1) * 128] = total[block, h, :, 128 + 128 * j:256 + 128 * j]
                kv_gather(s, 0).start()
                kv_gather(s, 1).start()
        each(steps, body)

    def kv_relay(*steps):
        def body(s):
            for d in (0, 1):
                kv_gather(s, d).wait_recv()
                kv_gather(s, 2 + d).start()
                kv_gather(s, 4 + d).start()
        each(steps, body)

    def kv_done(*steps):
        def body(s):
            kv_gather(s, 2).wait_recv()
            kv_gather(s, 3).wait_recv()
            kv_gather(s, 6).start()
        each(steps, body)

    def kv_whole(*steps):
        def body(s):
            for k in (4, 5, 6):
                kv_gather(s, k).wait_recv()
        each(steps, body)

    def part_free():
        for s in range(8):
            for d in (0, 1):
                rs1(0, s, d).wait_send()
                rs2(0, s, d).wait_send()

            @pl.when(is_away)
            def _():
                rs3(0, s).wait_send()

    transposed = (((1,), (1,)), ((), ()))
    by_rows = (((0,), (0,)), ((), ()))

    def query_of(h):
        return total[:, h, my_rows, 0:128].reshape(256, 128)

    def write_rows(t, h, low_half, high_half):
        rows = jnp.concatenate([low_half[:, :128], high_half], axis=1).T.astype(BF16)
        result[t, h, :, my_rows] = rows.reshape(8, 32, 128)

    def attend_forward(h):
        query = query_of(h)
        head = slice(h * 128, (h + 1) * 128)

        def masked(b, lanes):
            width = 256 - lanes
            s = lax.dot_general(kv[0, b, :, head], query[lanes:], transposed, preferred_element_type=F32) * scale
            key_at = b * 256 + lax.broadcasted_iota(jnp.int32, (256, width), 0)
            column = lanes + lax.broadcasted_iota(jnp.int32, (1, width), 1)
            query_at = (column // 32) * 256 + me.x * 64 + me.core * 32 + column % 32
            return jnp.where(key_at <= query_at, s, fill)

        def top(lanes):
            def body(b, m):
                s = masked(b, lanes)
                scores[b, :, lanes:] = s
                return jnp.maximum(m, jnp.max(s, axis=0, keepdims=True))
            return body

        m = lax.fori_loop(0, 4, top(0), jnp.full((1, 256), fill, F32), unroll=True)
        m_high = lax.fori_loop(4, 8, top(128), m[:, 128:], unroll=True)
        m = jnp.concatenate([m[:, :128], m_high], axis=1)

        def sums(lanes, m):
            def body(b, norm):
                e = jnp.exp(scores[b, :, lanes:] - m)
                scores[b, :, lanes:] = e
                return norm + jnp.sum(e, axis=0, keepdims=True)
            return body

        norm = lax.fori_loop(0, 4, sums(0, m), jnp.zeros((1, 256), F32), unroll=True)
        norm_high = lax.fori_loop(4, 8, sums(128, m_high), norm[:, 128:], unroll=True)
        inverse = 1.0 / jnp.concatenate([norm[:, :128], norm_high], axis=1)

        def rows(lanes):
            def body(b, att):
                w = (scores[b, :, lanes:] * inverse[:, lanes:]).astype(BF16)
                part[b, h, :, lanes:256] = w
                return att + lax.dot_general(kv[1, b, :, head], w, by_rows, preferred_element_type=F32)
            return body

        att = lax.fori_loop(0, 4, rows(0), jnp.zeros((128, 256), F32), unroll=True)
        att_high = lax.fori_loop(4, 8, rows(128), att[:, 128:], unroll=True)
        write_rows(0, h, att, att_high)
        pl.when(is_away)(lambda: lift(h, 0).start())

    def attend_backward(h):
        query = query_of(h)
        head = slice(h * 128, (h + 1) * 128)
        cotangent = total[:, 3, my_rows, head].reshape(256, 128)

        def sums(lanes):
            def body(b, slope):
                dp = lax.dot_general(kv[1, b, :, head], cotangent[lanes:], transposed, preferred_element_type=F32)
                slopes[b, :, lanes:] = dp
                return slope + jnp.sum(part[b, h, :, lanes:256].astype(F32) * dp, axis=0, keepdims=True)
            return body

        slope = lax.fori_loop(0, 4, sums(0), jnp.zeros((1, 256), F32), unroll=True)
        slope_high = lax.fori_loop(4, 8, sums(128), slope[:, 128:], unroll=True)
        slope = jnp.concatenate([slope[:, :128], slope_high], axis=1)

        def terms(lanes):
            def body(b, dq):
                w = part[b, h, :, lanes:256]
                ds = (w.astype(F32) * (slopes[b, :, lanes:] - slope[:, lanes:]) * scale).astype(BF16)
                grads[h, 0, b] = jnp.dot(ds, query[lanes:], preferred_element_type=F32).astype(BF16)
                grads[h, 1, b] = jnp.dot(w, cotangent[lanes:], preferred_element_type=F32).astype(BF16)
                return dq + lax.dot_general(kv[0, b, :, head], ds, by_rows, preferred_element_type=F32)
            return body

        dq = lax.fori_loop(0, 4, terms(0), jnp.zeros((128, 256), F32), unroll=True)
        dq_high = lax.fori_loop(4, 8, terms(128), dq[:, 128:], unroll=True)
        write_rows(1, h, dq, dq_high)
        to_twin(h).start()
        pl.when(is_away)(lambda: lift(h, 1).start())

    def to_twin(h):
        return remote(grads.at[h, 1 - me.core], twin_grads.at[h], tw_send.at[h], tw_recv.at[h], twin)

    def gs1(h, d):
        return remote(grads.at[h, me.core, (low, high)[d], own(2)], grads_relay.at[h, d],
                      g1_send.at[h, d], g1_recv.at[h, d], (right, left)[d])

    def gs2(h, d):
        return remote(grads.at[h, me.core, every, own((1, -1)[d])], grads_near.at[h, d],
                      g2_send.at[h, d], g2_recv.at[h, d], (right, left)[d])

    def add_twin(h):
        to_twin(h).wait_recv()

        @pl.loop(0, 8)
        def _(b):
            add(grads.at[h, me.core, b], twin_grads[h, b])

        for d in (0, 1):
            gs1(h, d).start()

    def add_grads_relay(h):
        for d in (0, 1):
            gs1(h, d).wait_recv()
            add(grads.at[h, me.core, (low, high)[d], own((1, -1)[d])], grads_relay[h, d])
            gs2(h, d).start()

    def add_grads_near(h):
        for d in (0, 1):
            gs2(h, d).wait_recv()
        result[2 + me.core, h] = (
            grads[h, me.core, :, own()].astype(F32) + grads_near[h, 0].astype(F32) + grads_near[h, 1].astype(F32)
        ).astype(BF16)

        @pl.when(is_away)
        def _():
            lift(h, 2).start()

    def lift(h, t):
        if t < 2:
            ref = result.at[t, h, every, my_rows]
        else:
            ref = result.at[2 + me.core, h]
        return remote(ref, ref, up_send.at[h, t], up_recv.at[h, t], twin)

    def lifted(h, t):
        ref = result.at[t, h, every, their_rows] if t < 2 else result.at[3 - me.core, h]
        remote(ref, ref, up_send.at[h, t], up_recv.at[h, t], twin).wait_recv()

    def spread(h, t, k):
        x, blocks, device = {
            0: (0, every, across),
            1: (0, every, right),
            2: (0, every, left),
            3: (-1, low, right),
            4: (1, high, left),
            5: (-1, every, across),
            6: (1, every, across),
            7: (2, every, across),
        }[k]
        ref = wide.at[t, h, blocks, own(x)]
        src = result.at[t, h] if k == 0 else ref
        return remote(src, ref, wide_send.at[h, t, k], wide_recv.at[h, t, k], device)

    def here(h, t):
        return pltpu.make_async_copy(result.at[t, h], wide.at[t, h, every, own()], here_sem.at[h, t])

    def spread_home(h, types):
        @pl.when(is_home)
        def _():
            for t in types:
                if t < 3:
                    lifted(h, t)
                spread(h, t, 0).start()
                here(h, t).start()
            for t in types:
                here(h, t).wait()
                spread(h, t, 1).start()
                spread(h, t, 2).start()

    def spread_away(h, types):
        @pl.when(is_away)
        def _():
            for t in types:
                spread(h, t, 0).wait_recv()
                if t not in along_x_first:
                    spread(h, t, 1).start()
                    spread(h, t, 2).start()

    def spread_relay(h, types):
        def around(t):
            for d in (0, 1):
                spread(h, t, 1 + d).wait_recv()
                spread(h, t, 3 + d).start()
                if t in along_x_first:
                    spread(h, t, 5 + d).start()

        for t in types:
            if t not in along_x_first:
                around(t)

        def home_rows():
            for t in types:
                if t in along_x_first:
                    around(t)

        def away_rows():
            for t in types:
                if t in along_x_first:
                    spread(h, t, 5).wait_recv()
                    spread(h, t, 6).wait_recv()

        pl.when(is_home)(home_rows)
        pl.when(is_away)(away_rows)

    def keep_grads(h, t):
        lanes = pl.ds(h * 384 + (t - 1) * 128, 128)
        return pltpu.make_async_copy(wide.at[t, h], grads_out.at[:, :, lanes], out_sem.at[h, t - 1])

    def spread_done(h, types):
        def arrived(t):
            spread(h, t, 3).wait_recv()
            spread(h, t, 4).wait_recv()

        def home_rows():
            for t in types:
                if t in along_x_first:
                    arrived(t)
                    spread(h, t, 7).start()

        def away_rows():
            for t in types:
                if t in along_x_first:
                    spread(h, t, 7).wait_recv()

        for t in types:
            if t not in along_x_first:
                arrived(t)
        pl.when(is_home)(home_rows)
        pl.when(is_away)(away_rows)
        for t in types:
            if t > 0:
                keep_grads(h, t).start()

    def block_lanes(core, n=None):
        if n is None:
            return pl.ds(pl.multiple_of(core * 768, 768), 768)
        return pl.ds(pl.multiple_of(core * 768 + n * 384, 384), 384)

    def b0(i, n):
        return remote(held.at[0, pl.ds(i * 8, 8), :, block_lanes(1 - me.core, n)], near.at[:, n, i],
                      b0_send.at[i, n], b0_recv.at[i, n], twin)

    def z_at(z):
        return lax.rem(me.z + z + 4, 4)

    def term_at(i, y, z):
        return held.at[0, i * 8 + y * 4 + z, :, block_lanes(me.core)]

    def b1(i, d):
        return remote(term_at(i, d, z_at(2)), block_relay.at[i, d], b1_send.at[i, d], b1_recv.at[i, d], (up, down)[d])

    def b2(i, d, y):
        return remote(term_at(i, y, z_at((1, -1)[d])), block_near.at[i, d, y], b2_send.at[i, d, y], b2_recv.at[i, d, y], (up, down)[d])

    def b3(i):
        return remote(term_at(i, 1 - me.ylo, me.z), block_far.at[i], b3_send.at[i], b3_recv.at[i], beside)

    def multiply_out(i):
        mine = jnp.concatenate([wide[0, h, :, own(slice_at[i])].reshape(512, 128) for h in range(3)], axis=1)
        turned[...] = mine.T

        for n in (0, 1):
            lanes = slice(n * 768, (n + 1) * 768)
            held[0, pl.ds(i * 8, 8), :, lanes] = jnp.dot(
                mine, wo_ref[:, :, lanes].reshape(384, 768), preferred_element_type=F32
            ).astype(BF16).reshape(8, 64, 768)
        b0(i, 0).start()
        b0(i, 1).start()
        for n in (0, 1):
            lanes = slice(n * 768, (n + 1) * 768)
            tokens = [held[1, b * 4 + me.col_x(slice_at[i]), :, lanes] for b in range(8)]
            term = jnp.dot(
                turned[...], jnp.concatenate(tokens, axis=0), preferred_element_type=F32
            ).reshape(3, 128, 768)
            if i == 0:
                grad_out[:, :, lanes] = term
            else:
                grad_out[:, :, lanes] += term

    def add_block_twin(i):
        for n in (0, 1):
            b0(i, n).wait_recv()

            @pl.loop(0, 8)
            def _(b):
                add(held.at[0, i * 8 + b, :, block_lanes(me.core, n)], near[b, n, i])

        for d in (0, 1):
            b1(i, d).start()

    def add_block_relay(i):
        for d in (0, 1):
            b2(i, d, 1 - d).start()
        for d in (0, 1):
            b1(i, d).wait_recv()
            add(term_at(i, d, z_at((1, -1)[d])), block_relay[i, d])
            b2(i, d, d).start()

    def add_block_near(i):
        for d in (0, 1):
            for y in (0, 1):
                b2(i, d, y).wait_recv()
        for y in (0, 1):
            add(term_at(i, y, me.z), block_near[i, 0, y], block_near[i, 1, y])
        b3(i).start()

    def add_block_far(i):
        b3(i).wait_recv()
        final[own(slice_at[i])] = (term_at(i, me.ylo, me.z)[...].astype(F32) + block_far[i].astype(F32)).astype(BF16)

    own_copy[0].wait()
    go(0, 9, 0, 1, 2)
    own_copy[1].wait()
    go(1, 9)
    wo_copy.wait()
    work(1, 0, 1)
    for copy in w_copy:
        copy.wait()
    work(0, 0, 1)
    add_relay(0, 0, 1)
    landed(0, 0)
    go(0, 3, 4, 10)
    landed(0, 2)
    go(0, 6, 12)
    landed(0, 1)
    go(0, 5, 11)
    add_relay(1, 0, 1)
    work(0, 1, 4)
    add_relay(0, 2, 3)
    add_near(0, 0, 1)
    landed(0, 4)
    go(0, 8, 14)
    add_relay(0, 1, 2)
    go(1, 0)
    add_relay(0, 3, 4)
    landed(0, 3)
    go(0, 7, 13)
    work(0, 4, 5)
    go(1, 1, 2)
    add_near(1, 0, 1)
    work(0, 5, 6)
    add_far(0, 0, 1)
    landed(0, 5, 6)
    go(0, 15)
    landed(0, 7, 8)
    go(0, 16)
    work(0, 6, 7)
    add_near(0, 3, 4)
    landed(1, 0)
    go(1, 3, 4, 10)
    work(0, 7, 8)
    add_relay(0, 4, 5)
    work(1, 1, 2)
    add_far(0, 3, 4)
    add_near(0, 1, 2)
    add_relay(0, 5, 6)
    add_near(0, 4, 5)
    add_relay(0, 6, 7)
    kv_relay(3, 4)
    add_far(1, 0, 1)
    kv_relay(0, 1)
    turn(0, 1)
    landed(1, 1)
    go(1, 5, 11)
    add_far(0, 1, 2)
    landed(1, 2)
    go(1, 6, 12)
    add_near(0, 5, 6)
    add_near(0, 2, 3)
    landed(1, 3)
    go(1, 7, 13)
    add_far(0, 4, 5)
    work(1, 2, 3)
    landed(1, 4)
    go(1, 8, 14)
    add_relay(0, 7, 8)
    work(1, 3, 4)
    work(1, 5, 6)
    landed(1, 5, 6)
    go(1, 15)
    add_far(0, 5, 6)
    add_near(0, 6, 8)
    add_far(0, 2, 3)
    kv_relay(1, 2)
    kv_relay(4, 5)
    landed(1, 7, 8)
    go(1, 16)
    add_relay(1, 1, 3)
    work(1, 6, 7)
    work(1, 4, 5)
    kv_done(3, 4)
    add_near(1, 1, 2)
    kv_done(1, 2)
    kv_done(4, 5)
    add_relay(1, 5, 6)
    work(1, 7, 8)
    kv_done(0, 1)
    kv_relay(2, 3)
    add_relay(1, 6, 7)
    add_relay(1, 3, 4)
    add_near(1, 2, 3)
    add_relay(1, 4, 5)
    add_near(1, 5, 6)
    turn(1, 2)
    add_far(0, 7, 8)
    kv_whole(0, 1)
    add_relay(1, 7, 8)
    add_near(1, 3, 4)
    add_far(1, 1, 2)
    kv_done(2, 3)
    add_far(0, 6, 7)
    add_far(1, 2, 3)
    add_near(1, 4, 5)
    add_near(1, 6, 7)
    kv_relay(7, 8)
    add_far(1, 5, 6)
    kv_relay(5, 6)
    kv_whole(1, 2)
    add_near(1, 7, 8)
    kv_whole(4, 5)
    kv_whole(3, 4)
    kv_relay(6, 7)
    kv_done(7, 8)
    turn(2, 3)
    kv_done(5, 6)
    add_far(1, 3, 4)
    kv_done(6, 7)
    kv_whole(2, 3)
    add_far(1, 6, 7)
    kv_whole(7, 8)
    add_far(1, 4, 5)
    add_far(1, 7, 8)
    kv_whole(5, 7)
    part_free()
    attend_forward(0)
    attend_backward(0)
    spread_home(0, (0,))
    attend_forward(1)
    spread_away(0, (0,))
    add_twin(0)
    attend_backward(1)
    spread_home(0, (1,))
    add_grads_relay(0)
    turn(3, 4)
    attend_forward(2)
    spread_away(0, (1,))
    spread_home(1, (1,))
    spread_home(1, (0,))
    attend_backward(2)
    spread_home(2, (0,))
    spread_away(1, (0,))
    spread_away(2, (0,))
    spread_away(1, (1,))
    add_twin(1)
    spread_relay(0, (1,))
    turn(4, 5)
    turn(5, 6)
    spread_home(2, (1,))
    spread_away(2, (1,))
    add_twin(2)
    add_grads_near(0)
    add_grads_relay(1)
    turn(6, 7)
    turn(7, 8)
    spread_relay(0, (0,))
    spread_relay(1, (1,))
    for k in range(17):
        gather(0, k).wait_send()
    multiply_out(0)
    spread_relay(2, (1,))
    add_grads_near(1)
    add_grads_relay(2)
    spread_relay(1, (0,))
    spread_home(0, (2,))
    spread_relay(2, (0,))
    spread_home(0, (3,))
    add_block_twin(0)
    spread_away(0, (2,))
    multiply_out(1)
    add_block_relay(0)
    multiply_out(2)
    add_block_twin(1)
    spread_home(1, (2,))
    spread_done(0, (0,))
    spread_done(1, (0,))
    spread_away(0, (3,))
    add_grads_near(2)
    add_block_twin(2)
    spread_away(1, (2,))
    spread_relay(0, (2,))
    add_block_near(0)
    add_block_relay(1)
    spread_done(1, (1,))
    spread_home(2, (2,))
    spread_relay(0, (3,))
    add_block_relay(2)
    spread_home(2, (3,))
    spread_done(2, (0,))
    multiply_out(3)
    grad_out_copy = pltpu.make_async_copy(grad_out, grad_out_hbm, last_sem.at[0])
    grad_out_copy.start()
    spread_home(1, (3,))
    add_block_far(0)
    add_block_near(1)
    spread_away(2, (2,))
    spread_away(2, (3,))
    spread_away(1, (3,))
    spread_relay(1, (2,))
    spread_done(0, (3,))
    spread_done(0, (2,))
    add_block_twin(3)
    spread_done(2, (1,))
    add_block_near(2)
    add_block_relay(3)
    spread_done(0, (1,))
    spread_relay(2, (2,))
    spread_relay(2, (3,))
    add_block_far(2)
    spread_relay(1, (3,))
    spread_done(1, (2,))
    add_block_near(3)
    spread_done(2, (3,))
    spread_done(2, (2,))
    add_block_far(1)
    spread_done(1, (3,))
    add_block_far(3)
    their_half = pl.ds(pl.multiple_of(128 - me.core * 128, 128), 128)
    end = remote(final.at[their_half], theirs, end_send, end_recv, twin)
    end.start()
    end.wait_recv()
    mine = final[pl.ds(pl.multiple_of(me.core * 128, 128), 128)]

    @pl.when(me.core == 0)
    def _():
        block_out[:, :768] = mine
        block_out[:, 768:] = theirs[...]

    @pl.when(me.core == 1)
    def _():
        block_out[:, :768] = theirs[...]
        block_out[:, 768:] = mine

    block_copy = pltpu.make_async_copy(block_out, block_hbm, last_sem.at[1])
    block_copy.start()

    @pl.when(is_away)
    def _():
        pl.loop(0, 8)(lambda s: rs3(1, s).wait_send())
        for h in range(3):
            for t in range(3):
                lift(h, t).wait_send()

    @pl.when(is_home)
    def _():
        for a in (0, 1):
            @pl.loop(0, 8)
            def _(s):
                rs4(a, s).wait_send()
        for h in range(3):
            for t in range(4):
                spread(h, t, 0).wait_send()
                if t in along_x_first:
                    for k in range(1, 8):
                        spread(h, t, k).wait_send()

    for k in range(17):
        gather(1, k).wait_send()

    @pl.loop(0, 8)
    def _(s):
        for d in (0, 1):
            rs1(1, s, d).wait_send()
            rs2(1, s, d).wait_send()
        for k in range(7):
            kv_gather(s, k).wait_send()

    for h in range(3):
        to_twin(h).wait_send()
        for d in (0, 1):
            gs1(h, d).wait_send()
            gs2(h, d).wait_send()
        for t in range(4):
            if t not in along_x_first:
                for k in range(1, 5):
                    spread(h, t, k).wait_send()
            if t > 0:
                keep_grads(h, t).wait()
    for i in range(4):
        for d in (0, 1):
            b0(i, d).wait_send()
            b1(i, d).wait_send()
            for y in (0, 1):
                b2(i, d, y).wait_send()
        b3(i).wait_send()
    for s in (4, 5, 6, 7):
        keep(s).wait()
    grad_out_copy.wait()
    block_copy.wait()
    end.wait_send()


def block(inputs, grad_block, w_qkv, w_out):
    dma = pltpu.SemaphoreType.DMA
    anywhere = pl.BlockSpec(memory_space=pl.ANY)
    return pl.pallas_call(
        block_kernel,
        name="block",
        out_shape=(
            jax.ShapeDtypeStruct((1536, 2048), BF16),
            jax.ShapeDtypeStruct((8, 256, 1152), BF16),
            jax.ShapeDtypeStruct((128, 1536), BF16),
            jax.ShapeDtypeStruct((3, 128, 1536), F32),
        ),
        in_specs=[anywhere] * 4,
        out_specs=(anywhere,) * 4,
        scratch_shapes=[
            pltpu.VMEM((2, 32, 64, 1536), BF16),
            pltpu.VMEM((8, 4, 256, 384), BF16),
            pltpu.VMEM((8, 2, 4, 32, 384), BF16),
            pltpu.VMEM((8, 2, 4, 64, 384), BF16),
            pltpu.VMEM((8, 4, 64, 384), BF16),
            pltpu.VMEM((8, 4, 64, 384), BF16),
            pltpu.VMEM((1536, 1152), BF16),
            pltpu.VMEM((3, 128, 1536), BF16),
            pltpu.VMEM((128, 1536), BF16),
            pltpu.VMEM((3, 128, 1536), F32),
            pltpu.VMEM((2, 8, 256, 384), BF16),
            pltpu.VMEM((8, 256, 256), F32),
            pltpu.VMEM((8, 256, 256), F32),
            pltpu.VMEM((3, 2, 8, 256, 128), BF16),
            pltpu.VMEM((3, 8, 256, 128), BF16),
            pltpu.VMEM((3, 2, 4, 64, 128), BF16),
            pltpu.VMEM((3, 2, 8, 64, 128), BF16),
            pltpu.VMEM((4, 3, 8, 64, 128), BF16),
            pltpu.VMEM((4, 3, 8, 256, 128), BF16),
            pltpu.VMEM((384, 512), BF16),
            pltpu.VMEM((4, 2, 64, 768), BF16),
            pltpu.VMEM((4, 2, 2, 64, 768), BF16),
            pltpu.VMEM((4, 64, 768), BF16),
            pltpu.VMEM((256, 768), BF16),
            pltpu.VMEM((128, 768), BF16),
            dma((2, 17)), dma((2, 17)),
            dma((2, 8, 2)), dma((2, 8, 2)),
            dma((2, 8, 2)), dma((2, 8, 2)),
            dma((2, 8)), dma((2, 8)),
            dma((2, 8)), dma((2, 8)),
            dma((8,)), dma((4,)), dma((2,)), dma((2,)),
            dma((8, 7)), dma((8, 7)),
            dma((3,)), dma((3,)),
            dma((3, 2)), dma((3, 2)),
            dma((3, 2)), dma((3, 2)),
            dma((3, 3)), dma((3, 3)),
            dma((3, 4, 8)), dma((3, 4, 8)),
            dma((3, 4)), dma((3, 3)),
            dma((4, 2)), dma((4, 2)),
            dma((4, 2)), dma((4, 2)),
            dma((4, 2, 2)), dma((4, 2, 2)),
            dma((4,)), dma((4,)),
            dma(()), dma(()),
        ],
        compiler_params=pltpu.CompilerParams(
            collective_id=1, has_side_effects=True, vmem_limit_bytes=63 << 20
        ),
    )(inputs.reshape(2, 64, 1536), grad_block.reshape(2, 64, 1536), jnp.transpose(w_qkv, (1, 0, 2)), w_out)


def weight_kernel(x_hbm, rows_hbm, block_hbm, grad_out_hbm, out_hbm, block_copy, grad_out_copy, x, rows, out, block_rows, grad_out, x_sem, sem, out_sem):
    def load(m):
        features = pl.ds(m * 256, 256)
        return pltpu.make_async_copy(x_hbm.at[features], x.at[features], x_sem.at[m])

    def store(m, h):
        return pltpu.make_async_copy(out.at[m % 2, :, h * 384:(h + 1) * 384], out_hbm.at[h, pl.ds(m * 256, 256)], out_sem.at[m, h])

    copies = [
        pltpu.make_async_copy(rows_hbm, rows, sem.at[0]),
        pltpu.make_async_copy(block_hbm, block_rows, sem.at[1]),
        pltpu.make_async_copy(grad_out_hbm, grad_out, sem.at[2]),
    ]
    passed_on = [
        pltpu.make_async_copy(block_rows, block_copy, sem.at[1]),
        pltpu.make_async_copy(grad_out, grad_out_copy, sem.at[2]),
    ]
    copies[0].start()
    for m in range(6):
        load(m).start()
    copies[1].start()
    copies[2].start()
    copies[0].wait()
    for m in range(6):
        load(m).wait()
        if m >= 2:
            for h in range(3):
                store(m - 2, h).wait()
        out[m % 2] = jnp.dot(x[m * 256:(m + 1) * 256], rows[...].reshape(2048, 1152), preferred_element_type=F32)
        for h in range(3):
            store(m, h).start()
        if m == 1:
            for k in (1, 2):
                copies[k].wait()
                passed_on[k - 1].start()
    for m in (4, 5):
        for h in range(3):
            store(m, h).wait()
    for copy in passed_on:
        copy.wait()


def weight_grad(turned, rows, block_rows, grad_out):
    dma = pltpu.SemaphoreType.DMA
    anywhere = pl.BlockSpec(memory_space=pl.ANY)
    return pl.pallas_call(
        weight_kernel,
        name="weight_grad",
        out_shape=(
            jax.ShapeDtypeStruct((3, 1536, 384), F32),
            jax.ShapeDtypeStruct((128, 1536), BF16),
            jax.ShapeDtypeStruct((3, 128, 1536), F32),
        ),
        in_specs=[anywhere] * 4,
        out_specs=(anywhere,) * 3,
        scratch_shapes=[
            pltpu.VMEM((1536, 2048), BF16),
            pltpu.VMEM((8, 256, 1152), BF16),
            pltpu.VMEM((2, 256, 1152), F32),
            pltpu.VMEM((128, 1536), BF16),
            pltpu.VMEM((3, 128, 1536), F32),
            dma((6,)), dma((3,)), dma((6, 3)),
        ],
        compiler_params=pltpu.CompilerParams(vmem_limit_bytes=63 << 20),
    )(turned, rows, block_rows, grad_out)


def local(inputs, w_qkv, w_out, grad_block):
    turned, rows, block_rows, grad_out = block(inputs, grad_block, w_qkv, w_out)
    grad_qkv, block_out, grad_out = weight_grad(turned, rows, block_rows, grad_out)
    return block_out, jnp.transpose(grad_qkv, (1, 0, 2)), grad_out


def solution(mesh):
    placed = (P("row", "col"), P("col", "row", None), P("row", None, "col"), P("row", "col"))
    return jax.shard_map(
        local,
        mesh=mesh,
        in_specs=placed,
        out_specs=(P("row", "col"), P("col", "row", None), P("row", None, "col")),
        check_vma=False,
    )
```

```python
import jax
import jax.numpy as jnp
from jax import lax
from jax.experimental import pallas as pl
from jax.experimental.pallas import tpu as pltpu
from jax.sharding import PartitionSpec as P

MESH = pl.DeviceIdType.MESH
BF16 = jnp.bfloat16
F32 = jnp.float32


class Place:
    def __init__(self):
        r = lax.axis_index("row")
        c = lax.axis_index("col")
        self.ylo, self.z, self.core = r // 8, (r // 2) % 4, r % 2
        self.yhi, self.x = c // 4, c % 4

    def at(self, ylo=0, z=0, core=0, yhi=0, x=0):
        return (
            lax.rem(self.ylo + ylo, 2) * 8 + lax.rem(self.z + z + 4, 4) * 2 + lax.rem(self.core + core, 2),
            lax.rem(self.yhi + yhi, 2) * 4 + lax.rem(self.x + x + 4, 4),
        )

    def slot(self, ylo=0, z=0, core=0):
        return self.at(ylo=ylo, z=z, core=core)[0]

    def col_x(self, x):
        return lax.rem(self.x + x + 4, 4)


def meet(partners):
    barrier = pltpu.get_barrier_semaphore()
    for partner in partners:
        pl.semaphore_signal(barrier, inc=1, device_id=partner, device_id_type=MESH)
    pl.semaphore_wait(barrier, len(partners))


def remote(src, dst, send, recv, device):
    return pltpu.make_async_remote_copy(
        src_ref=src, dst_ref=dst, send_sem=send, recv_sem=recv, device_id=device, device_id_type=MESH
    )


slice_at = (0, -1, 1, 2)
along_x_first = (1,)


def block_kernel(
    x_hbm, g_hbm, w_hbm, wo_hbm,
    turned_out, grads_out, block_hbm, grad_out_hbm,
    held, part, relay, near, far, total, w_ref, wo_ref, block_out, grad_out,
    kv, scores, slopes, grads, twin_grads, grads_relay, grads_near, result,
    wide, turned, block_relay, block_near, block_far, final, theirs,
    ag_send, ag_recv, s1_send, s1_recv, s2_send, s2_recv, s3_send, s3_recv, s4_send, s4_recv, x_sem, w_sem, own_sem, last_sem,
    kv_send, kv_recv, tw_send, tw_recv, g1_send, g1_recv, g2_send, g2_recv, up_send, up_recv,
    wide_send, wide_recv, here_sem, out_sem, b0_send, b0_recv, b1_send, b1_recv, b2_send, b2_recv, b3_send, b3_recv,
    end_send, end_recv,
):
    me = Place()
    up, down, beside = me.at(z=1), me.at(z=-1), me.at(ylo=1)
    right, left, across, twin = me.at(x=1), me.at(x=-1), me.at(yhi=1), me.at(core=1)
    is_home = me.core == me.yhi
    is_away = jnp.logical_not(is_home)
    scale = 128 ** (-0.5)
    fill = -1e30
    low, high, every = pl.ds(0, 4), pl.ds(4, 4), pl.ds(0, 8)
    my_rows = pl.ds(pl.multiple_of(me.core * 32, 32), 32)
    their_rows = pl.ds(pl.multiple_of(32 - me.core * 32, 32), 32)

    def own(x=0):
        return pl.ds(pl.multiple_of(me.col_x(x) * 64, 64), 64)

    own_copy = [
        pltpu.make_async_copy(ref, held.at[a, pl.ds(me.slot() * 2, 2)], own_sem.at[a])
        for a, ref in enumerate((x_hbm, g_hbm))
    ]
    w_copy = [pltpu.make_async_copy(w_hbm.at[h], w_ref.at[:, h * 384:(h + 1) * 384], w_sem.at[h]) for h in range(3)]
    wo_copy = pltpu.make_async_copy(wo_hbm, wo_ref, w_sem.at[3])
    own_copy[0].start()
    for copy in w_copy:
        copy.start()
    own_copy[1].start()
    wo_copy.start()
    meet([beside, up, down, twin, right, left, across])

    def gather(a, k):
        slot, device = {
            0: (me.slot(), beside),
            1: (me.slot(), up),
            2: (me.slot(), down),
            3: (me.slot(ylo=1), up),
            4: (me.slot(ylo=1), down),
            5: (me.slot(z=-1), up),
            6: (me.slot(z=1), down),
            7: (me.slot(ylo=1, z=-1), up),
            8: (me.slot(ylo=1, z=1), down),
            9: (me.slot(), twin),
            10: (me.slot(ylo=1), twin),
            11: (me.slot(z=-1), twin),
            12: (me.slot(z=1), twin),
            13: (me.slot(ylo=1, z=-1), twin),
            14: (me.slot(ylo=1, z=1), twin),
            15: (me.slot(z=2), twin),
            16: (me.slot(ylo=1, z=2), twin),
        }[k]
        if k in (5, 7):
            rows = pl.ds(slot * 2, 1)
        elif k in (6, 8):
            rows = pl.ds(slot * 2 + 1, 1)
        else:
            rows = pl.ds(slot * 2, 2)
        ref = held.at[a, rows]
        return remote(ref, ref, ag_send.at[a, k], ag_recv.at[a, k], device)

    def go(a, *kinds):
        for k in kinds:
            gather(a, k).start()

    def landed(a, *kinds):
        for k in kinds:
            gather(a, k).wait_recv()

    def block_of(s):
        ylo = jnp.where((s == 1) | (s == 4) | (s == 5) | (s == 7), 1, 0)
        z = jnp.where((s == 2) | (s == 4), 3, jnp.where((s == 3) | (s == 5), 1, jnp.where(s >= 6, 2, 0)))
        return lax.rem(me.ylo + ylo, 2) * 4 + lax.rem(me.z + z, 4)

    def unit(a):
        return pl.ds(0, 3) if a == 0 else pl.ds(3, 1)

    def keep(s):
        columns = pl.ds(pl.multiple_of(block_of(s) * 256, 256), 256)
        return pltpu.make_async_copy(w_ref.at[:, s % 4 * 256:s % 4 * 256 + 256], turned_out.at[:, columns], x_sem.at[s])

    def turn(*steps):
        for s in range(*steps):
            if s >= 4:
                keep(s - 4).wait()
            for n in range(12):
                lanes = slice(n * 128, (n + 1) * 128)
                rows = held[0, pl.ds(block_of(s) * 4, 4), :, lanes].reshape(256, 128)
                w_ref[lanes, s % 4 * 256:s % 4 * 256 + 256] = rows.T

            keep(s).start()

    def rs1(a, s, d):
        rows = pl.ds(pl.multiple_of(me.col_x(2) * 64 + 32 * d, 32), 32)
        return remote(part.at[s, unit(a), rows], relay.at[s, d, unit(a)], s1_send.at[a, s, d], s1_recv.at[a, s, d], (right, left)[d])

    def rs2(a, s, d):
        return remote(part.at[s, unit(a), own((1, -1)[d])], near.at[s, d, unit(a)],
                      s2_send.at[a, s, d], s2_recv.at[a, s, d], (right, left)[d])

    def rs3(a, s):
        return remote(part.at[s, unit(a), own()], far.at[s, unit(a)], s3_send.at[a, s], s3_recv.at[a, s], across)

    def rs4(a, s):
        ref = total.at[block_of(s), unit(a)]
        return remote(ref, ref, s4_send.at[a, s], s4_recv.at[a, s], twin)

    def each(steps, body):
        lo, hi = steps
        if hi - lo == 1:
            body(lo)
        else:
            pl.loop(lo, hi)(body)

    def work(a, *steps):
        def body(s):
            remote(held.at[a, pl.ds(0, 2)], held.at[a, pl.ds(0, 2)], ag_send.at[a, 9 + s], ag_recv.at[a, 9 + s], twin).wait_recv()
            rows = held.at[a, pl.ds(block_of(s) * 4, 4)]
            if a == 0:
                product = jnp.dot(
                    rows[...].reshape(256, 1536), w_ref[...], preferred_element_type=F32
                ).astype(BF16)
                for h in range(3):
                    part[s, h] = product[:, h * 384:(h + 1) * 384]
            else:
                part[s, 3] = lax.dot_general(
                    rows[...].reshape(256, 1536), wo_ref[...].reshape(384, 1536),
                    (((1,), (1,)), ((), ())), preferred_element_type=F32,
                ).astype(BF16)
            for d in (0, 1):
                rs1(a, s, d).start()
        each(steps, body)

    def add(ref, *terms):
        value = ref[...].astype(F32)
        for term in terms:
            value = value + term.astype(F32)
        ref[...] = value.astype(BF16)

    def add_relay(a, *steps):
        def body(s):
            for d in (0, 1):
                rs1(a, s, d).wait_recv()
                rows = pl.ds(pl.multiple_of(me.col_x((1, -1)[d]) * 64 + 32 * d, 32), 32)
                add(part.at[s, unit(a), rows], relay[s, d, unit(a)])
                rs2(a, s, d).start()
        each(steps, body)

    def add_near(a, *steps):
        def body(s):
            for d in (0, 1):
                rs2(a, s, d).wait_recv()
            add(part.at[s, unit(a), own()], near[s, 0, unit(a)], near[s, 1, unit(a)])
            pl.when(is_away)(lambda: rs3(a, s).start())
        each(steps, body)

    def kv_gather(s, k):
        x, rows, device = {
            0: (0, 0, right),
            1: (0, 0, left),
            2: (-1, 1, right),
            3: (1, 2, left),
            4: (-1, 0, twin),
            5: (1, 0, twin),
            6: (2, 0, twin),
        }[k]
        start = me.col_x(x) * 64
        if rows == 0:
            span = pl.ds(pl.multiple_of(start, 64), 64)
        else:
            span = pl.ds(pl.multiple_of(start + 32 * (rows - 1), 32), 32)
        ref = kv.at[me.core, block_of(s), span]
        return remote(ref, ref, kv_send.at[s, k], kv_recv.at[s, k], device)

    def add_far(a, *steps):
        def body(s):
            block = block_of(s)

            @pl.when(is_home)
            def _():
                rs3(a, s).wait_recv()
                total[block, unit(a)] = (
                    part[s, unit(a), own()].astype(F32) + far[s, unit(a)].astype(F32)
                ).astype(BF16)
                rs4(a, s).start()

            @pl.when(is_away)
            def _():
                rs4(a, s).wait_recv()

            if a == 0:
                for j in (0, 1):
                    for h in range(3):
                        kv[j, block, own(), h * 128:(h + 1) * 128] = total[block, h, :, 128 + 128 * j:256 + 128 * j]
                kv_gather(s, 0).start()
                kv_gather(s, 1).start()
        each(steps, body)

    def kv_relay(*steps):
        def body(s):
            for d in (0, 1):
                kv_gather(s, d).wait_recv()
                kv_gather(s, 2 + d).start()
                kv_gather(s, 4 + d).start()
        each(steps, body)

    def kv_done(*steps):
        def body(s):
            kv_gather(s, 2).wait_recv()
            kv_gather(s, 3).wait_recv()
            kv_gather(s, 6).start()
        each(steps, body)

    def kv_whole(*steps):
        def body(s):
            for k in (4, 5, 6):
                kv_gather(s, k).wait_recv()
        each(steps, body)

    def part_free():
        for s in range(8):
            for d in (0, 1):
                rs1(0, s, d).wait_send()
                rs2(0, s, d).wait_send()

            @pl.when(is_away)
            def _():
                rs3(0, s).wait_send()

    transposed = (((1,), (1,)), ((), ()))
    by_rows = (((0,), (0,)), ((), ()))

    def query_of(h):
        return total[:, h, my_rows, 0:128].reshape(256, 128)

    def write_rows(t, h, low_half, high_half):
        rows = jnp.concatenate([low_half[:, :128], high_half], axis=1).T.astype(BF16)
        result[t, h, :, my_rows] = rows.reshape(8, 32, 128)

    def attend_forward(h):
        query = query_of(h)
        head = slice(h * 128, (h + 1) * 128)

        def masked(b, lanes):
            width = 256 - lanes
            s = lax.dot_general(kv[0, b, :, head], query[lanes:], transposed, preferred_element_type=F32) * scale
            key_at = b * 256 + lax.broadcasted_iota(jnp.int32, (256, width), 0)
            column = lanes + lax.broadcasted_iota(jnp.int32, (1, width), 1)
            query_at = (column // 32) * 256 + me.x * 64 + me.core * 32 + column % 32
            return jnp.where(key_at <= query_at, s, fill)

        def top(lanes):
            def body(b, m):
                s = masked(b, lanes)
                scores[b, :, lanes:] = s
                return jnp.maximum(m, jnp.max(s, axis=0, keepdims=True))
            return body

        m = lax.fori_loop(0, 4, top(0), jnp.full((1, 256), fill, F32), unroll=True)
        m_high = lax.fori_loop(4, 8, top(128), m[:, 128:], unroll=True)
        m = jnp.concatenate([m[:, :128], m_high], axis=1)

        def sums(lanes, m):
            def body(b, norm):
                e = jnp.exp(scores[b, :, lanes:] - m)
                scores[b, :, lanes:] = e
                return norm + jnp.sum(e, axis=0, keepdims=True)
            return body

        norm = lax.fori_loop(0, 4, sums(0, m), jnp.zeros((1, 256), F32), unroll=True)
        norm_high = lax.fori_loop(4, 8, sums(128, m_high), norm[:, 128:], unroll=True)
        inverse = 1.0 / jnp.concatenate([norm[:, :128], norm_high], axis=1)

        def rows(lanes):
            def body(b, att):
                w = (scores[b, :, lanes:] * inverse[:, lanes:]).astype(BF16)
                part[b, h, :, lanes:256] = w
                return att + lax.dot_general(kv[1, b, :, head], w, by_rows, preferred_element_type=F32)
            return body

        att = lax.fori_loop(0, 4, rows(0), jnp.zeros((128, 256), F32), unroll=True)
        att_high = lax.fori_loop(4, 8, rows(128), att[:, 128:], unroll=True)
        write_rows(0, h, att, att_high)
        pl.when(is_away)(lambda: lift(h, 0).start())

    def attend_backward(h):
        query = query_of(h)
        head = slice(h * 128, (h + 1) * 128)
        cotangent = total[:, 3, my_rows, head].reshape(256, 128)

        def sums(lanes):
            def body(b, slope):
                dp = lax.dot_general(kv[1, b, :, head], cotangent[lanes:], transposed, preferred_element_type=F32)
                slopes[b, :, lanes:] = dp
                return slope + jnp.sum(part[b, h, :, lanes:256].astype(F32) * dp, axis=0, keepdims=True)
            return body

        slope = lax.fori_loop(0, 4, sums(0), jnp.zeros((1, 256), F32), unroll=True)
        slope_high = lax.fori_loop(4, 8, sums(128), slope[:, 128:], unroll=True)
        slope = jnp.concatenate([slope[:, :128], slope_high], axis=1)

        def terms(lanes):
            def body(b, dq):
                w = part[b, h, :, lanes:256]
                ds = (w.astype(F32) * (slopes[b, :, lanes:] - slope[:, lanes:]) * scale).astype(BF16)
                grads[h, 0, b] = jnp.dot(ds, query[lanes:], preferred_element_type=F32).astype(BF16)
                grads[h, 1, b] = jnp.dot(w, cotangent[lanes:], preferred_element_type=F32).astype(BF16)
                return dq + lax.dot_general(kv[0, b, :, head], ds, by_rows, preferred_element_type=F32)
            return body

        dq = lax.fori_loop(0, 4, terms(0), jnp.zeros((128, 256), F32), unroll=True)
        dq_high = lax.fori_loop(4, 8, terms(128), dq[:, 128:], unroll=True)
        write_rows(1, h, dq, dq_high)
        to_twin(h).start()
        pl.when(is_away)(lambda: lift(h, 1).start())

    def to_twin(h):
        return remote(grads.at[h, 1 - me.core], twin_grads.at[h], tw_send.at[h], tw_recv.at[h], twin)

    def gs1(h, d):
        return remote(grads.at[h, me.core, (low, high)[d], own(2)], grads_relay.at[h, d],
                      g1_send.at[h, d], g1_recv.at[h, d], (right, left)[d])

    def gs2(h, d):
        return remote(grads.at[h, me.core, every, own((1, -1)[d])], grads_near.at[h, d],
                      g2_send.at[h, d], g2_recv.at[h, d], (right, left)[d])

    def add_twin(h):
        to_twin(h).wait_recv()

        @pl.loop(0, 8)
        def _(b):
            add(grads.at[h, me.core, b], twin_grads[h, b])

        for d in (0, 1):
            gs1(h, d).start()

    def add_grads_relay(h):
        for d in (0, 1):
            gs1(h, d).wait_recv()
            add(grads.at[h, me.core, (low, high)[d], own((1, -1)[d])], grads_relay[h, d])
            gs2(h, d).start()

    def add_grads_near(h):
        for d in (0, 1):
            gs2(h, d).wait_recv()
        result[2 + me.core, h] = (
            grads[h, me.core, :, own()].astype(F32) + grads_near[h, 0].astype(F32) + grads_near[h, 1].astype(F32)
        ).astype(BF16)

        @pl.when(is_away)
        def _():
            lift(h, 2).start()

    def lift(h, t):
        if t < 2:
            ref = result.at[t, h, every, my_rows]
        else:
            ref = result.at[2 + me.core, h]
        return remote(ref, ref, up_send.at[h, t], up_recv.at[h, t], twin)

    def lifted(h, t):
        ref = result.at[t, h, every, their_rows] if t < 2 else result.at[3 - me.core, h]
        remote(ref, ref, up_send.at[h, t], up_recv.at[h, t], twin).wait_recv()

    def spread(h, t, k):
        x, blocks, device = {
            0: (0, every, across),
            1: (0, every, right),
            2: (0, every, left),
            3: (-1, low, right),
            4: (1, high, left),
            5: (-1, every, across),
            6: (1, every, across),
            7: (2, every, across),
        }[k]
        ref = wide.at[t, h, blocks, own(x)]
        src = result.at[t, h] if k == 0 else ref
        return remote(src, ref, wide_send.at[h, t, k], wide_recv.at[h, t, k], device)

    def here(h, t):
        return pltpu.make_async_copy(result.at[t, h], wide.at[t, h, every, own()], here_sem.at[h, t])

    def spread_home(h, types):
        @pl.when(is_home)
        def _():
            for t in types:
                if t < 3:
                    lifted(h, t)
                spread(h, t, 0).start()
                here(h, t).start()
            for t in types:
                here(h, t).wait()
                spread(h, t, 1).start()
                spread(h, t, 2).start()

    def spread_away(h, types):
        @pl.when(is_away)
        def _():
            for t in types:
                spread(h, t, 0).wait_recv()
                if t not in along_x_first:
                    spread(h, t, 1).start()
                    spread(h, t, 2).start()

    def spread_relay(h, types):
        def around(t):
            for d in (0, 1):
                spread(h, t, 1 + d).wait_recv()
                spread(h, t, 3 + d).start()
                if t in along_x_first:
                    spread(h, t, 5 + d).start()

        for t in types:
            if t not in along_x_first:
                around(t)

        def home_rows():
            for t in types:
                if t in along_x_first:
                    around(t)

        def away_rows():
            for t in types:
                if t in along_x_first:
                    spread(h, t, 5).wait_recv()
                    spread(h, t, 6).wait_recv()

        pl.when(is_home)(home_rows)
        pl.when(is_away)(away_rows)

    def keep_grads(h, t):
        lanes = pl.ds(h * 384 + (t - 1) * 128, 128)
        return pltpu.make_async_copy(wide.at[t, h], grads_out.at[:, :, lanes], out_sem.at[h, t - 1])

    def spread_done(h, types):
        def arrived(t):
            spread(h, t, 3).wait_recv()
            spread(h, t, 4).wait_recv()

        def home_rows():
            for t in types:
                if t in along_x_first:
                    arrived(t)
                    spread(h, t, 7).start()

        def away_rows():
            for t in types:
                if t in along_x_first:
                    spread(h, t, 7).wait_recv()

        for t in types:
            if t not in along_x_first:
                arrived(t)
        pl.when(is_home)(home_rows)
        pl.when(is_away)(away_rows)
        for t in types:
            if t > 0:
                keep_grads(h, t).start()

    def block_lanes(core, n=None):
        if n is None:
            return pl.ds(pl.multiple_of(core * 768, 768), 768)
        return pl.ds(pl.multiple_of(core * 768 + n * 384, 384), 384)

    def b0(i, n):
        return remote(held.at[0, pl.ds(i * 8, 8), :, block_lanes(1 - me.core, n)], near.at[:, n, i],
                      b0_send.at[i, n], b0_recv.at[i, n], twin)

    def z_at(z):
        return lax.rem(me.z + z + 4, 4)

    def term_at(i, y, z):
        return held.at[0, i * 8 + y * 4 + z, :, block_lanes(me.core)]

    def b1(i, d):
        return remote(term_at(i, d, z_at(2)), block_relay.at[i, d], b1_send.at[i, d], b1_recv.at[i, d], (up, down)[d])

    def b2(i, d, y):
        return remote(term_at(i, y, z_at((1, -1)[d])), block_near.at[i, d, y], b2_send.at[i, d, y], b2_recv.at[i, d, y], (up, down)[d])

    def b3(i):
        return remote(term_at(i, 1 - me.ylo, me.z), block_far.at[i], b3_send.at[i], b3_recv.at[i], beside)

    def multiply_out(i):
        mine = jnp.concatenate([wide[0, h, :, own(slice_at[i])].reshape(512, 128) for h in range(3)], axis=1)
        turned[...] = mine.T

        for n in (0, 1):
            lanes = slice(n * 768, (n + 1) * 768)
            held[0, pl.ds(i * 8, 8), :, lanes] = jnp.dot(
                mine, wo_ref[:, :, lanes].reshape(384, 768), preferred_element_type=F32
            ).astype(BF16).reshape(8, 64, 768)
        b0(i, 0).start()
        b0(i, 1).start()
        for n in (0, 1):
            lanes = slice(n * 768, (n + 1) * 768)
            tokens = [held[1, b * 4 + me.col_x(slice_at[i]), :, lanes] for b in range(8)]
            term = jnp.dot(
                turned[...], jnp.concatenate(tokens, axis=0), preferred_element_type=F32
            ).reshape(3, 128, 768)
            if i == 0:
                grad_out[:, :, lanes] = term
            else:
                grad_out[:, :, lanes] += term

    def add_block_twin(i):
        for n in (0, 1):
            b0(i, n).wait_recv()

            @pl.loop(0, 8)
            def _(b):
                add(held.at[0, i * 8 + b, :, block_lanes(me.core, n)], near[b, n, i])

        for d in (0, 1):
            b1(i, d).start()

    def add_block_relay(i):
        for d in (0, 1):
            b2(i, d, 1 - d).start()
        for d in (0, 1):
            b1(i, d).wait_recv()
            add(term_at(i, d, z_at((1, -1)[d])), block_relay[i, d])
            b2(i, d, d).start()

    def add_block_near(i):
        for d in (0, 1):
            for y in (0, 1):
                b2(i, d, y).wait_recv()
        for y in (0, 1):
            add(term_at(i, y, me.z), block_near[i, 0, y], block_near[i, 1, y])
        b3(i).start()

    def add_block_far(i):
        b3(i).wait_recv()
        final[own(slice_at[i])] = (term_at(i, me.ylo, me.z)[...].astype(F32) + block_far[i].astype(F32)).astype(BF16)

    own_copy[0].wait()
    go(0, 9, 0, 1, 2)
    own_copy[1].wait()
    go(1, 9)
    wo_copy.wait()
    work(1, 0, 1)
    for copy in w_copy:
        copy.wait()
    work(0, 0, 1)
    add_relay(0, 0, 1)
    landed(0, 0)
    go(0, 3, 4, 10)
    landed(0, 2)
    go(0, 6, 12)
    landed(0, 1)
    go(0, 5, 11)
    add_relay(1, 0, 1)
    work(0, 1, 4)
    add_relay(0, 2, 3)
    add_near(0, 0, 1)
    landed(0, 4)
    go(0, 8, 14)
    add_relay(0, 1, 2)
    go(1, 0)
    add_relay(0, 3, 4)
    landed(0, 3)
    go(0, 7, 13)
    work(0, 4, 5)
    go(1, 1, 2)
    add_near(1, 0, 1)
    work(0, 5, 6)
    add_far(0, 0, 1)
    landed(0, 5, 6)
    go(0, 15)
    landed(0, 7, 8)
    go(0, 16)
    work(0, 6, 7)
    add_near(0, 3, 4)
    landed(1, 0)
    go(1, 3, 4, 10)
    work(0, 7, 8)
    add_relay(0, 4, 5)
    work(1, 1, 2)
    add_far(0, 3, 4)
    add_near(0, 1, 2)
    add_relay(0, 5, 6)
    add_near(0, 4, 5)
    add_relay(0, 6, 7)
    kv_relay(3, 4)
    add_far(1, 0, 1)
    kv_relay(0, 1)
    turn(0, 1)
    landed(1, 1)
    go(1, 5, 11)
    add_far(0, 1, 2)
    landed(1, 2)
    go(1, 6, 12)
    add_near(0, 5, 6)
    add_near(0, 2, 3)
    landed(1, 3)
    go(1, 7, 13)
    add_far(0, 4, 5)
    work(1, 2, 3)
    landed(1, 4)
    go(1, 8, 14)
    add_relay(0, 7, 8)
    work(1, 3, 4)
    work(1, 5, 6)
    landed(1, 5, 6)
    go(1, 15)
    add_far(0, 5, 6)
    add_near(0, 6, 8)
    add_far(0, 2, 3)
    kv_relay(1, 2)
    kv_relay(4, 5)
    landed(1, 7, 8)
    go(1, 16)
    add_relay(1, 1, 3)
    work(1, 6, 7)
    work(1, 4, 5)
    kv_done(3, 4)
    add_near(1, 1, 2)
    kv_done(1, 2)
    kv_done(4, 5)
    add_relay(1, 5, 6)
    work(1, 7, 8)
    kv_done(0, 1)
    kv_relay(2, 3)
    add_relay(1, 6, 7)
    add_relay(1, 3, 4)
    add_near(1, 2, 3)
    add_relay(1, 4, 5)
    add_near(1, 5, 6)
    turn(1, 2)
    add_far(0, 7, 8)
    kv_whole(0, 1)
    add_relay(1, 7, 8)
    add_near(1, 3, 4)
    add_far(1, 1, 2)
    kv_done(2, 3)
    add_far(0, 6, 7)
    add_far(1, 2, 3)
    add_near(1, 4, 5)
    add_near(1, 6, 7)
    kv_relay(7, 8)
    add_far(1, 5, 6)
    kv_relay(5, 6)
    kv_whole(1, 2)
    add_near(1, 7, 8)
    kv_whole(4, 5)
    kv_whole(3, 4)
    kv_relay(6, 7)
    kv_done(7, 8)
    turn(2, 3)
    kv_done(5, 6)
    add_far(1, 3, 4)
    kv_done(6, 7)
    kv_whole(2, 3)
    add_far(1, 6, 7)
    kv_whole(7, 8)
    add_far(1, 4, 5)
    add_far(1, 7, 8)
    kv_whole(5, 7)
    part_free()
    attend_forward(0)
    attend_backward(0)
    spread_home(0, (0,))
    attend_forward(1)
    spread_away(0, (0,))
    add_twin(0)
    attend_backward(1)
    spread_home(0, (1,))
    add_grads_relay(0)
    turn(3, 4)
    attend_forward(2)
    spread_away(0, (1,))
    spread_home(1, (1,))
    spread_home(1, (0,))
    attend_backward(2)
    spread_home(2, (0,))
    spread_away(1, (0,))
    spread_away(2, (0,))
    spread_away(1, (1,))
    add_twin(1)
    spread_relay(0, (1,))
    turn(4, 5)
    turn(5, 6)
    spread_home(2, (1,))
    spread_away(2, (1,))
    add_twin(2)
    add_grads_near(0)
    add_grads_relay(1)
    turn(6, 7)
    turn(7, 8)
    spread_relay(0, (0,))
    spread_relay(1, (1,))
    for k in range(17):
        gather(0, k).wait_send()
    multiply_out(0)
    spread_relay(2, (1,))
    add_grads_near(1)
    add_grads_relay(2)
    spread_relay(1, (0,))
    spread_home(0, (2,))
    spread_relay(2, (0,))
    spread_home(0, (3,))
    add_block_twin(0)
    spread_away(0, (2,))
    multiply_out(1)
    add_block_relay(0)
    multiply_out(2)
    add_block_twin(1)
    spread_home(1, (2,))
    spread_done(0, (0,))
    spread_done(1, (0,))
    spread_away(0, (3,))
    add_grads_near(2)
    add_block_twin(2)
    spread_away(1, (2,))
    spread_relay(0, (2,))
    add_block_near(0)
    add_block_relay(1)
    spread_done(1, (1,))
    spread_home(2, (2,))
    spread_relay(0, (3,))
    add_block_relay(2)
    spread_home(2, (3,))
    spread_done(2, (0,))
    multiply_out(3)
    grad_out_copy = pltpu.make_async_copy(grad_out, grad_out_hbm, last_sem.at[0])
    grad_out_copy.start()
    spread_home(1, (3,))
    add_block_far(0)
    add_block_near(1)
    spread_away(2, (2,))
    spread_away(2, (3,))
    spread_away(1, (3,))
    spread_relay(1, (2,))
    spread_done(0, (3,))
    spread_done(0, (2,))
    add_block_twin(3)
    spread_done(2, (1,))
    add_block_near(2)
    add_block_relay(3)
    spread_done(0, (1,))
    spread_relay(2, (2,))
    spread_relay(2, (3,))
    add_block_far(2)
    spread_relay(1, (3,))
    spread_done(1, (2,))
    add_block_near(3)
    spread_done(2, (3,))
    spread_done(2, (2,))
    add_block_far(1)
    spread_done(1, (3,))
    add_block_far(3)
    their_half = pl.ds(pl.multiple_of(128 - me.core * 128, 128), 128)
    end = remote(final.at[their_half], theirs, end_send, end_recv, twin)
    end.start()
    end.wait_recv()
    mine = final[pl.ds(pl.multiple_of(me.core * 128, 128), 128)]

    @pl.when(me.core == 0)
    def _():
        block_out[:, :768] = mine
        block_out[:, 768:] = theirs[...]

    @pl.when(me.core == 1)
    def _():
        block_out[:, :768] = theirs[...]
        block_out[:, 768:] = mine

    block_copy = pltpu.make_async_copy(block_out, block_hbm, last_sem.at[1])
    block_copy.start()

    @pl.when(is_away)
    def _():
        pl.loop(0, 8)(lambda s: rs3(1, s).wait_send())
        for h in range(3):
            for t in range(3):
                lift(h, t).wait_send()

    @pl.when(is_home)
    def _():
        for a in (0, 1):
            @pl.loop(0, 8)
            def _(s):
                rs4(a, s).wait_send()
        for h in range(3):
            for t in range(4):
                spread(h, t, 0).wait_send()
                if t in along_x_first:
                    for k in range(1, 8):
                        spread(h, t, k).wait_send()

    for k in range(17):
        gather(1, k).wait_send()

    @pl.loop(0, 8)
    def _(s):
        for d in (0, 1):
            rs1(1, s, d).wait_send()
            rs2(1, s, d).wait_send()
        for k in range(7):
            kv_gather(s, k).wait_send()

    for h in range(3):
        to_twin(h).wait_send()
        for d in (0, 1):
            gs1(h, d).wait_send()
            gs2(h, d).wait_send()
        for t in range(4):
            if t not in along_x_first:
                for k in range(1, 5):
                    spread(h, t, k).wait_send()
            if t > 0:
                keep_grads(h, t).wait()
    for i in range(4):
        for d in (0, 1):
            b0(i, d).wait_send()
            b1(i, d).wait_send()
            for y in (0, 1):
                b2(i, d, y).wait_send()
        b3(i).wait_send()
    for s in (4, 5, 6, 7):
        keep(s).wait()
    grad_out_copy.wait()
    block_copy.wait()
    end.wait_send()


def block(inputs, grad_block, w_qkv, w_out):
    dma = pltpu.SemaphoreType.DMA
    anywhere = pl.BlockSpec(memory_space=pl.ANY)
    return pl.pallas_call(
        block_kernel,
        name="block",
        out_shape=(
            jax.ShapeDtypeStruct((1536, 2048), BF16),
            jax.ShapeDtypeStruct((8, 256, 1152), BF16),
            jax.ShapeDtypeStruct((128, 1536), BF16),
            jax.ShapeDtypeStruct((3, 128, 1536), F32),
        ),
        in_specs=[anywhere] * 4,
        out_specs=(anywhere,) * 4,
        scratch_shapes=[
            pltpu.VMEM((2, 32, 64, 1536), BF16),
            pltpu.VMEM((8, 4, 256, 384), BF16),
            pltpu.VMEM((8, 2, 4, 32, 384), BF16),
            pltpu.VMEM((8, 2, 4, 64, 384), BF16),
            pltpu.VMEM((8, 4, 64, 384), BF16),
            pltpu.VMEM((8, 4, 64, 384), BF16),
            pltpu.VMEM((1536, 1152), BF16),
            pltpu.VMEM((3, 128, 1536), BF16),
            pltpu.VMEM((128, 1536), BF16),
            pltpu.VMEM((3, 128, 1536), F32),
            pltpu.VMEM((2, 8, 256, 384), BF16),
            pltpu.VMEM((8, 256, 256), F32),
            pltpu.VMEM((8, 256, 256), F32),
            pltpu.VMEM((3, 2, 8, 256, 128), BF16),
            pltpu.VMEM((3, 8, 256, 128), BF16),
            pltpu.VMEM((3, 2, 4, 64, 128), BF16),
            pltpu.VMEM((3, 2, 8, 64, 128), BF16),
            pltpu.VMEM((4, 3, 8, 64, 128), BF16),
            pltpu.VMEM((4, 3, 8, 256, 128), BF16),
            pltpu.VMEM((384, 512), BF16),
            pltpu.VMEM((4, 2, 64, 768), BF16),
            pltpu.VMEM((4, 2, 2, 64, 768), BF16),
            pltpu.VMEM((4, 64, 768), BF16),
            pltpu.VMEM((256, 768), BF16),
            pltpu.VMEM((128, 768), BF16),
            dma((2, 17)), dma((2, 17)),
            dma((2, 8, 2)), dma((2, 8, 2)),
            dma((2, 8, 2)), dma((2, 8, 2)),
            dma((2, 8)), dma((2, 8)),
            dma((2, 8)), dma((2, 8)),
            dma((8,)), dma((4,)), dma((2,)), dma((2,)),
            dma((8, 7)), dma((8, 7)),
            dma((3,)), dma((3,)),
            dma((3, 2)), dma((3, 2)),
            dma((3, 2)), dma((3, 2)),
            dma((3, 3)), dma((3, 3)),
            dma((3, 4, 8)), dma((3, 4, 8)),
            dma((3, 4)), dma((3, 3)),
            dma((4, 2)), dma((4, 2)),
            dma((4, 2)), dma((4, 2)),
            dma((4, 2, 2)), dma((4, 2, 2)),
            dma((4,)), dma((4,)),
            dma(()), dma(()),
        ],
        compiler_params=pltpu.CompilerParams(
            collective_id=1, has_side_effects=True, vmem_limit_bytes=63 << 20
        ),
    )(inputs.reshape(2, 64, 1536), grad_block.reshape(2, 64, 1536), jnp.transpose(w_qkv, (1, 0, 2)), w_out)


def weight_kernel(x_hbm, rows_hbm, block_hbm, grad_out_hbm, out_hbm, block_copy, grad_out_copy, x, rows, out, block_rows, grad_out, x_sem, sem, out_sem):
    def load(m):
        features = pl.ds(m * 256, 256)
        return pltpu.make_async_copy(x_hbm.at[features], x.at[features], x_sem.at[m])

    def store(m, h):
        return pltpu.make_async_copy(out.at[m % 2, :, h * 384:(h + 1) * 384], out_hbm.at[h, pl.ds(m * 256, 256)], out_sem.at[m, h])

    copies = [
        None,
        pltpu.make_async_copy(block_hbm, block_rows, sem.at[1]),
        pltpu.make_async_copy(grad_out_hbm, grad_out, sem.at[2]),
    ]
    passed_on = [
        pltpu.make_async_copy(block_rows, block_copy, sem.at[1]),
        pltpu.make_async_copy(grad_out, grad_out_copy, sem.at[2]),
    ]
    first, rest = slice(0, 512), slice(512, 1152)
    parts = [
        pltpu.make_async_copy(rows_hbm.at[:, :, lanes], rows.at[:, :, lanes], sem.at[k])
        for k, lanes in ((0, first), (3, rest))
    ]
    parts[0].start()
    load(0).start()
    parts[1].start()
    for m in range(1, 6):
        load(m).start()
    copies[1].start()
    copies[2].start()
    for m in range(6):
        load(m).wait()
        if m >= 2:
            for h in range(3):
                store(m - 2, h).wait()
        factor = x[m * 256:(m + 1) * 256]
        if m == 0:
            for part, lanes in zip(parts, (first, rest)):
                part.wait()
                out[0, :, lanes] = jnp.dot(
                    factor, rows[:, :, lanes].reshape(2048, lanes.stop - lanes.start), preferred_element_type=F32
                )
        else:
            out[m % 2] = jnp.dot(factor, rows[...].reshape(2048, 1152), preferred_element_type=F32)
        for h in range(3):
            store(m, h).start()
        if m == 1:
            for k in (1, 2):
                copies[k].wait()
                passed_on[k - 1].start()
    for m in (4, 5):
        for h in range(3):
            store(m, h).wait()
    for copy in passed_on:
        copy.wait()


def weight_grad(turned, rows, block_rows, grad_out):
    dma = pltpu.SemaphoreType.DMA
    anywhere = pl.BlockSpec(memory_space=pl.ANY)
    return pl.pallas_call(
        weight_kernel,
        name="weight_grad",
        out_shape=(
            jax.ShapeDtypeStruct((3, 1536, 384), F32),
            jax.ShapeDtypeStruct((128, 1536), BF16),
            jax.ShapeDtypeStruct((3, 128, 1536), F32),
        ),
        in_specs=[anywhere] * 4,
        out_specs=(anywhere,) * 3,
        scratch_shapes=[
            pltpu.VMEM((1536, 2048), BF16),
            pltpu.VMEM((8, 256, 1152), BF16),
            pltpu.VMEM((2, 256, 1152), F32),
            pltpu.VMEM((128, 1536), BF16),
            pltpu.VMEM((3, 128, 1536), F32),
            dma((6,)), dma((4,)), dma((6, 3)),
        ],
        compiler_params=pltpu.CompilerParams(vmem_limit_bytes=63 << 20),
    )(turned, rows, block_rows, grad_out)


def local(inputs, w_qkv, w_out, grad_block):
    turned, rows, block_rows, grad_out = block(inputs, grad_block, w_qkv, w_out)
    grad_qkv, block_out, grad_out = weight_grad(turned, rows, block_rows, grad_out)
    return block_out, jnp.transpose(grad_qkv, (1, 0, 2)), grad_out


def solution(mesh):
    placed = (P("row", "col"), P("col", "row", None), P("row", None, "col"), P("row", "col"))
    return jax.shard_map(
        local,
        mesh=mesh,
        in_specs=placed,
        out_specs=(P("row", "col"), P("col", "row", None), P("row", None, "col")),
        check_vma=False,
    )
```
